128 devices in a mesh: replica: 4 (over z), fsdp: 16 (over y, x), tensor: 2 (over core).
Axes of the slice: x: 4, y: 4, z: 4, core: 2. Of those that a mesh axis runs over, the one named last changes fastest.
Arguments:
- tokens: bfloat16 [49152, 12288], P(('replica', 'fsdp', 'tensor')), may hold values from -60 to 60
- norm_gain: bfloat16 [12288], replicated, may hold values from 0.099609375 to 1.8984375
- fragment: bfloat16 [4, 12288, 2048], P('replica', 'fsdp', 'tensor'), may hold values from -6.25 to 6.25
- exponents: int32 [4, 12288, 64], P('replica', 'fsdp', 'tensor'), may hold values from -4 to -1
- base_weight: float32 [12288, 2048], P(('fsdp', 'replica'), 'tensor'), may hold values from -5 to 5, as said below
- momentum: float32 [12288, 2048], P(('fsdp', 'replica'), 'tensor'), may hold values from -3 to 3
Outputs:
- new_base: float32 [12288, 2048], P(('fsdp', 'replica'), 'tensor')
- new_momentum: float32 [12288, 2048], P(('fsdp', 'replica'), 'tensor')
- keys_values: bfloat16 [49152, 2048], P(('replica', 'fsdp'), 'tensor')
The draws below stay inside these ranges and needn't reach their ends.
Inputs may be any that keep to these rules, and one draw needn't show every extreme that they name: base_weight holds multiples of 2 ** -10.
All inputs are finite; a program needn't handle non-finite values.
Results may differ from the reference program's by a relative error of at most 0.0054.
Values may be sent and summed in bfloat16 or wider, within the bound.
A program may use at most 192 MiB of HBM per device.

```python
import math
import jax
import jax.numpy as jnp
from jax import lax

D = 12288
KVW = 2048
BLOCK = 32
TOK_DEV = 384
REPLICAS = 4
TOKENS = 49152
N_FSDP = 16
N_TENSOR = 2


def shared_base(key):
    values = jnp.clip(jax.random.normal(key, (D, KVW), jnp.float32), -5.0, 5.0)
    return jnp.floor(values * 1024.0) / 1024.0


def draw_base_weight(key, part):
    shared = shared_base(key)
    return shared


def draw_fragment(key, part):
    shared = shared_base(key)
    key = jax.random.fold_in(key, 7)
    drift = jnp.clip(0.5 * jax.random.normal(key, (REPLICAS, D, KVW), jnp.float32), -1.25, 1.25)
    drift = jnp.floor(drift * 64.0) / 64.0
    return (shared[None] - drift).astype(jnp.bfloat16)


def draw_tokens(key, part):
    key = jax.random.fold_in(key, 9)
    key_rows, key_cols, key_vals = jax.random.split(key, 3)
    col_scale = jnp.exp(jax.random.uniform(key_cols, (1, D), jnp.float32, math.log(0.3), math.log(3.0)))
    row_scale = jnp.exp(jax.random.uniform(key_rows, (TOKENS, 1), jnp.float32, math.log(0.5), math.log(5.0)))
    values = jnp.clip(jax.random.normal(key_vals, (TOKENS, D), jnp.float32), -4.0, 4.0)
    return (values * row_scale * col_scale).astype(jnp.bfloat16)


def plant(values, own_key, smallest, largest):
    longest = values.shape.index(max(values.shape))
    spots = []
    for shift in (0, 1):
        where = [jax.random.randint(jax.random.fold_in(own_key, axis), (), 0, length) for axis, length in enumerate(values.shape)]
        where[longest] = (where[longest] + shift) % values.shape[longest]
        spots.append(tuple(where))
    return values.at[spots[0]].set(smallest).at[spots[1]].set(largest)


def block_scale(stream_key, dims, cuts, low, high):
    factor_of, own = 1.0, jax.random.fold_in(stream_key, 6)
    for axis_at, shards_of in cuts:
        steps = jnp.exp(jax.random.uniform(jax.random.fold_in(own, axis_at), (shards_of,), jnp.float32, low / len(cuts), high / len(cuts)))
        factor_of = factor_of * jnp.repeat(steps, dims[axis_at] // shards_of).reshape([-1 if axis == axis_at else 1 for axis in range(len(dims))])
    return factor_of


def gaussian(key, extent, spread, limit, pieces=(), kind=jnp.bfloat16):
    values = spread * jax.random.normal(key, extent, jnp.float32)
    if pieces:
        values = values * block_scale(key, extent, pieces, -0.22, 0.18)
    return jnp.clip(values, -limit, limit).astype(kind)


def setup_inputs(seed: int = 0) -> dict:
    key_of = jax.random.split(jax.random.key(seed), 7)
    tokens = draw_tokens(jax.random.fold_in(key_of[6], 71), 0)
    norm_gain = jnp.clip(1.0 + 0.18 * jax.random.normal(key_of[1], (D,), jnp.float32), 0.099609375, 1.8984375).astype(jnp.bfloat16)
    fragment = draw_fragment(jax.random.fold_in(key_of[6], 71), 0)
    exponents = plant(jax.random.randint(key_of[3], (REPLICAS, D, KVW // BLOCK), -4, 0), jax.random.fold_in(key_of[3], 1), -4, -1).astype(jnp.int32)
    base_weight = draw_base_weight(jax.random.fold_in(key_of[6], 71), 0)
    momentum = gaussian(key_of[5], (D, KVW), 0.5, 3.0, ((0, 64), (1, 2)), jnp.float32)
    return dict(tokens=tokens, norm_gain=norm_gain, fragment=fragment, exponents=exponents, base_weight=base_weight, momentum=momentum)


OUTER_RATE = 0.7
MOMENTUM_COEF = 0.9
LEVEL_STEPS = ((0.25, 0.5), (0.75, 0.5), (1.25, 0.5), (1.75, 0.5), (2.5, 1.0), (3.5, 1.0), (5.0, 2.0))

def block_factors(exponents, sign):
    return jnp.repeat(jnp.exp2(sign * exponents.astype(jnp.float32)), BLOCK, axis=-1)

def fp4_levels(values):
    clipped = jnp.clip(values, -6.0, 6.0)
    magnitude = jnp.abs(clipped)
    level = jnp.zeros_like(magnitude)
    for middle, rise in LEVEL_STEPS:
        level = level + jnp.where(magnitude >= middle, rise, 0.0).astype(magnitude.dtype)
    return jnp.where(clipped < 0.0, -level, level)

def encoded_terms(base, fragment, exponents):
    inverse = block_factors(exponents, -1.0)
    scales = block_factors(exponents, 1.0)
    codes = fp4_levels((base - fragment.astype(jnp.float32)) * inverse).astype(jnp.bfloat16)
    codes = lax.optimization_barrier(codes)
    return codes.astype(jnp.float32) * scales

def outer_step(base, moment, summed, count):
    gradient = summed / count
    new_moment = MOMENTUM_COEF * moment + gradient
    new_base = base - OUTER_RATE * (gradient + MOMENTUM_COEF * new_moment)
    return (new_base, new_moment)

def normalize(rows, gain):
    values = rows.astype(jnp.float32)
    factor = lax.rsqrt(lax.optimization_barrier(jnp.mean(values * values, axis=-1, keepdims=True)) + 1e-05)
    return (values * factor * gain.astype(jnp.float32)).astype(jnp.bfloat16)

def reference(tokens, norm_gain, fragment, exponents, base_weight, momentum):
    summed = jnp.zeros(base_weight.shape, jnp.float32)
    for replica in range(REPLICAS):
        summed = summed + encoded_terms(base_weight, fragment[replica], exponents[replica])
    new_base, new_moment = outer_step(base_weight, momentum, summed, REPLICAS)
    weight = new_base.astype(jnp.bfloat16)
    groups = tokens.reshape(REPLICAS * N_FSDP, N_TENSOR * TOK_DEV, D)

    def project(rows):
        normed = normalize(rows, norm_gain)
        return (jnp.dot(normed, weight, preferred_element_type=jnp.float32) * D ** (-0.5)).astype(jnp.bfloat16)
    keys_values = lax.map(project, groups).reshape(TOKENS, KVW)
    return (new_base, new_moment, keys_values)
```

```python
import jax
import jax.numpy as jnp
from jax import lax
from jax.experimental import pallas as pl
from jax.experimental.pallas import tpu as pltpu
from jax.sharding import PartitionSpec as P

MESH = pl.DeviceIdType.MESH
F32, BF16 = jnp.float32, jnp.bfloat16
D, KVW, BLOCK, TOK = 12288, 1024, 32, 384
ROWS = 192
FROWS = 768
SLAB = 48
OUTER_RATE = 0.7
MOMENTUM_COEF = 0.9
CLS = ((0, 384), (384, 384), (768, 256))
ORDER = (("x", "y", "z"), ("z", "y", "x"), ("z", "x", "y"))
THRESH = ((0.25, 0.5), (0.75, 1.0), (1.25, 1.5), (1.75, 2.0), (2.5, 3.0), (3.5, 4.0), (5.0, 6.0))


def mod4(v):
    return lax.rem(v + 8, 4)


def kernel(
    tokens, gain, frag, exps, base, mom,
    nb_out, nm_out, kv_out,
    w0, w1, w2, tok, acc, kv, fb, rl, bs, ms, gn, ex, ep, er, erl, sc, iv, ss,
    loc, a_snd, a_rcv, e_snd, e_rcv, t_snd, t_rcv, g_snd, g_rcv, o_sem,
):
    W = (w0, w1, w2)
    rep = lax.axis_index("replica")
    fs = lax.axis_index("fsdp")
    core = lax.axis_index("tensor")
    pos = {"x": lax.rem(fs, 4), "y": lax.div(fs, 4), "z": rep}

    def nbr(axis, step):
        c = dict(pos)
        c[axis] = mod4(pos[axis] + step)
        return (c["z"], c["y"] * 4 + c["x"], core)

    other = (rep, fs, 1 - core)

    def remote(src, dst, ss_, rs_, dev):
        return pltpu.make_async_remote_copy(
            src_ref=src, dst_ref=dst, send_sem=ss_, recv_sem=rs_, device_id=dev, device_id_type=MESH
        )

    pending = []

    def go(copy):
        copy.start()
        pending.append(copy)

    l_ex = pltpu.make_async_copy(exps, ex, loc.at[0])
    l_ex.start()
    l_fr = pltpu.make_async_copy(frag.at[rep], fb.at[0], loc.at[1])
    l_fr.start()
    l_bs = pltpu.make_async_copy(base, bs, loc.at[2])
    l_bs.start()
    l_ms = pltpu.make_async_copy(mom, ms, loc.at[3])
    l_ms.start()
    l_gn = pltpu.make_async_copy(gain, gn, loc.at[4])
    l_gn.start()

    barrier = pltpu.get_barrier_semaphore()
    peers = [nbr(a, s) for a in "xyz" for s in (1, -1)] + [other]
    for p in peers:
        pl.semaphore_signal(barrier, inc=1, device_id=p, device_id_type=MESH)

    l_ex.wait()
    for d in range(4):
        packed = jnp.zeros((SLAB, 128), F32)
        for q in range(4):
            rows = ex[pl.ds(d * ROWS + q * SLAB, SLAB), :].astype(F32).astype(BF16)
            i = lax.broadcasted_iota(jnp.int32, (BLOCK, 128), 0)
            l = lax.broadcasted_iota(jnp.int32, (BLOCK, 128), 1)
            place = jnp.where(l == i + BLOCK * q, 1.0, 0.0).astype(BF16)
            packed = packed + jnp.dot(rows, place, preferred_element_type=F32)
        ep[d] = packed.astype(BF16)

    pl.semaphore_wait(barrier, len(peers))

    up, down = nbr("z", 1), nbr("z", -1)
    zu, zd, zo = mod4(rep + 1), mod4(rep - 1), mod4(rep + 2)

    e_cp = [
        remote(ep.at[zo], erl, e_snd.at[0], e_rcv.at[0], up),
        remote(ep.at[zu], er.at[1], e_snd.at[1], e_rcv.at[1], up),
        remote(ep.at[zd], er.at[2], e_snd.at[2], e_rcv.at[2], down),
        remote(erl, er.at[3], e_snd.at[3], e_rcv.at[3], up),
    ]

    def cols(c):
        return pl.ds(CLS[c][0], CLS[c][1])

    H = ROWS // 2

    def a2a(c):
        k = 6 * c
        cc = cols(c)
        return [
            remote(frag.at[zo, pl.ds(0, H), cc], rl.at[0, :, cc], a_snd.at[k], a_rcv.at[k], up),
            remote(frag.at[zo, pl.ds(H, H), cc], rl.at[1, :, cc], a_snd.at[k + 1], a_rcv.at[k + 1], down),
            remote(frag.at[zu, :, cc], fb.at[1, :, cc], a_snd.at[k + 2], a_rcv.at[k + 2], up),
            remote(frag.at[zd, :, cc], fb.at[2, :, cc], a_snd.at[k + 3], a_rcv.at[k + 3], down),
            remote(rl.at[0, :, cc], fb.at[3, pl.ds(0, H), cc], a_snd.at[k + 4], a_rcv.at[k + 4], up),
            remote(rl.at[1, :, cc], fb.at[3, pl.ds(H, H), cc], a_snd.at[k + 5], a_rcv.at[k + 5], down),
        ]

    A = [a2a(c) for c in range(3)]

    def a2a_send(c):
        for m in A[c][:4]:
            go(m)

    def a2a_relay(c):
        for m in (0, 1):
            A[c][m].wait_recv()
            go(A[c][4 + m])

    for m in e_cp[:3]:
        go(m)
    a2a_send(0)
    mine = pl.ds(pl.multiple_of(core * TOK, TOK), TOK)
    t_cp = remote(tokens, tok.at[mine, :], t_snd.at[0], t_rcv.at[0], other)
    l_tk = pltpu.make_async_copy(tokens, tok.at[mine, :], loc.at[5])

    def expand(slot):
        e = (ep[rep] if slot == 0 else er[slot]).astype(F32)
        small = jnp.exp2(e).astype(BF16)
        small_inv = jnp.exp2(-e).astype(BF16)
        l = lax.broadcasted_iota(jnp.int32, (128, KVW), 0)
        n = lax.broadcasted_iota(jnp.int32, (128, KVW), 1)
        for q in range(4):
            pick = jnp.where(l == BLOCK * q + lax.div(n, BLOCK), 1.0, 0.0).astype(BF16)
            sc[slot, pl.ds(q * SLAB, SLAB), :] = jnp.dot(small, pick, preferred_element_type=F32).astype(BF16)
            iv[slot, pl.ds(q * SLAB, SLAB), :] = jnp.dot(small_inv, pick, preferred_element_type=F32).astype(BF16)

    e_cp[0].wait_recv()
    go(e_cp[3])
    a2a_relay(0)
    a2a_send(1)
    go(t_cp)
    l_tk.start()
    expand(0)
    for s in (1, 2, 3):
        e_cp[s].wait_recv()
        expand(s)
    acc[...] = jnp.zeros_like(acc)
    l_fr.wait()
    l_bs.wait()
    l_ms.wait()
    l_gn.wait()

    def encode(c):
        lo, width = CLS[c]
        for m in A[c][2:]:
            m.wait_recv()
        row0 = pl.multiple_of(rep * ROWS, ROWS)

        def step(t, carry):
            rr = pl.ds(pl.multiple_of(t * SLAB, SLAB), SLAB)
            wr = pl.ds(pl.multiple_of(row0 + t * SLAB, SLAB), SLAB)
            g = gn[rr, :]
            for k in range(width // 128):
                cc = pl.ds(lo + 128 * k, 128)
                b = bs[rr, cc]
                total = jnp.zeros((SLAB, 128), F32)
                for s in range(4):
                    v = (b - fb[s, rr, cc].astype(F32)) * iv[s, rr, cc].astype(F32)
                    m = jnp.abs(v)
                    level = jnp.zeros_like(m)
                    for mid, val in THRESH:
                        level = jnp.where(m >= mid, val, level)
                    total = total + jnp.where(v < 0.0, -level, level) * sc[s, rr, cc].astype(F32)
                grad = total * 0.25
                nm = MOMENTUM_COEF * ms[rr, cc] + grad
                nb = b - OUTER_RATE * (grad + MOMENTUM_COEF * nm)
                ms[rr, cc] = nm
                bs[rr, cc] = nb
                W[c][pos["y"], pos["x"], wr, pl.ds(128 * k, 128)] = (nb * g).astype(BF16)
            return carry

        lax.fori_loop(0, ROWS // SLAB, step, 0)

    def region(c, xs, ys, z0, z1):
        return W[c].at[ys, xs, pl.ds(z0, z1), :]

    def place(c, **at):
        half = at.pop("half", None)
        xs, ys = at.get("x", slice(None)), at.get("y", slice(None))
        if "z" in at:
            r0, n = at["z"] * ROWS, ROWS
        else:
            r0, n = 0, FROWS
        if half is not None:
            n = n // 2
            r0 = r0 + half * n
        if not isinstance(r0, int):
            r0 = pl.multiple_of(r0, 96)
        return W[c].at[ys, xs, pl.ds(r0, n), :]

    def ring(c, axis, idx, fixed):
        k = 24 * c + 4 * idx
        out = []
        here = place(c, **{**fixed, axis: pos[axis]})
        for j, s in enumerate((1, -1)):
            out.append(remote(here, here, g_snd.at[k + j], g_rcv.at[k + j], nbr(axis, s)))
        for j, s in enumerate((1, -1)):
            part = place(c, **{**fixed, axis: mod4(pos[axis] - s), "half": j})
            out.append(remote(part, part, g_snd.at[k + 2 + j], g_rcv.at[k + 2 + j], nbr(axis, s)))
        return out

    OFF = (0, 1, -1, 2)
    R = {}
    for c in range(3):
        a, b, l = ORDER[c]
        R[c, 1] = ring(c, a, 0, {b: pos[b], l: pos[l]})
        R[c, 2] = ring(c, b, 1, {l: pos[l]})
        for i in range(4):
            R[c, 3, i] = ring(c, l, 2 + i, {b: mod4(pos[b] + OFF[i])})

    def send(*key):
        go(R[key][0])
        go(R[key][1])

    def fwd(*key):
        for j in (0, 1):
            R[key][j].wait_recv()
            go(R[key][2 + j])

    def halves(*key):
        R[key][2].wait_recv()
        R[key][3].wait_recv()

    def mm(c, count, coords):
        lo, width = CLS[c]
        cc = pl.ds(lo, width)

        def chunk(t, carry):
            yy, xx = coords(t)
            kk = pl.ds(pl.multiple_of((yy * 4 + xx) * FROWS, FROWS), FROWS)

            def block(m, carry):
                mr = pl.ds(pl.multiple_of(m * 256, 256), 256)
                acc[mr, cc] += jnp.dot(tok[mr, kk], W[c][yy, xx], preferred_element_type=F32)
                return carry

            return lax.fori_loop(0, 3, block, carry)

        lax.fori_loop(0, count, chunk, 0)

    def mm_near(c, i):
        if c == 1:
            yy = mod4(pos["y"] + OFF[i])
            mm(c, 3, lambda t: (yy, mod4(pos["x"] + t + lax.div(t, 2))))
        else:
            xx = mod4(pos["x"] + OFF[i])
            mm(c, 3, lambda t: (mod4(pos["y"] + t + lax.div(t, 2)), xx))

    def mm_far(c, i):
        if c == 0:
            yy = mod4(pos["y"] + OFF[i])
            mm(c, 4, lambda t: (yy, t))
        elif c == 1:
            yy = mod4(pos["y"] + OFF[i])
            mm(c, 1, lambda t: (yy, mod4(pos["x"] + 2)))
        else:
            xx = mod4(pos["x"] + OFF[i])
            mm(c, 1, lambda t: (mod4(pos["y"] + 2), xx))

    def squares(i):
        rr = pl.ds(i * 128, 128)

        def step(t, s):
            for k in range(4):
                v = tok[rr, pl.ds(pl.multiple_of(t * 512 + k * 128, 128), 128)].astype(F32)
                s = s + v * v
            return s

        s = lax.fori_loop(0, D // 512, step, jnp.zeros((128, 128), F32))
        mean = jnp.sum(s, axis=1, keepdims=True) * (1.0 / D)
        ss[rr, :] = jnp.broadcast_to(lax.rsqrt(mean + 1e-05) * (D ** -0.5), (128, 128))

    encode(0)
    send(0, 1)
    a2a_relay(1)
    a2a_send(2)
    fwd(0, 1)
    encode(1)
    send(1, 1)
    a2a_relay(2)
    halves(0, 1)
    send(0, 2)
    fwd(1, 1)
    encode(2)
    send(2, 1)
    outs = [
        pltpu.make_async_copy(bs, nb_out, o_sem.at[0]),
        pltpu.make_async_copy(ms, nm_out, o_sem.at[1]),
    ]
    for o in outs:
        o.start()
    halves(1, 1)
    send(1, 2)
    send(1, 3, 0)
    fwd(2, 1)
    send(0, 3, 0)
    halves(2, 1)
    send(2, 2)
    send(2, 3, 0)
    l_tk.wait()
    t_cp.wait_recv()
    squares(0)
    squares(1)
    fwd(0, 2)
    squares(2)
    squares(3)
    fwd(1, 3, 0)
    fwd(1, 2)
    send(1, 3, 1)
    squares(4)
    squares(5)
    fwd(2, 2)
    fwd(2, 3, 0)
    send(2, 3, 1)
    fwd(0, 3, 0)
    halves(0, 2)
    send(0, 3, 1)
    halves(1, 2)
    halves(2, 2)
    for i in range(4):
        if i:
            fwd(1, 3, i)
        if i < 2:
            send(1, 3, i + 2)
        mm_near(1, i)
        if i:
            fwd(2, 3, i)
        if i < 2:
            send(2, 3, i + 2)
        mm_near(2, i)
        if i:
            fwd(0, 3, i)
        if i < 2:
            send(0, 3, i + 2)
        halves(1, 3, i)
        mm_far(1, i)
        halves(2, 3, i)
        mm_far(2, i)
        halves(0, 3, i)
        mm_far(0, i)

    for m in range(3):
        mr = pl.ds(m * 256, 256)

        def scale(k, carry):
            cc = pl.ds(pl.multiple_of(k * 128, 128), 128)
            kv[mr, cc] = (acc[mr, cc] * ss[mr, :]).astype(BF16)
            return carry

        lax.fori_loop(0, KVW // 128, scale, 0)
        o = pltpu.make_async_copy(kv.at[mr, :], kv_out.at[mr, :], o_sem.at[2 + m])
        o.start()
        outs.append(o)
    for p in pending:
        p.wait_send()
    for o in outs:
        o.wait()


def body(tokens, norm_gain, fragment, exponents, base_weight, momentum):
    row0 = lax.axis_index("fsdp") * FROWS + lax.axis_index("replica") * ROWS
    gain = lax.dynamic_slice(norm_gain, (row0,), (ROWS,)).astype(F32)
    gain = jnp.broadcast_to(gain[:, None], (ROWS, 128))
    any_ = pl.BlockSpec(memory_space=pl.ANY)
    dma = pltpu.SemaphoreType.DMA
    vm = pltpu.VMEM
    return pl.pallas_call(
        kernel,
        out_shape=(
            jax.ShapeDtypeStruct((ROWS, KVW), F32),
            jax.ShapeDtypeStruct((ROWS, KVW), F32),
            jax.ShapeDtypeStruct((2 * TOK, KVW), BF16),
        ),
        in_specs=[any_] * 6,
        out_specs=[any_] * 3,
        scratch_shapes=[
            vm((4, 4, FROWS, CLS[0][1]), BF16),
            vm((4, 4, FROWS, CLS[1][1]), BF16),
            vm((4, 4, FROWS, CLS[2][1]), BF16),
            vm((2 * TOK, D), BF16),
            vm((2 * TOK, KVW), F32),
            vm((2 * TOK, KVW), BF16),
            vm((4, ROWS, KVW), BF16),
            vm((2, ROWS // 2, KVW), BF16),
            vm((ROWS, KVW), F32),
            vm((ROWS, KVW), F32),
            vm((ROWS, 128), F32),
            vm((4 * ROWS, BLOCK), jnp.int32),
            vm((4, SLAB, 128), BF16),
            vm((4, SLAB, 128), BF16),
            vm((SLAB, 128), BF16),
            vm((4, ROWS, KVW), BF16),
            vm((4, ROWS, KVW), BF16),
            vm((2 * TOK, 128), F32),
            dma((6,)),
            dma((18,)),
            dma((18,)),
            dma((4,)),
            dma((4,)),
            dma((1,)),
            dma((1,)),
            dma((72,)),
            dma((72,)),
            dma((5,)),
        ],
        compiler_params=pltpu.CompilerParams(
            collective_id=0, has_side_effects=True, vmem_limit_bytes=62 * 1024 * 1024
        ),
        cost_estimate=pl.CostEstimate(flops=2 * 768 * 12288 * 1024, bytes_accessed=30_000_000, transcendentals=0),
    )(tokens, gain, fragment.reshape(4, ROWS, KVW), exponents.reshape(4 * ROWS, BLOCK), base_weight, momentum)


def solution(mesh):
    in_specs = (
        P(("replica", "fsdp", "tensor"), None),
        P(),
        P("replica", "fsdp", "tensor"),
        P("replica", "fsdp", "tensor"),
        P(("fsdp", "replica"), "tensor"),
        P(("fsdp", "replica"), "tensor"),
    )
    out_specs = (
        P(("fsdp", "replica"), "tensor"),
        P(("fsdp", "replica"), "tensor"),
        P(("replica", "fsdp"), "tensor"),
    )
    return jax.shard_map(body, mesh=mesh, in_specs=in_specs, out_specs=out_specs, check_vma=False)
```

```python
import jax
import jax.numpy as jnp
from jax import lax
from jax.experimental import pallas as pl
from jax.experimental.pallas import tpu as pltpu
from jax.sharding import PartitionSpec as P

MESH = pl.DeviceIdType.MESH
F32, BF16 = jnp.float32, jnp.bfloat16
D, KVW, BLOCK, TOK = 12288, 1024, 32, 384
ROWS = 192
FROWS = 768
SLAB = 48
OUTER_RATE = 0.7
MOMENTUM_COEF = 0.9
CLS = ((0, 384), (384, 384), (768, 256))
ORDER = (("x", "y", "z"), ("z", "y", "x"), ("z", "x", "y"))

SCHEDULE = (
    ("S", "r", 0), ("S", "d", 0), ("S", "r", 1), ("S", "d", 1), ("W", "r", 0), ("S", "f", 0), ("S", "r", 2),
    ("W", "r", 1), ("S", "f", 1), ("S", "d", 2), ("W", "d", 0), ("W", "f", 0), ("E", 0), ("S", "1", 0),
    ("S", "2", 0, 0), ("W", "r", 2), ("S", "f", 2), ("S", "3", 0, 0), ("W", "d", 1), ("W", "f", 1), ("E", 1),
    ("S", "3", 1, 0), ("S", "2", 1, 0), ("S", "1", 1), ("W", "d", 2), ("D", "r", 0), ("W", "f", 2), ("E", 2),
    ("W", "1", 0), ("S", "1h", 0), ("S", "2", 2, 0), ("W", "2", 0, 0), ("S", "2h", 0, 0), ("S", "2", 0, 1),
    ("S", "1", 2), ("S", "3", 0, 1), ("S", "2", 0, 2), ("D", "d", 0), ("D", "r", 1), ("W", "3", 1, 0),
    ("S", "3h", 1, 0), ("W", "3", 0, 0), ("S", "3h", 0, 0), ("W", "1", 1), ("S", "3", 1, 1), ("W", "1h", 0),
    ("S", "2", 0, 3), ("S", "3", 1, 2), ("S", "1h", 1), ("D", "d", 1), ("D", "f", 0), ("W", "1", 2), ("S", "1h", 2),
    ("W", "2", 0, 1), ("S", "2h", 0, 1), ("W", "2", 2, 0), ("S", "2h", 2, 0), ("S", "3", 0, 2), ("S", "2", 2, 1),
    ("W", "2", 1, 0), ("S", "2h", 1, 0), ("D", "r", 2), ("D", "f", 1), ("W", "2", 0, 2), ("S", "2h", 0, 2),
    ("S", "2", 2, 2), ("W", "3", 0, 1), ("S", "3h", 0, 1), ("S", "2", 1, 1), ("S", "3", 0, 3), ("W", "3", 1, 1),
    ("S", "3h", 1, 1), ("D", "d", 2), ("D", "1", 0), ("D", "f", 2), ("W", "1h", 2), ("S", "2", 2, 3),
    ("W", "2", 0, 3), ("S", "2h", 0, 3), ("S", "3", 0, 4), ("C", "sq", 0), ("D", "2", 0, 0), ("D", "3", 0, 0),
    ("D", "3", 1, 0), ("D", "2", 1, 0), ("W", "2", 2, 1), ("S", "2h", 2, 1), ("S", "2", 1, 2), ("C", "sq", 1),
    ("D", "1", 1), ("D", "1h", 0), ("D", "2", 2, 0), ("D", "2h", 0, 0), ("W", "2", 2, 2), ("S", "2h", 2, 2),
    ("C", "sq", 2), ("W", "1h", 1), ("S", "3", 1, 3), ("C", "sq", 3), ("W", "2", 1, 1), ("S", "2h", 1, 1),
    ("C", "sq", 4), ("W", "2", 2, 3), ("S", "2h", 2, 3), ("S", "2", 1, 3), ("C", "sq", 5), ("W", "3", 1, 2),
    ("S", "3h", 1, 2), ("S", "3", 2, 0), ("D", "2", 0, 1), ("D", "1", 2), ("D", "3", 0, 1), ("D", "2", 0, 2),
    ("W", "2", 1, 2), ("S", "2h", 1, 2), ("D", "3h", 1, 0), ("D", "3h", 0, 0), ("D", "3", 1, 1), ("D", "2", 0, 3),
    ("W", "3", 1, 3), ("S", "3h", 1, 3), ("C", "mm", 1, 0, "near"), ("S", "3", 2, 1), ("W", "3", 0, 2),
    ("S", "3h", 0, 2), ("W", "2", 1, 3), ("S", "3", 1, 4), ("W", "3", 0, 3), ("S", "3h", 0, 3), ("S", "2h", 1, 3),
    ("W", "3h", 1, 0), ("W", "3h", 1, 1), ("W", "3h", 1, 2), ("D", "3", 1, 2), ("D", "1h", 1), ("D", "1h", 2),
    ("D", "2h", 0, 1), ("W", "3h", 1, 3), ("C", "mm", 1, 0, "far"), ("W", "3", 2, 0), ("S", "3h", 2, 0),
    ("S", "3", 0, 5), ("S", "3", 2, 2), ("S", "3", 2, 3), ("W", "3h", 0, 0), ("W", "3h", 0, 1), ("D", "2h", 2, 0),
    ("D", "3", 0, 2), ("D", "2", 2, 1), ("D", "2h", 1, 0), ("W", "3h", 0, 2), ("D", "2h", 0, 2), ("D", "2", 2, 2),
    ("D", "3h", 0, 1), ("D", "2", 1, 1), ("W", "3h", 0, 3), ("C", "mm", 0, 0, "all"), ("S", "3", 1, 5),
    ("W", "3", 2, 1), ("S", "3h", 2, 1), ("S", "3", 2, 4), ("W", "3", 2, 2), ("D", "3", 0, 3), ("D", "3h", 1, 1),
    ("D", "2", 2, 3), ("D", "2h", 0, 3), ("W", "3", 2, 3), ("C", "mm", 2, 0, "near"), ("W", "3", 1, 4),
    ("C", "mm", 1, 1, "near"), ("W", "3", 0, 4), ("S", "3h", 0, 4), ("S", "3h", 2, 2), ("S", "3h", 2, 3),
    ("S", "3", 2, 5), ("W", "2h", 0, 0), ("W", "2h", 0, 1), ("W", "2h", 0, 3), ("W", "2h", 0, 2), ("S", "3", 0, 6),
    ("S", "3h", 1, 4), ("D", "3", 0, 4), ("D", "2h", 2, 1), ("D", "2", 1, 2), ("D", "2h", 2, 2), ("W", "3", 2, 4),
    ("C", "mm", 2, 1, "near"), ("W", "3h", 2, 0), ("W", "3h", 2, 1), ("W", "3h", 2, 2), ("W", "3h", 2, 3),
    ("C", "mm", 2, 0, "far"), ("D", "3", 1, 3), ("D", "2h", 1, 1), ("D", "2h", 2, 3), ("D", "2", 1, 3),
    ("W", "3h", 0, 4), ("C", "mm", 0, 1, "all"), ("W", "2h", 1, 0), ("W", "2h", 1, 1), ("W", "2h", 1, 3),
    ("W", "2h", 1, 2), ("S", "3", 1, 6), ("S", "3h", 2, 4), ("W", "3", 1, 5), ("C", "mm", 1, 2, "near"),
    ("W", "2h", 2, 0), ("W", "2h", 2, 1), ("W", "2h", 2, 3), ("W", "2h", 2, 2), ("S", "3", 2, 6), ("D", "3h", 1, 2),
    ("D", "3", 2, 0), ("D", "2h", 1, 2), ("D", "3h", 1, 3), ("W", "3", 2, 5), ("C", "mm", 2, 2, "near"),
    ("W", "3", 0, 5), ("S", "3h", 0, 5), ("W", "3h", 1, 4), ("C", "mm", 1, 1, "far"), ("D", "3", 2, 1),
    ("D", "3h", 0, 2), ("D", "3", 1, 4), ("D", "3h", 0, 3), ("W", "3h", 2, 4), ("C", "mm", 2, 1, "far"),
    ("D", "2h", 1, 3), ("D", "3h", 2, 0), ("D", "3", 0, 5), ("D", "3", 2, 2), ("W", "3", 0, 6), ("S", "3h", 0, 6),
    ("S", "3h", 2, 5), ("S", "3h", 1, 5), ("D", "3", 2, 3), ("D", "3", 1, 5), ("D", "3h", 2, 1), ("D", "3", 2, 4),
    ("W", "3h", 0, 5), ("C", "mm", 0, 2, "all"), ("W", "3", 1, 6), ("S", "3h", 1, 6), ("W", "3", 2, 6),
    ("S", "3h", 2, 6), ("C", "mm", 1, 3, "near"), ("C", "mm", 2, 3, "near"), ("W", "3h", 0, 6),
    ("C", "mm", 0, 3, "all"), ("W", "3h", 1, 5), ("C", "mm", 1, 2, "far"), ("W", "3h", 2, 5),
    ("C", "mm", 2, 2, "far"), ("W", "3h", 2, 6), ("C", "mm", 2, 3, "far"), ("D", "3h", 0, 4), ("D", "3h", 2, 2),
    ("D", "3h", 2, 3), ("D", "3", 2, 5), ("W", "3h", 1, 6), ("C", "mm", 1, 3, "far"),
)

THRESH = ((0.25, 0.5), (0.75, 1.0), (1.25, 1.5), (1.75, 2.0), (2.5, 3.0), (3.5, 4.0), (5.0, 6.0))


def mod4(v):
    return lax.rem(v + 8, 4)


def kernel(
    tokens, gain, frag, exps, base, mom,
    nb_out, nm_out, kv_out,
    w0, w1, w2, tok, acc, kv, fb, rl, bs, ms, gb, gf, gn, ex, eb, er, erl, sc, iv, ss,
    loc, a_snd, a_rcv, e_snd, e_rcv, t_snd, t_rcv, g_snd, g_rcv, o_sem,
):
    W = (w0, w1, w2)
    rep = lax.axis_index("replica")
    fs = lax.axis_index("fsdp")
    core = lax.axis_index("tensor")
    pos = {"x": lax.rem(fs, 4), "y": lax.div(fs, 4), "z": rep}

    def nbr(axis, step):
        c = dict(pos)
        c[axis] = mod4(pos[axis] + step)
        return (c["z"], c["y"] * 4 + c["x"], core)

    other = (rep, fs, 1 - core)

    def remote(src, dst, ss_, rs_, dev):
        return pltpu.make_async_remote_copy(
            src_ref=src, dst_ref=dst, send_sem=ss_, recv_sem=rs_, device_id=dev, device_id_type=MESH
        )

    pending = []

    def go(copy):
        copy.start()
        pending.append(copy)

    l_ex = pltpu.make_async_copy(exps, ex, loc.at[0])
    l_ex.start()
    l_fr = pltpu.make_async_copy(frag.at[rep], fb.at[0], loc.at[1])
    l_fr.start()
    l_bs = pltpu.make_async_copy(base, bs, loc.at[2])
    l_bs.start()
    l_ms = pltpu.make_async_copy(mom, ms, loc.at[3])
    l_ms.start()
    l_gn = pltpu.make_async_copy(gain, gb, loc.at[4])
    l_gn.start()

    barrier = pltpu.get_barrier_semaphore()
    peers = [nbr(a, s) for a in "xyz" for s in (1, -1)] + [other]
    for p in peers:
        pl.semaphore_signal(barrier, inc=1, device_id=p, device_id_type=MESH)

    l_ex.wait()
    eb[...] = ex[...].astype(F32).astype(BF16)

    pl.semaphore_wait(barrier, len(peers))

    up, down = nbr("z", 1), nbr("z", -1)
    zu, zd, zo = mod4(rep + 1), mod4(rep - 1), mod4(rep + 2)

    def window(d):
        return eb.at[:, pl.ds(pl.multiple_of(128 * lax.div(3 * d, 2), 128), 256)]

    e_cp = [
        remote(window(zo), erl, e_snd.at[0], e_rcv.at[0], up),
        remote(window(zu), er.at[1], e_snd.at[1], e_rcv.at[1], up),
        remote(window(zd), er.at[2], e_snd.at[2], e_rcv.at[2], down),
        remote(erl, er.at[3], e_snd.at[3], e_rcv.at[3], up),
    ]

    def cols(c):
        return pl.ds(CLS[c][0], CLS[c][1])

    H = ROWS // 2

    def a2a(c):
        k = 6 * c
        cc = cols(c)
        return [
            remote(frag.at[zo, pl.ds(0, H), cc], rl.at[0, :, cc], a_snd.at[k], a_rcv.at[k], up),
            remote(frag.at[zo, pl.ds(H, H), cc], rl.at[1, :, cc], a_snd.at[k + 1], a_rcv.at[k + 1], down),
            remote(frag.at[zu, :, cc], fb.at[1, :, cc], a_snd.at[k + 2], a_rcv.at[k + 2], up),
            remote(frag.at[zd, :, cc], fb.at[2, :, cc], a_snd.at[k + 3], a_rcv.at[k + 3], down),
            remote(rl.at[0, :, cc], fb.at[3, pl.ds(0, H), cc], a_snd.at[k + 4], a_rcv.at[k + 4], up),
            remote(rl.at[1, :, cc], fb.at[3, pl.ds(H, H), cc], a_snd.at[k + 5], a_rcv.at[k + 5], down),
        ]

    for m in e_cp[:3]:
        go(m)
    mine = pl.ds(pl.multiple_of(core * TOK, TOK), TOK)
    t_cp = remote(tokens, tok.at[mine, :], t_snd.at[0], t_rcv.at[0], other)
    l_tk = pltpu.make_async_copy(tokens, tok.at[mine, :], loc.at[5])

    off = 64 * lax.rem(rep, 2)

    def expand(slot):
        e = (window(rep)[...] if slot == 0 else er[slot]).astype(F32)
        j = lax.broadcasted_iota(jnp.int32, (BLOCK, KVW), 0)
        n = lax.broadcasted_iota(jnp.int32, (BLOCK, KVW), 1)
        pick = jnp.where(j == lax.div(n, BLOCK), 1.0, 0.0).astype(BF16)
        for ref, sign in ((sc, 1.0), (iv, -1.0)):
            small = jnp.exp2(sign * e).astype(BF16)
            full = lax.dot_general(small, pick, (((0,), (0,)), ((), ())), preferred_element_type=F32)
            ref[slot] = full.astype(BF16)

    def prepare():
        go(t_cp)
        l_tk.start()
        expand(0)
        e_cp[0].wait_recv()
        go(e_cp[3])
        l_gn.wait()
        gf[...] = gb[...].astype(F32)
        first = 6 * fs + lax.div(3 * rep, 2)
        i = lax.broadcasted_iota(jnp.int32, (128, 128), 0)
        l = lax.broadcasted_iota(jnp.int32, (128, 128), 1)
        for h in range(2):
            row = jnp.broadcast_to(gf[pl.ds(first + h, 1), :], (128, 128))
            column = jnp.sum(jnp.where(i == l, row, 0.0), axis=1, keepdims=True)
            gn[pl.ds(128 * h, 128), :] = jnp.broadcast_to(column, (128, 128))
        for s in (1, 2, 3):
            e_cp[s].wait_recv()
            expand(s)
        acc[...] = jnp.zeros_like(acc)
        l_fr.wait()
        l_bs.wait()
        l_ms.wait()

    def encode(c):
        lo, width = CLS[c]
        row0 = pl.multiple_of(rep * ROWS, ROWS)

        def step(t, carry):
            rr = pl.ds(pl.multiple_of(t * SLAB, SLAB), SLAB)
            wr = pl.ds(pl.multiple_of(row0 + t * SLAB, SLAB), SLAB)
            fr = pl.ds(pl.multiple_of(off + t * SLAB, 16), SLAB)
            g = gn[fr, :]
            for k in range(width // 128):
                cc = pl.ds(lo + 128 * k, 128)
                b = bs[rr, cc]
                total = jnp.zeros((SLAB, 128), F32)
                for s in range(4):
                    v = (b - fb[s, rr, cc].astype(F32)) * iv[s, fr, cc].astype(F32)
                    m = jnp.abs(v)
                    level = jnp.zeros_like(m)
                    for mid, val in THRESH:
                        level = jnp.where(m >= mid, val, level)
                    total = total + jnp.where(v < 0.0, -level, level) * sc[s, fr, cc].astype(F32)
                grad = total * 0.25
                nm = MOMENTUM_COEF * ms[rr, cc] + grad
                nb = b - OUTER_RATE * (grad + MOMENTUM_COEF * nm)
                ms[rr, cc] = nm
                bs[rr, cc] = nb
                W[c][pos["y"], pos["x"], wr, pl.ds(128 * k, 128)] = (nb * g).astype(BF16)
            return carry

        lax.fori_loop(0, ROWS // SLAB, step, 0)

    def place(c, **at):
        half = at.pop("half", None)
        xs, ys = at.get("x", slice(None)), at.get("y", slice(None))
        if "z" in at:
            r0, n = at["z"] * ROWS, ROWS
        else:
            r0, n = 0, FROWS
        if half is not None:
            n = n // 2
            r0 = r0 + half * n
        if not isinstance(r0, int):
            r0 = pl.multiple_of(r0, 96)
        return W[c].at[ys, xs, pl.ds(r0, n), :]

    M = {}
    OFF = (0, 1, -1, 2)
    for c in range(3):
        m = a2a(c)
        M["r", c], M["d", c], M["f", c] = m[:2], m[2:4], m[4:]

    def ring(level, c, i, k, axis, fixed):
        k = 48 * c + 4 * k
        key = (c,) if level == "1" else (c, i)
        here = place(c, **{**fixed, axis: pos[axis]})
        M[(level,) + key] = [
            remote(here, here, g_snd.at[k + j], g_rcv.at[k + j], nbr(axis, s)) for j, s in enumerate((1, -1))
        ]
        M[(level + "h",) + key] = []
        for j, s in enumerate((1, -1)):
            part = place(c, **{**fixed, axis: mod4(pos[axis] - s), "half": j})
            M[(level + "h",) + key].append(
                remote(part, part, g_snd.at[k + 2 + j], g_rcv.at[k + 2 + j], nbr(axis, s))
            )

    for c in range(3):
        a, b, l = ORDER[c]
        ring("1", c, 0, 0, a, {b: pos[b], l: pos[l]})
        for i in range(4):
            at = mod4(pos[a] + OFF[i])
            ring("2", c, i, 1 + i, b, {a: at, l: pos[l]})
            ring("3", c, i, 5 + i, l, {a: at, b: pos[b]})
        for i in range(1, 4):
            ring("3", c, 3 + i, 8 + i, l, {b: mod4(pos[b] + OFF[i])})

    def mm(c, count, coords):
        lo, width = CLS[c]
        cc = pl.ds(lo, width)

        def chunk(t, carry):
            yy, xx = coords(t)
            kk = pl.ds(pl.multiple_of((yy * 4 + xx) * FROWS, FROWS), FROWS)

            def block(m, carry):
                mr = pl.ds(pl.multiple_of(m * 256, 256), 256)
                acc[mr, cc] += jnp.dot(tok[mr, kk], W[c][yy, xx], preferred_element_type=F32)
                return carry

            return lax.fori_loop(0, 3, block, carry)

        lax.fori_loop(0, count, chunk, 0)

    def mm_near(c, i):
        if c == 1:
            yy = mod4(pos["y"] + OFF[i])
            mm(c, 3, lambda t: (yy, mod4(pos["x"] + t + lax.div(t, 2))))
        else:
            xx = mod4(pos["x"] + OFF[i])
            mm(c, 3, lambda t: (mod4(pos["y"] + t + lax.div(t, 2)), xx))

    def mm_far(c, i):
        if c == 0:
            yy = mod4(pos["y"] + OFF[i])
            mm(c, 4, lambda t: (yy, t))
        elif c == 1:
            yy = mod4(pos["y"] + OFF[i])
            mm(c, 1, lambda t: (yy, mod4(pos["x"] + 2)))
        else:
            xx = mod4(pos["x"] + OFF[i])
            mm(c, 1, lambda t: (mod4(pos["y"] + 2), xx))

    def squares(i):
        rr = pl.ds(i * 128, 128)

        def step(t, s):
            for k in range(4):
                v = tok[rr, pl.ds(pl.multiple_of(t * 512 + k * 128, 128), 128)].astype(F32)
                s = s + v * v
            return s

        s = lax.fori_loop(0, D // 512, step, jnp.zeros((128, 128), F32))
        mean = jnp.sum(s, axis=1, keepdims=True) * (1.0 / D)
        ss[rr, :] = jnp.broadcast_to(lax.rsqrt(mean + 1e-05) * (D ** -0.5), (128, 128))

    outs = []
    left = []
    encoded = 0
    squared = 0
    for kind, *key in SCHEDULE:
        key = tuple(key)
        if kind == "S":
            for m in M[key]:
                m.start()
            left.append(key)
        elif kind == "W":
            if key == ("d", 0):
                prepare()
            for m in M[key]:
                m.wait_recv()
        elif kind == "D":
            for m in M[key]:
                m.wait_send()
            left.remove(key)
        elif kind == "E":
            encode(*key)
            encoded += 1
            if encoded == 3:
                outs.append(pltpu.make_async_copy(bs, nb_out, o_sem.at[0]))
                outs.append(pltpu.make_async_copy(ms, nm_out, o_sem.at[1]))
                for o in outs:
                    o.start()
        elif key[0] == "sq":
            if squared == 0:
                l_tk.wait()
                t_cp.wait_recv()
            squared += 1
            squares(key[1])
        elif key[3] == "near":
            mm_near(key[1], key[2])
        else:
            mm_far(key[1], key[2])

    for m in range(3):
        mr = pl.ds(m * 256, 256)

        def scale(k, carry):
            cc = pl.ds(pl.multiple_of(k * 128, 128), 128)
            kv[mr, cc] = (acc[mr, cc] * ss[mr, :]).astype(BF16)
            return carry

        lax.fori_loop(0, KVW // 128, scale, 0)
        o = pltpu.make_async_copy(kv.at[mr, :], kv_out.at[mr, :], o_sem.at[2 + m])
        o.start()
        outs.append(o)
    for key in left:
        for m in M[key]:
            m.wait_send()
    for p in pending:
        p.wait_send()
    for o in outs:
        o.wait()


def body(tokens, norm_gain, fragment, exponents, base_weight, momentum):
    any_ = pl.BlockSpec(memory_space=pl.ANY)
    dma = pltpu.SemaphoreType.DMA
    vm = pltpu.VMEM
    return pl.pallas_call(
        kernel,
        out_shape=(
            jax.ShapeDtypeStruct((ROWS, KVW), F32),
            jax.ShapeDtypeStruct((ROWS, KVW), F32),
            jax.ShapeDtypeStruct((2 * TOK, KVW), BF16),
        ),
        in_specs=[any_] * 6,
        out_specs=[any_] * 3,
        scratch_shapes=[
            vm((4, 4, FROWS, CLS[0][1]), BF16),
            vm((4, 4, FROWS, CLS[1][1]), BF16),
            vm((4, 4, FROWS, CLS[2][1]), BF16),
            vm((2 * TOK, D), BF16),
            vm((2 * TOK, KVW), F32),
            vm((2 * TOK, KVW), BF16),
            vm((4, ROWS, KVW), BF16),
            vm((2, ROWS // 2, KVW), BF16),
            vm((ROWS, KVW), F32),
            vm((ROWS, KVW), F32),
            vm((D // 128, 128), BF16),
            vm((D // 128, 128), F32),
            vm((256, 128), F32),
            vm((BLOCK, 4 * ROWS), jnp.int32),
            vm((BLOCK, 4 * ROWS), BF16),
            vm((4, BLOCK, 256), BF16),
            vm((BLOCK, 256), BF16),
            vm((4, 256, KVW), BF16),
            vm((4, 256, KVW), BF16),
            vm((2 * TOK, 128), F32),
            dma((6,)),
            dma((18,)),
            dma((18,)),
            dma((4,)),
            dma((4,)),
            dma((1,)),
            dma((1,)),
            dma((144,)),
            dma((144,)),
            dma((5,)),
        ],
        compiler_params=pltpu.CompilerParams(
            collective_id=0, has_side_effects=True, vmem_limit_bytes=62 * 1024 * 1024
        ),
        cost_estimate=pl.CostEstimate(flops=2 * 768 * 12288 * 1024, bytes_accessed=30_000_000, transcendentals=0),
    )(
        tokens,
        norm_gain.reshape(D // 128, 128),
        fragment.reshape(4, ROWS, KVW),
        exponents[0].T,
        base_weight,
        momentum,
    )


def solution(mesh):
    in_specs = (
        P(("replica", "fsdp", "tensor"), None),
        P(),
        P("replica", "fsdp", "tensor"),
        P("replica", "fsdp", "tensor"),
        P(("fsdp", "replica"), "tensor"),
        P(("fsdp", "replica"), "tensor"),
    )
    out_specs = (
        P(("fsdp", "replica"), "tensor"),
        P(("fsdp", "replica"), "tensor"),
        P(("replica", "fsdp"), "tensor"),
    )
    return jax.shard_map(body, mesh=mesh, in_specs=in_specs, out_specs=out_specs, check_vma=False)
```

```python
import jax
import jax.numpy as jnp
from jax import lax
from jax.experimental import pallas as pl
from jax.experimental.pallas import tpu as pltpu
from jax.sharding import PartitionSpec as P

MESH = pl.DeviceIdType.MESH
F32, BF16 = jnp.float32, jnp.bfloat16
D, KVW, BLOCK, TOK = 12288, 1024, 32, 384
ROWS = 192
FROWS = 768
SLAB = 48
OUTER_RATE = 0.7
MOMENTUM_COEF = 0.9
CLS = ((0, 256), (256, 384), (640, 384))
PARTS = (
    (0, 0, 128, ("x", "y", "z")),
    (0, 128, 128, ("y", "x", "z")),
    (1, 0, 128, ("z", "y", "x")),
    (2, 0, 128, ("z", "x", "y")),
    (1, 128, 256, ("y", "z", "x")),
    (2, 128, 256, ("x", "z", "y")),
)

SCHEDULE = (
    ("S", "r", 0), ("S", "d", 0), ("S", "r", 1), ("D", "r", 0), ("S", "d", 1), ("W", "r", 0), ("S", "f", 0),
    ("D", "r", 1), ("D", "d", 0), ("S", "r", 2), ("S", "d", 2), ("D", "f", 0), ("D", "d", 1), ("W", "r", 1),
    ("S", "f", 1), ("D", "r", 2), ("S", "r", 3), ("W", "d", 0), ("W", "f", 0), ("E", 0), ("S", "1", 0),
    ("S", "2", 0, 0), ("D", "f", 1), ("D", "d", 2), ("D", "r", 3), ("W", "r", 2), ("S", "f", 2), ("S", "d", 3),
    ("W", "d", 1), ("W", "f", 1), ("E", 1), ("D", "1", 0), ("S", "2", 1, 0), ("D", "2", 0, 0), ("S", "1", 1),
    ("D", "f", 2), ("W", "r", 3), ("S", "f", 3), ("D", "d", 3), ("S", "r", 4), ("W", "1", 0), ("S", "1h", 0),
    ("W", "2", 0, 0), ("S", "2h", 0, 0), ("S", "2", 0, 1), ("D", "f", 3), ("S", "d", 4), ("D", "1", 1),
    ("S", "2", 0, 2), ("W", "d", 2), ("W", "f", 2), ("E", 2), ("D", "2", 1, 0), ("D", "1h", 0), ("W", "2", 1, 0),
    ("S", "2h", 1, 0), ("W", "1", 1), ("S", "2", 1, 1), ("D", "2h", 0, 0), ("S", "1h", 1), ("D", "r", 4),
    ("S", "r", 5), ("S", "2", 1, 2), ("W", "1h", 0), ("S", "2", 0, 3), ("D", "2", 0, 1), ("S", "2", 2, 0),
    ("D", "2h", 1, 0), ("S", "3", 2, 0), ("W", "r", 4), ("S", "f", 4), ("W", "d", 3), ("W", "f", 3), ("E", 3),
    ("D", "d", 4), ("S", "d", 5), ("D", "2", 1, 1), ("S", "2", 3, 0), ("D", "2", 0, 2), ("D", "1h", 1),
    ("W", "2", 0, 1), ("S", "2h", 0, 1), ("W", "2", 0, 2), ("S", "2h", 0, 2), ("D", "2", 1, 2), ("W", "1h", 1),
    ("S", "2", 1, 3), ("D", "r", 5), ("S", "1", 2), ("W", "2", 1, 1), ("S", "2h", 1, 1), ("D", "2", 0, 3),
    ("D", "2", 2, 0), ("S", "3", 3, 0), ("D", "3", 2, 0), ("W", "2", 1, 2), ("S", "2h", 1, 2), ("D", "2h", 0, 1),
    ("D", "2h", 0, 2), ("W", "2", 0, 3), ("S", "2h", 0, 3), ("W", "2", 2, 0), ("S", "2h", 2, 0), ("D", "f", 4),
    ("W", "r", 5), ("S", "f", 5), ("S", "1", 3), ("W", "d", 4), ("W", "f", 4), ("E", 4), ("D", "3", 3, 0),
    ("D", "2h", 0, 3), ("D", "2h", 2, 0), ("S", "1", 4), ("D", "2h", 1, 1), ("D", "2", 3, 0), ("D", "2h", 1, 2),
    ("D", "2", 1, 3), ("W", "2", 3, 0), ("S", "2h", 3, 0), ("W", "2", 1, 3), ("S", "2h", 1, 3), ("D", "1", 2),
    ("D", "d", 5), ("W", "1", 2), ("S", "1h", 2), ("D", "f", 5), ("D", "1", 3), ("S", "2", 4, 0), ("S", "2", 2, 1),
    ("S", "2", 2, 2), ("D", "2h", 3, 0), ("D", "2h", 1, 3), ("S", "3", 4, 0), ("W", "d", 5), ("W", "f", 5), ("E", 5),
    ("D", "1h", 2), ("W", "1", 3), ("S", "1h", 3), ("S", "1", 5), ("D", "2", 4, 0), ("S", "2", 5, 0), ("D", "1", 4),
    ("W", "1h", 2), ("S", "2", 2, 3), ("D", "3", 4, 0), ("S", "2", 3, 1), ("D", "2", 2, 1), ("D", "2", 2, 2),
    ("W", "1", 4), ("S", "1h", 4), ("D", "1h", 3), ("W", "2", 4, 0), ("S", "2h", 4, 0), ("S", "2", 3, 2),
    ("S", "2", 4, 1), ("W", "2", 2, 1), ("S", "2h", 2, 1), ("W", "2", 2, 2), ("S", "2h", 2, 2), ("W", "1h", 3),
    ("S", "2", 3, 3), ("D", "2", 2, 3), ("S", "3", 5, 0), ("S", "2", 4, 2), ("W", "2", 2, 3), ("S", "2h", 2, 3),
    ("D", "2", 3, 1), ("S", "3", 2, 1), ("D", "2h", 2, 1), ("D", "1h", 4), ("D", "2h", 2, 2), ("D", "2h", 2, 3),
    ("S", "3", 3, 1), ("W", "2", 3, 1), ("S", "2h", 3, 1), ("D", "2h", 4, 0), ("D", "2", 5, 0), ("W", "1h", 4),
    ("S", "2", 4, 3), ("D", "2", 3, 2), ("D", "1", 5), ("S", "3", 4, 1), ("W", "2", 5, 0), ("S", "3", 5, 1),
    ("D", "2", 3, 3), ("W", "2", 3, 2), ("S", "2h", 3, 2), ("D", "2h", 3, 1), ("W", "1", 5), ("S", "1h", 5),
    ("S", "2h", 5, 0), ("D", "3", 5, 0), ("D", "3", 3, 1), ("S", "3", 3, 2), ("D", "3", 2, 1), ("W", "2", 3, 3),
    ("S", "2h", 3, 3), ("D", "2", 4, 1), ("S", "2", 5, 1), ("S", "3", 5, 2), ("D", "2h", 3, 2), ("S", "3", 2, 2),
    ("D", "2", 4, 2), ("W", "2", 4, 1), ("S", "2h", 4, 1), ("D", "2h", 3, 3), ("D", "1h", 5), ("S", "3", 4, 2),
    ("D", "3", 5, 1), ("D", "3", 3, 2), ("S", "3", 3, 3), ("D", "2h", 5, 0), ("W", "2", 4, 2), ("S", "2h", 4, 2),
    ("S", "3", 3, 4), ("D", "2", 4, 3), ("S", "2", 5, 2), ("D", "3", 4, 1), ("D", "3", 2, 2), ("S", "3", 2, 3),
    ("W", "2h", 4, 0), ("S", "3", 4, 3), ("D", "2h", 4, 1), ("W", "2", 4, 3), ("S", "2h", 4, 3), ("C", "sq", 0),
    ("D", "2h", 4, 2), ("W", "1h", 5), ("S", "2", 5, 3), ("D", "3", 4, 2), ("D", "3", 2, 3), ("S", "3", 2, 4),
    ("D", "3", 5, 2), ("D", "3", 3, 3), ("W", "2h", 5, 0), ("S", "3", 5, 3), ("C", "sq", 1), ("D", "2", 5, 1),
    ("W", "2", 5, 1), ("S", "2h", 5, 1), ("W", "3", 3, 0), ("W", "3", 3, 1), ("W", "3", 3, 2), ("W", "3", 3, 3),
    ("S", "3h", 3, 0), ("C", "sq", 2), ("D", "2h", 4, 3), ("S", "3", 0, 0), ("D", "3", 4, 3), ("W", "2h", 4, 1),
    ("S", "3", 4, 4), ("D", "3", 3, 4), ("S", "3", 3, 5), ("D", "2", 5, 2), ("S", "3", 1, 0), ("S", "3", 0, 1),
    ("W", "3", 2, 0), ("W", "3", 2, 1), ("W", "3", 2, 2), ("W", "3", 2, 3), ("W", "3", 4, 0), ("W", "3", 4, 1),
    ("W", "3", 4, 2), ("W", "3", 4, 3), ("C", "mm", 1, 0, "near"), ("D", "2h", 5, 1), ("D", "2", 5, 3),
    ("W", "2", 5, 2), ("S", "2h", 5, 2), ("D", "3", 0, 0), ("S", "3", 1, 1), ("D", "3", 5, 3), ("D", "3h", 3, 0),
    ("W", "2h", 5, 1), ("S", "3", 5, 4), ("W", "2", 5, 3), ("S", "2h", 5, 3), ("D", "3", 1, 0), ("D", "3", 0, 1),
    ("S", "3", 0, 2), ("W", "3", 5, 0), ("W", "3", 5, 1), ("W", "3", 5, 2), ("W", "3", 5, 3),
    ("C", "mm", 2, 0, "near"), ("S", "3", 1, 2), ("D", "2h", 5, 2), ("D", "3", 1, 1), ("S", "3", 0, 3),
    ("D", "3", 2, 4), ("S", "3h", 2, 0), ("D", "2h", 5, 3), ("D", "3", 0, 2), ("S", "3", 1, 3), ("S", "3", 0, 4),
    ("S", "3h", 4, 0), ("D", "3", 3, 5), ("S", "3h", 5, 0), ("W", "3", 2, 4), ("W", "3", 4, 4),
    ("C", "mm", 1, 1, "near"), ("D", "3", 1, 2), ("D", "3", 0, 3), ("D", "3", 1, 3), ("S", "3", 1, 4),
    ("D", "3", 4, 4), ("D", "3h", 2, 0), ("S", "3", 2, 5), ("D", "3", 5, 4), ("W", "2h", 5, 2), ("S", "3", 5, 5),
    ("D", "3", 0, 4), ("W", "3", 0, 0), ("W", "3", 0, 1), ("W", "3", 0, 2), ("W", "3", 0, 3), ("S", "3h", 0, 0),
    ("D", "3h", 4, 0), ("W", "2h", 4, 2), ("S", "3", 4, 5), ("W", "3", 3, 4), ("W", "3", 5, 4),
    ("C", "mm", 2, 1, "near"), ("W", "3", 1, 0), ("W", "3", 1, 1), ("W", "3", 1, 2), ("W", "3", 1, 3),
    ("S", "3h", 1, 0), ("W", "3h", 2, 0), ("W", "3h", 4, 0), ("C", "mm", 1, 0, "far"), ("W", "3h", 3, 0),
    ("W", "3h", 5, 0), ("C", "mm", 2, 0, "far"), ("D", "3h", 0, 0), ("D", "3", 1, 4), ("S", "3", 0, 5),
    ("D", "3h", 5, 0), ("S", "3h", 3, 1), ("W", "3h", 0, 0), ("W", "3h", 1, 0), ("C", "mm", 0, 0, "all"),
    ("D", "3h", 1, 0), ("S", "3", 1, 5), ("D", "3", 2, 5), ("S", "3h", 2, 1), ("S", "3h", 5, 1), ("S", "3h", 4, 1),
    ("W", "3", 3, 5), ("W", "3", 5, 5), ("C", "mm", 2, 2, "near"), ("D", "3", 0, 5), ("W", "3", 0, 4),
    ("S", "3h", 0, 1), ("D", "3", 5, 5), ("D", "3h", 3, 1), ("W", "2h", 3, 0), ("W", "2h", 3, 1), ("W", "2h", 3, 2),
    ("W", "2h", 3, 3), ("S", "3", 3, 6), ("W", "3", 1, 4), ("S", "3h", 1, 1), ("D", "3", 4, 5), ("D", "3h", 2, 1),
    ("W", "2h", 2, 0), ("W", "2h", 2, 1), ("W", "2h", 2, 2), ("W", "2h", 2, 3), ("S", "3", 2, 6), ("W", "3", 2, 5),
    ("W", "3", 4, 5), ("C", "mm", 1, 2, "near"), ("D", "3", 1, 5), ("W", "2h", 0, 0), ("W", "2h", 0, 1),
    ("W", "2h", 0, 2), ("W", "2h", 0, 3), ("S", "3", 0, 6), ("D", "3h", 5, 1), ("W", "2h", 5, 3), ("S", "3", 5, 6),
    ("W", "3h", 3, 1), ("W", "3h", 5, 1), ("C", "mm", 2, 1, "far"), ("D", "3h", 4, 1), ("W", "2h", 4, 3),
    ("S", "3", 4, 6), ("W", "3h", 2, 1), ("W", "3h", 4, 1), ("C", "mm", 1, 1, "far"), ("D", "3h", 0, 1),
    ("D", "3h", 1, 1), ("W", "2h", 1, 0), ("W", "2h", 1, 1), ("W", "2h", 1, 2), ("W", "2h", 1, 3), ("S", "3", 1, 6),
    ("W", "3h", 0, 1), ("W", "3h", 1, 1), ("C", "mm", 0, 1, "all"), ("D", "3", 0, 6), ("W", "3", 0, 5),
    ("S", "3h", 0, 2), ("D", "3", 3, 6), ("S", "3h", 3, 2), ("W", "3", 1, 5), ("S", "3h", 1, 2), ("D", "3", 2, 6),
    ("S", "3h", 2, 2), ("S", "3h", 5, 2), ("D", "3", 1, 6), ("W", "3", 0, 6), ("S", "3h", 0, 3), ("S", "3h", 4, 2),
    ("D", "3h", 0, 2), ("W", "3", 1, 6), ("S", "3h", 1, 3), ("W", "3", 3, 6), ("W", "3", 5, 6),
    ("C", "mm", 2, 3, "near"), ("D", "3", 5, 6), ("D", "3h", 3, 2), ("S", "3h", 3, 3), ("D", "3", 4, 6),
    ("D", "3h", 2, 2), ("W", "3", 2, 6), ("S", "3h", 2, 3), ("S", "3h", 5, 3), ("W", "3", 4, 6),
    ("C", "mm", 1, 3, "near"), ("S", "3h", 4, 3), ("W", "3h", 0, 2), ("W", "3h", 1, 2), ("C", "mm", 0, 2, "all"),
    ("W", "3h", 0, 3), ("W", "3h", 1, 3), ("C", "mm", 0, 3, "all"), ("W", "3h", 2, 2), ("W", "3h", 4, 2),
    ("C", "mm", 1, 2, "far"), ("W", "3h", 2, 3), ("W", "3h", 4, 3), ("C", "mm", 1, 3, "far"), ("W", "3h", 3, 2),
    ("W", "3h", 5, 2), ("C", "mm", 2, 2, "far"), ("W", "3h", 3, 3), ("W", "3h", 5, 3), ("C", "mm", 2, 3, "far"),
)

THRESH = ((0.25, 0.5), (0.75, 1.0), (1.25, 1.5), (1.75, 2.0), (2.5, 3.0), (3.5, 4.0), (5.0, 6.0))


def mod4(v):
    return lax.rem(v + 8, 4)


def kernel(
    tokens, gain, frag, exps, base, mom,
    nb_out, nm_out, kv_out,
    w0, w1, w2, tok, acc, kv, fb, rl, bs, ms, gb, gf, gn, ex, eb, er, erl, sc, iv, ss,
    loc, a_snd, a_rcv, e_snd, e_rcv, t_snd, t_rcv, g_snd, g_rcv, o_sem,
):
    W = (w0, w1, w2)
    rep = lax.axis_index("replica")
    fs = lax.axis_index("fsdp")
    core = lax.axis_index("tensor")
    pos = {"x": lax.rem(fs, 4), "y": lax.div(fs, 4), "z": rep}

    def nbr(axis, step):
        c = dict(pos)
        c[axis] = mod4(pos[axis] + step)
        return (c["z"], c["y"] * 4 + c["x"], core)

    other = (rep, fs, 1 - core)

    def remote(src, dst, ss_, rs_, dev):
        return pltpu.make_async_remote_copy(
            src_ref=src, dst_ref=dst, send_sem=ss_, recv_sem=rs_, device_id=dev, device_id_type=MESH
        )

    pending = []

    def go(copy):
        copy.start()
        pending.append(copy)

    l_ex = pltpu.make_async_copy(exps, ex, loc.at[0])
    l_ex.start()
    l_fr = pltpu.make_async_copy(frag.at[rep], fb.at[0], loc.at[1])
    l_fr.start()
    l_bs = pltpu.make_async_copy(base, bs, loc.at[2])
    l_bs.start()
    l_ms = pltpu.make_async_copy(mom, ms, loc.at[3])
    l_ms.start()
    l_gn = pltpu.make_async_copy(gain, gb, loc.at[4])
    l_gn.start()

    barrier = pltpu.get_barrier_semaphore()
    peers = [nbr(a, s) for a in "xyz" for s in (1, -1)] + [other]
    for p in peers:
        pl.semaphore_signal(barrier, inc=1, device_id=p, device_id_type=MESH)

    l_ex.wait()
    eb[...] = ex[...].astype(F32).astype(BF16)

    def window(d):
        return eb.at[:, pl.ds(pl.multiple_of(128 * lax.div(3 * d, 2), 128), 256)]

    off = 64 * lax.rem(rep, 2)

    def expand(slot):
        e = (window(rep)[...] if slot == 0 else er[slot]).astype(F32)
        j = lax.broadcasted_iota(jnp.int32, (BLOCK, KVW), 0)
        n = lax.broadcasted_iota(jnp.int32, (BLOCK, KVW), 1)
        pick = jnp.where(j == lax.div(n, BLOCK), 1.0, 0.0).astype(BF16)
        for ref, sign in ((sc, 1.0), (iv, -1.0)):
            small = jnp.exp2(sign * e).astype(BF16)
            full = lax.dot_general(small, pick, (((0,), (0,)), ((), ())), preferred_element_type=F32)
            ref[slot] = full.astype(BF16)

    expand(0)
    l_gn.wait()
    gf[...] = gb[...].astype(F32)
    first = 6 * fs + lax.div(3 * rep, 2)
    i = lax.broadcasted_iota(jnp.int32, (128, 128), 0)
    l = lax.broadcasted_iota(jnp.int32, (128, 128), 1)
    for h in range(2):
        row = jnp.broadcast_to(gf[pl.ds(first + h, 1), :], (128, 128))
        column = jnp.sum(jnp.where(i == l, row, 0.0), axis=1, keepdims=True)
        gn[pl.ds(128 * h, 128), :] = jnp.broadcast_to(column, (128, 128))
    acc[...] = jnp.zeros_like(acc)

    pl.semaphore_wait(barrier, len(peers))

    up, down = nbr("z", 1), nbr("z", -1)
    zu, zd, zo = mod4(rep + 1), mod4(rep - 1), mod4(rep + 2)

    e_cp = [
        remote(window(zo), erl, e_snd.at[0], e_rcv.at[0], up),
        remote(window(zu), er.at[1], e_snd.at[1], e_rcv.at[1], up),
        remote(window(zd), er.at[2], e_snd.at[2], e_rcv.at[2], down),
        remote(erl, er.at[3], e_snd.at[3], e_rcv.at[3], up),
    ]

    def cols(p):
        c, lo, width, _ = PARTS[p]
        return pl.ds(CLS[c][0] + lo, width)

    H = ROWS // 2

    def a2a(p):
        k = 6 * p
        cc = cols(p)
        return [
            remote(frag.at[zo, pl.ds(0, H), cc], rl.at[0, :, cc], a_snd.at[k], a_rcv.at[k], up),
            remote(frag.at[zo, pl.ds(H, H), cc], rl.at[1, :, cc], a_snd.at[k + 1], a_rcv.at[k + 1], down),
            remote(frag.at[zu, :, cc], fb.at[1, :, cc], a_snd.at[k + 2], a_rcv.at[k + 2], up),
            remote(frag.at[zd, :, cc], fb.at[2, :, cc], a_snd.at[k + 3], a_rcv.at[k + 3], down),
            remote(rl.at[0, :, cc], fb.at[3, pl.ds(0, H), cc], a_snd.at[k + 4], a_rcv.at[k + 4], up),
            remote(rl.at[1, :, cc], fb.at[3, pl.ds(H, H), cc], a_snd.at[k + 5], a_rcv.at[k + 5], down),
        ]

    for m in e_cp[:3]:
        go(m)
    mine = pl.ds(pl.multiple_of(core * TOK, TOK), TOK)
    t_cp = remote(tokens, tok.at[mine, :], t_snd.at[0], t_rcv.at[0], other)
    l_tk = pltpu.make_async_copy(tokens, tok.at[mine, :], loc.at[5])

    def prepare():
        for s in (1, 2, 3):
            e_cp[s].wait_recv()
            expand(s)
        l_fr.wait()
        l_bs.wait()
        l_ms.wait()

    def encode(p):
        c, sub, width, _ = PARTS[p]
        lo = CLS[c][0] + sub
        row0 = pl.multiple_of(rep * ROWS, ROWS)

        def step(t, carry):
            rr = pl.ds(pl.multiple_of(t * SLAB, SLAB), SLAB)
            wr = pl.ds(pl.multiple_of(row0 + t * SLAB, SLAB), SLAB)
            fr = pl.ds(pl.multiple_of(off + t * SLAB, 16), SLAB)
            g = gn[fr, :]
            for k in range(width // 128):
                cc = pl.ds(lo + 128 * k, 128)
                b = bs[rr, cc]
                total = jnp.zeros((SLAB, 128), F32)
                for s in range(4):
                    v = (b - fb[s, rr, cc].astype(F32)) * iv[s, fr, cc].astype(F32)
                    m = jnp.abs(v)
                    level = jnp.zeros_like(m)
                    for mid, val in THRESH:
                        level = jnp.where(m >= mid, val, level)
                    total = total + jnp.where(v < 0.0, -level, level) * sc[s, fr, cc].astype(F32)
                grad = total * 0.25
                nm = MOMENTUM_COEF * ms[rr, cc] + grad
                nb = b - OUTER_RATE * (grad + MOMENTUM_COEF * nm)
                ms[rr, cc] = nm
                bs[rr, cc] = nb
                W[c][pos["y"], pos["x"], wr, pl.ds(sub + 128 * k, 128)] = (nb * g).astype(BF16)
            return carry

        lax.fori_loop(0, ROWS // SLAB, step, 0)

    def place(p, **at):
        half = at.pop("half", None)
        xs, ys = at.get("x", slice(None)), at.get("y", slice(None))
        if "z" in at:
            r0, n = at["z"] * ROWS, ROWS
        else:
            r0, n = 0, FROWS
        if half is not None:
            n = n // 2
            r0 = r0 + half * n
        if not isinstance(r0, int):
            r0 = pl.multiple_of(r0, 96)
        c, lo, width, _ = PARTS[p]
        return W[c].at[ys, xs, pl.ds(r0, n), pl.ds(lo, width)]

    M = {}
    OFF = (0, 1, -1, 2)
    used = [0]

    def both(*pair):
        out = []
        for j, s in enumerate((1, -1)):
            axis, ref = pair[j]
            out.append(remote(ref, ref, g_snd.at[used[0]], g_rcv.at[used[0]], nbr(axis, s)))
            used[0] += 1
        return out

    def full(p, axis, **fixed):
        here = place(p, **fixed, **{axis: pos[axis]})
        return both((axis, here), (axis, here))

    def half(p, axis, **fixed):
        return both(
            *[(axis, place(p, **fixed, **{axis: mod4(pos[axis] - s), "half": j})) for j, s in enumerate((1, -1))]
        )

    for p in range(len(PARTS)):
        m = a2a(p)
        M["r", p], M["d", p], M["f", p] = m[:2], m[2:4], m[4:]
        a, b, l = PARTS[p][3]
        R, S = (a, b) if b == "z" else (b, a)
        at = {b: pos[b], l: pos[l]}
        M["1", p], M["1h", p] = full(p, a, **at), half(p, a, **at)
        for i in range(4):
            at = {a: mod4(pos[a] + OFF[i]), l: pos[l]}
            M["2", p, i], M["2h", p, i] = full(p, b, **at), half(p, b, **at)
            M["3", p, i] = full(p, l, **{R: pos[R], S: mod4(pos[S] + OFF[i])})
            M["3h", p, i] = half(p, l, **{R: mod4(pos[R] + OFF[i])})
            if i:
                M["3", p, 3 + i] = full(p, l, **{R: mod4(pos[R] + OFF[i])})

    def mm(c, count, coords):
        lo, width = CLS[c]
        cc = pl.ds(lo, width)

        def chunk(t, carry):
            yy, xx = coords(t)
            kk = pl.ds(pl.multiple_of((yy * 4 + xx) * FROWS, FROWS), FROWS)

            def block(m, carry):
                mr = pl.ds(pl.multiple_of(m * 256, 256), 256)
                acc[mr, cc] += jnp.dot(tok[mr, kk], W[c][yy, xx], preferred_element_type=F32)
                return carry

            return lax.fori_loop(0, 3, block, carry)

        lax.fori_loop(0, count, chunk, 0)

    def offset(i):
        return i + lax.div(i, 2) - 2 * lax.div(i, 3)

    def mm_near(c, i):
        if c == 1:
            yy = mod4(pos["y"] + OFF[i])
            mm(c, 3, lambda t: (yy, mod4(pos["x"] + offset(t))))
        else:
            xx = mod4(pos["x"] + OFF[i])
            mm(c, 3, lambda t: (mod4(pos["y"] + offset(t)), xx))

    def mm_far(c, i):
        if c == 1:
            mm(c, 1, lambda t: (mod4(pos["y"] + OFF[i]), mod4(pos["x"] + 2)))
        else:
            mm(c, 1, lambda t: (mod4(pos["y"] + 2), mod4(pos["x"] + OFF[i])))

    def mm_level(c, i):
        def coords(t):
            turn = lax.div(t, i + 1)
            iy = i * (1 - turn) + (t - i - 1) * turn
            ix = t * (1 - turn) + i * turn
            return mod4(pos["y"] + offset(iy)), mod4(pos["x"] + offset(ix))

        mm(c, 2 * i + 1, coords)

    def squares(i):
        rr = pl.ds(pl.multiple_of(core * TOK + i * 128, 128), 128)

        def step(t, s):
            for k in range(4):
                v = tok[rr, pl.ds(pl.multiple_of(t * 512 + k * 128, 128), 128)].astype(F32)
                s = s + v * v
            return s

        s = lax.fori_loop(0, D // 512, step, jnp.zeros((128, 128), F32))
        mean = jnp.sum(s, axis=1, keepdims=True) * (1.0 / D)
        ss[rr, :] = jnp.broadcast_to(lax.rsqrt(mean + 1e-05) * (D ** -0.5), (128, 128))

    s_cp = remote(ss.at[mine, :], ss.at[mine, :], t_snd.at[1], t_rcv.at[1], other)
    outs = []
    left = []
    seen = set()

    def once(name):
        new = name not in seen
        seen.add(name)
        return new

    for kind, *key in SCHEDULE:
        key = tuple(key)
        if kind == "S":
            for m in M[key]:
                m.start()
            left.append(key)
        elif kind == "W":
            if once("wait"):
                go(t_cp)
                l_tk.start()
                e_cp[0].wait_recv()
                go(e_cp[3])
            if key == ("d", 0):
                prepare()
            for m in M[key]:
                m.wait_recv()
        elif kind == "D":
            for m in M[key]:
                m.wait_send()
            left.remove(key)
        elif kind == "E":
            encode(*key)
            left_to_encode = len(PARTS) - 1 - key[0]
            if left_to_encode == 0:
                outs.append(pltpu.make_async_copy(bs, nb_out, o_sem.at[0]))
                outs.append(pltpu.make_async_copy(ms, nm_out, o_sem.at[1]))
                for o in outs:
                    o.start()
        elif key[0] == "sq":
            if once("own tokens"):
                l_tk.wait()
            squares(key[1])
            if key[1] == 2:
                go(s_cp)
        else:
            if once("all tokens"):
                t_cp.wait_recv()
            {"near": mm_near, "far": mm_far, "all": mm_level}[key[3]](key[1], key[2])
    s_cp.wait_recv()

    for m in range(3):
        mr = pl.ds(m * 256, 256)

        def scale(k, carry):
            cc = pl.ds(pl.multiple_of(k * 128, 128), 128)
            kv[mr, cc] = (acc[mr, cc] * ss[mr, :]).astype(BF16)
            return carry

        lax.fori_loop(0, KVW // 128, scale, 0)
        o = pltpu.make_async_copy(kv.at[mr, :], kv_out.at[mr, :], o_sem.at[2 + m])
        o.start()
        outs.append(o)
    for key in left:
        for m in M[key]:
            m.wait_send()
    for p in pending:
        p.wait_send()
    for o in outs:
        o.wait()


def body(tokens, norm_gain, fragment, exponents, base_weight, momentum):
    any_ = pl.BlockSpec(memory_space=pl.ANY)
    dma = pltpu.SemaphoreType.DMA
    vm = pltpu.VMEM
    return pl.pallas_call(
        kernel,
        out_shape=(
            jax.ShapeDtypeStruct((ROWS, KVW), F32),
            jax.ShapeDtypeStruct((ROWS, KVW), F32),
            jax.ShapeDtypeStruct((2 * TOK, KVW), BF16),
        ),
        in_specs=[any_] * 6,
        out_specs=[any_] * 3,
        scratch_shapes=[
            *[vm((4, 4, FROWS, width), BF16) for _, width in CLS],
            vm((2 * TOK, D), BF16),
            vm((2 * TOK, KVW), F32),
            vm((2 * TOK, KVW), BF16),
            vm((4, ROWS, KVW), BF16),
            vm((2, ROWS // 2, KVW), BF16),
            vm((ROWS, KVW), F32),
            vm((ROWS, KVW), F32),
            vm((D // 128, 128), BF16),
            vm((D // 128, 128), F32),
            vm((256, 128), F32),
            vm((BLOCK, 4 * ROWS), jnp.int32),
            vm((BLOCK, 4 * ROWS), BF16),
            vm((4, BLOCK, 256), BF16),
            vm((BLOCK, 256), BF16),
            vm((4, 256, KVW), BF16),
            vm((4, 256, KVW), BF16),
            vm((2 * TOK, 128), F32),
            dma((6,)),
            dma((6 * len(PARTS),)),
            dma((6 * len(PARTS),)),
            dma((4,)),
            dma((4,)),
            dma((2,)),
            dma((2,)),
            dma((42 * len(PARTS),)),
            dma((42 * len(PARTS),)),
            dma((5,)),
        ],
        compiler_params=pltpu.CompilerParams(
            collective_id=0, has_side_effects=True, vmem_limit_bytes=62 * 1024 * 1024
        ),
        cost_estimate=pl.CostEstimate(flops=2 * 768 * 12288 * 1024, bytes_accessed=30_000_000, transcendentals=0),
    )(
        tokens,
        norm_gain.reshape(D // 128, 128),
        fragment.reshape(4, ROWS, KVW),
        exponents[0].T,
        base_weight,
        momentum,
    )


def solution(mesh):
    in_specs = (
        P(("replica", "fsdp", "tensor"), None),
        P(),
        P("replica", "fsdp", "tensor"),
        P("replica", "fsdp", "tensor"),
        P(("fsdp", "replica"), "tensor"),
        P(("fsdp", "replica"), "tensor"),
    )
    out_specs = (
        P(("fsdp", "replica"), "tensor"),
        P(("fsdp", "replica"), "tensor"),
        P(("replica", "fsdp"), "tensor"),
    )
    return jax.shard_map(body, mesh=mesh, in_specs=in_specs, out_specs=out_specs, check_vma=False)
```

```python
import jax
import jax.numpy as jnp
from jax import lax
from jax.experimental import pallas as pl
from jax.experimental.pallas import tpu as pltpu
from jax.sharding import PartitionSpec as P

MESH = pl.DeviceIdType.MESH
F32, BF16 = jnp.float32, jnp.bfloat16
D, KVW, BLOCK, TOK = 12288, 1024, 32, 384
ROWS = 192
FROWS = 768
SLAB = 48
OUTER_RATE = 0.7
MOMENTUM_COEF = 0.9
CLS = ((0, 256), (256, 384), (640, 384))
PARTS = (
    (0, 0, 128, ("x", "y", "z")),
    (0, 128, 128, ("y", "x", "z")),
    (1, 0, 128, ("z", "y", "x")),
    (2, 0, 128, ("z", "x", "y")),
    (1, 128, 256, ("y", "z", "x")),
    (2, 128, 256, ("x", "z", "y")),
)

SCHEDULE = (
    ("S", "r", 0), ("S", "d", 0), ("S", "r", 1), ("D", "r", 0), ("S", "d", 1), ("W", "r", 0), ("S", "f", 0),
    ("D", "d", 0), ("D", "r", 1), ("S", "r", 2), ("S", "d", 2), ("D", "d", 1), ("D", "f", 0), ("W", "r", 1),
    ("S", "f", 1), ("D", "r", 2), ("S", "r", 3), ("W", "d", 0), ("W", "f", 0), ("E", 0), ("S", "1", 0),
    ("S", "2", 0, 0), ("D", "f", 1), ("D", "d", 2), ("D", "r", 3), ("W", "r", 2), ("S", "f", 2), ("S", "d", 3),
    ("W", "d", 1), ("W", "f", 1), ("E", 1), ("D", "1", 0), ("S", "2", 1, 0), ("D", "2", 0, 0), ("S", "1", 1),
    ("D", "f", 2), ("W", "r", 3), ("S", "f", 3), ("S", "r", 4), ("W", "1", 0), ("S", "1h", 0), ("W", "2", 0, 0),
    ("S", "2h", 0, 0), ("S", "2", 0, 1), ("D", "d", 3), ("D", "f", 3), ("S", "d", 4), ("D", "1", 1), ("S", "2", 0, 2),
    ("W", "d", 2), ("W", "f", 2), ("E", 2), ("D", "2", 1, 0), ("D", "1h", 0), ("W", "2", 1, 0), ("S", "2h", 1, 0),
    ("W", "1", 1), ("S", "2", 1, 1), ("D", "2h", 0, 0), ("S", "1h", 1), ("S", "2", 1, 2), ("D", "r", 4),
    ("S", "r", 5), ("W", "1h", 0), ("S", "2", 0, 3), ("S", "2", 2, 0), ("W", "d", 3), ("W", "f", 3), ("E", 3),
    ("W", "r", 4), ("S", "f", 4), ("D", "2h", 1, 0), ("S", "2", 3, 0), ("D", "2", 1, 1), ("S", "3", 2, 0),
    ("D", "2", 0, 1), ("D", "2", 0, 2), ("D", "1h", 1), ("W", "2", 0, 1), ("S", "2h", 0, 1), ("D", "d", 4),
    ("D", "r", 5), ("S", "d", 5), ("S", "3", 3, 0), ("W", "2", 0, 2), ("S", "2h", 0, 2), ("D", "2", 1, 2),
    ("W", "2", 1, 1), ("S", "2h", 1, 1), ("W", "1h", 1), ("S", "2", 1, 3), ("W", "2", 1, 2), ("S", "2h", 1, 2),
    ("D", "f", 4), ("W", "r", 5), ("S", "f", 5), ("S", "1", 2), ("W", "d", 4), ("W", "f", 4), ("E", 4),
    ("D", "2", 0, 3), ("D", "2", 2, 0), ("D", "2h", 0, 1), ("D", "2h", 0, 2), ("D", "3", 3, 0), ("S", "1", 4),
    ("D", "2", 3, 0), ("D", "3", 2, 0), ("D", "2h", 1, 1), ("D", "2h", 1, 2), ("W", "2", 3, 0), ("S", "2h", 3, 0),
    ("D", "d", 5), ("S", "1", 3), ("W", "2", 0, 3), ("S", "2h", 0, 3), ("S", "2", 4, 0), ("W", "2", 2, 0),
    ("S", "2h", 2, 0), ("D", "2", 1, 3), ("D", "2h", 3, 0), ("S", "3", 4, 0), ("W", "2", 1, 3), ("S", "2h", 1, 3),
    ("W", "d", 5), ("W", "f", 5), ("E", 5), ("D", "2h", 0, 3), ("D", "2h", 2, 0), ("D", "1", 4), ("W", "1", 2),
    ("S", "2", 2, 1), ("D", "2h", 1, 3), ("S", "1", 5), ("D", "f", 5), ("D", "1", 2), ("D", "1", 3), ("S", "1h", 2),
    ("S", "2", 2, 2), ("W", "1", 3), ("S", "1h", 3), ("D", "2", 4, 0), ("W", "1", 4), ("S", "2", 4, 1),
    ("S", "1h", 4), ("D", "3", 4, 0), ("S", "2", 3, 1), ("S", "2", 3, 2), ("D", "1h", 2), ("S", "2", 4, 2),
    ("D", "2", 2, 1), ("S", "3", 5, 0), ("D", "2", 2, 2), ("W", "2", 2, 1), ("S", "2h", 2, 1), ("W", "1h", 3),
    ("S", "2", 3, 3), ("W", "1h", 2), ("S", "2", 2, 3), ("D", "1h", 3), ("W", "2", 4, 0), ("S", "2h", 4, 0),
    ("S", "3", 2, 1), ("D", "1h", 4), ("W", "2", 2, 2), ("S", "2h", 2, 2), ("S", "2", 5, 0), ("D", "1", 5),
    ("D", "2", 3, 1), ("D", "2", 3, 2), ("S", "3", 4, 1), ("D", "2h", 2, 1), ("S", "3", 3, 1), ("W", "1", 5),
    ("S", "1h", 5), ("D", "2", 4, 1), ("W", "1h", 4), ("S", "2", 4, 3), ("D", "2h", 2, 2), ("D", "2", 2, 3),
    ("S", "3", 3, 2), ("D", "2", 3, 3), ("D", "3", 2, 1), ("W", "2", 3, 1), ("S", "2h", 3, 1), ("D", "3", 5, 0),
    ("S", "3", 3, 3), ("W", "2", 2, 3), ("S", "2h", 2, 3), ("W", "2", 3, 2), ("S", "2h", 3, 2), ("W", "2", 3, 3),
    ("S", "2h", 3, 3), ("D", "2h", 4, 0), ("D", "2", 4, 2), ("W", "2", 4, 1), ("S", "2h", 4, 1), ("D", "3", 3, 1),
    ("S", "3", 3, 4), ("W", "2", 4, 2), ("S", "2h", 4, 2), ("D", "2h", 3, 1), ("S", "3", 2, 2), ("S", "2", 5, 1),
    ("D", "1h", 5), ("D", "2h", 3, 2), ("S", "3", 4, 2), ("D", "2", 5, 0), ("W", "2", 5, 0), ("S", "2h", 5, 0),
    ("D", "2h", 3, 3), ("D", "3", 4, 1), ("D", "3", 2, 2), ("S", "3", 2, 3), ("D", "2h", 2, 3), ("D", "3", 3, 2),
    ("D", "3", 3, 3), ("S", "3", 5, 1), ("C", "sq", 0), ("D", "2h", 4, 1), ("D", "2", 4, 3), ("D", "2h", 4, 2),
    ("W", "2", 4, 3), ("S", "2h", 4, 3), ("W", "2h", 4, 0), ("S", "3", 4, 3), ("S", "2", 5, 2), ("C", "sq", 1),
    ("D", "3", 3, 4), ("S", "3", 5, 2), ("D", "3", 2, 3), ("D", "3", 4, 2), ("S", "3", 2, 4), ("C", "sq", 2),
    ("D", "2h", 5, 0), ("D", "2", 5, 1), ("W", "1h", 5), ("S", "2", 5, 3), ("D", "3", 5, 1), ("W", "2h", 5, 0),
    ("S", "3", 5, 3), ("D", "2h", 4, 3), ("W", "2", 5, 1), ("S", "2h", 5, 1), ("W", "3", 3, 0), ("W", "3", 3, 1),
    ("W", "3", 3, 2), ("W", "3", 3, 3), ("S", "3h", 3, 0), ("D", "3", 4, 3), ("W", "2h", 4, 1), ("S", "3", 4, 4),
    ("S", "3", 0, 0), ("D", "3", 5, 2), ("S", "3", 3, 5), ("S", "3", 1, 0), ("W", "3", 2, 0), ("W", "3", 2, 1),
    ("W", "3", 2, 2), ("W", "3", 2, 3), ("W", "3", 4, 0), ("W", "3", 4, 1), ("W", "3", 4, 2), ("W", "3", 4, 3),
    ("C", "mm", 1, 0, "near"), ("D", "2", 5, 2), ("D", "2h", 5, 1), ("D", "2", 5, 3), ("W", "2", 5, 2),
    ("S", "2h", 5, 2), ("D", "3", 0, 0), ("D", "3", 1, 0), ("S", "3", 0, 1), ("S", "3", 1, 1), ("D", "3", 5, 3),
    ("W", "2h", 5, 1), ("S", "3", 5, 4), ("S", "3", 0, 2), ("W", "2", 5, 3), ("S", "2h", 5, 3), ("W", "3", 5, 0),
    ("W", "3", 5, 1), ("W", "3", 5, 2), ("W", "3", 5, 3), ("C", "mm", 2, 0, "near"), ("D", "2h", 5, 2),
    ("S", "3", 1, 2), ("D", "3", 2, 4), ("S", "3h", 2, 0), ("D", "3", 0, 1), ("D", "3", 1, 1), ("S", "3", 0, 3),
    ("D", "3", 0, 2), ("D", "2h", 5, 3), ("S", "3", 1, 3), ("S", "3h", 4, 0), ("S", "3", 0, 4), ("W", "3", 2, 4),
    ("W", "3", 4, 4), ("C", "mm", 1, 1, "near"), ("D", "3h", 3, 0), ("D", "3", 3, 5), ("S", "3h", 5, 0),
    ("D", "3", 4, 4), ("D", "3h", 2, 0), ("S", "3", 2, 5), ("D", "3", 1, 2), ("D", "3", 0, 3), ("D", "3", 1, 3),
    ("S", "3", 1, 4), ("D", "3", 5, 4), ("W", "2h", 5, 2), ("S", "3", 5, 5), ("D", "3h", 4, 0), ("W", "2h", 4, 2),
    ("S", "3", 4, 5), ("W", "3", 0, 0), ("W", "3", 0, 1), ("W", "3", 0, 2), ("W", "3", 0, 3), ("S", "3h", 0, 0),
    ("W", "3", 3, 4), ("W", "3", 5, 4), ("C", "mm", 2, 1, "near"), ("W", "3h", 2, 0), ("W", "3h", 4, 0),
    ("C", "mm", 1, 0, "far"), ("D", "3", 0, 4), ("W", "3", 1, 0), ("W", "3", 1, 1), ("W", "3", 1, 2),
    ("W", "3", 1, 3), ("S", "3h", 1, 0), ("W", "3h", 3, 0), ("W", "3h", 5, 0), ("C", "mm", 2, 0, "far"),
    ("D", "3h", 0, 0), ("D", "3", 1, 4), ("S", "3", 0, 5), ("D", "3h", 5, 0), ("S", "3h", 3, 1), ("W", "3h", 0, 0),
    ("W", "3h", 1, 0), ("C", "mm", 0, 0, "all"), ("D", "3", 2, 5), ("S", "3h", 2, 1), ("D", "3h", 1, 0),
    ("S", "3", 1, 5), ("S", "3h", 5, 1), ("D", "3", 4, 5), ("S", "3h", 4, 1), ("W", "3", 0, 4), ("S", "3h", 0, 1),
    ("W", "3", 2, 5), ("W", "3", 4, 5), ("C", "mm", 1, 2, "near"), ("D", "3", 5, 5), ("D", "3h", 3, 1),
    ("W", "2h", 3, 0), ("W", "2h", 3, 1), ("W", "2h", 3, 2), ("W", "2h", 3, 3), ("S", "3", 3, 6), ("D", "3h", 2, 1),
    ("W", "2h", 2, 0), ("W", "2h", 2, 1), ("W", "2h", 2, 2), ("W", "2h", 2, 3), ("S", "3", 2, 6), ("D", "3", 0, 5),
    ("W", "3", 1, 4), ("S", "3h", 1, 1), ("W", "2h", 0, 0), ("W", "2h", 0, 1), ("W", "2h", 0, 2), ("W", "2h", 0, 3),
    ("S", "3", 0, 6), ("D", "3h", 5, 1), ("W", "2h", 5, 3), ("S", "3", 5, 6), ("W", "3", 3, 5), ("W", "3", 5, 5),
    ("C", "mm", 2, 2, "near"), ("D", "3h", 4, 1), ("W", "2h", 4, 3), ("S", "3", 4, 6), ("W", "3h", 2, 1),
    ("W", "3h", 4, 1), ("C", "mm", 1, 1, "far"), ("W", "3h", 3, 1), ("W", "3h", 5, 1), ("C", "mm", 2, 1, "far"),
    ("D", "3h", 0, 1), ("D", "3", 1, 5), ("D", "3h", 1, 1), ("W", "2h", 1, 0), ("W", "2h", 1, 1), ("W", "2h", 1, 2),
    ("W", "2h", 1, 3), ("S", "3", 1, 6), ("W", "3h", 0, 1), ("W", "3h", 1, 1), ("C", "mm", 0, 1, "all"),
    ("D", "3", 0, 6), ("W", "3", 0, 5), ("S", "3h", 0, 2), ("D", "3", 3, 6), ("S", "3h", 3, 2), ("D", "3", 2, 6),
    ("S", "3h", 2, 2), ("W", "3", 1, 5), ("S", "3h", 1, 2), ("S", "3h", 5, 2), ("S", "3h", 4, 2), ("D", "3", 1, 6),
    ("W", "3", 0, 6), ("S", "3h", 0, 3), ("D", "3h", 0, 2), ("W", "3", 1, 6), ("S", "3h", 1, 3), ("W", "3", 3, 6),
    ("W", "3", 5, 6), ("C", "mm", 2, 3, "near"), ("D", "3", 5, 6), ("D", "3h", 3, 2), ("S", "3h", 3, 3),
    ("D", "3", 4, 6), ("D", "3h", 2, 2), ("W", "3", 2, 6), ("S", "3h", 2, 3), ("S", "3h", 5, 3), ("W", "3", 4, 6),
    ("S", "3h", 4, 3), ("W", "3h", 0, 2), ("W", "3h", 1, 2), ("C", "mm", 0, 2, "all"), ("W", "3h", 0, 3),
    ("W", "3h", 1, 3), ("C", "mm", 0, 3, "all"), ("C", "mm", 1, 3, "near"), ("W", "3h", 2, 2), ("W", "3h", 4, 2),
    ("C", "mm", 1, 2, "far"), ("W", "3h", 2, 3), ("W", "3h", 4, 3), ("C", "mm", 1, 3, "far"), ("W", "3h", 3, 2),
    ("W", "3h", 5, 2), ("C", "mm", 2, 2, "far"), ("W", "3h", 3, 3), ("W", "3h", 5, 3), ("C", "mm", 2, 3, "far"),
)

THRESH = ((0.25, 0.5), (0.75, 1.0), (1.25, 1.5), (1.75, 2.0), (2.5, 3.0), (3.5, 4.0), (5.0, 6.0))


def mod4(v):
    return lax.rem(v + 8, 4)


def kernel(
    tokens, gain, frag, exps, base, mom,
    grad_out, kv_out,
    w0, w1, w2, tok, acc, kv, fb, rl, bs, ms, gr, gb, gf, gn, ex, eb, er, erl, sc, iv, ss,
    loc, a_snd, a_rcv, e_snd, e_rcv, t_snd, t_rcv, g_snd, g_rcv, o_sem,
):
    W = (w0, w1, w2)
    rep = lax.axis_index("replica")
    fs = lax.axis_index("fsdp")
    core = lax.axis_index("tensor")
    pos = {"x": lax.rem(fs, 4), "y": lax.div(fs, 4), "z": rep}

    def nbr(axis, step):
        c = dict(pos)
        c[axis] = mod4(pos[axis] + step)
        return (c["z"], c["y"] * 4 + c["x"], core)

    other = (rep, fs, 1 - core)

    def remote(src, dst, ss_, rs_, dev):
        return pltpu.make_async_remote_copy(
            src_ref=src, dst_ref=dst, send_sem=ss_, recv_sem=rs_, device_id=dev, device_id_type=MESH
        )

    pending = []

    def go(copy):
        copy.start()
        pending.append(copy)

    l_ex = pltpu.make_async_copy(exps, ex, loc.at[0])
    l_ex.start()
    l_fr = pltpu.make_async_copy(frag.at[rep], fb.at[0], loc.at[1])
    l_fr.start()
    l_bs = pltpu.make_async_copy(base, bs, loc.at[2])
    l_bs.start()
    l_ms = pltpu.make_async_copy(mom, ms, loc.at[3])
    l_ms.start()
    l_gn = pltpu.make_async_copy(gain, gb, loc.at[4])
    l_gn.start()

    barrier = pltpu.get_barrier_semaphore()
    peers = [nbr(a, s) for a in "xyz" for s in (1, -1)] + [other]
    for p in peers:
        pl.semaphore_signal(barrier, inc=1, device_id=p, device_id_type=MESH)

    l_ex.wait()
    eb[...] = ex[...].astype(F32).astype(BF16)

    def window(d):
        return eb.at[:, pl.ds(pl.multiple_of(128 * lax.div(3 * d, 2), 128), 256)]

    off = 64 * lax.rem(rep, 2)

    def expand(slot):
        e = (window(rep)[...] if slot == 0 else er[slot]).astype(F32)
        j = lax.broadcasted_iota(jnp.int32, (BLOCK, KVW), 0)
        n = lax.broadcasted_iota(jnp.int32, (BLOCK, KVW), 1)
        pick = jnp.where(j == lax.div(n, BLOCK), 1.0, 0.0).astype(BF16)
        for ref, sign in ((sc, 1.0), (iv, -1.0)):
            small = jnp.exp2(sign * e).astype(BF16)
            full = lax.dot_general(small, pick, (((0,), (0,)), ((), ())), preferred_element_type=F32)
            ref[slot] = full.astype(BF16)

    expand(0)
    l_gn.wait()
    gf[...] = gb[...].astype(F32)
    first = 6 * fs + lax.div(3 * rep, 2)
    i = lax.broadcasted_iota(jnp.int32, (128, 128), 0)
    l = lax.broadcasted_iota(jnp.int32, (128, 128), 1)
    for h in range(2):
        row = jnp.broadcast_to(gf[pl.ds(first + h, 1), :], (128, 128))
        column = jnp.sum(jnp.where(i == l, row, 0.0), axis=1, keepdims=True)
        gn[pl.ds(128 * h, 128), :] = jnp.broadcast_to(column, (128, 128))
    acc[...] = jnp.zeros_like(acc)

    pl.semaphore_wait(barrier, len(peers))

    up, down = nbr("z", 1), nbr("z", -1)
    zu, zd, zo = mod4(rep + 1), mod4(rep - 1), mod4(rep + 2)

    e_cp = [
        remote(window(zo), erl, e_snd.at[0], e_rcv.at[0], up),
        remote(window(zu), er.at[1], e_snd.at[1], e_rcv.at[1], up),
        remote(window(zd), er.at[2], e_snd.at[2], e_rcv.at[2], down),
        remote(erl, er.at[3], e_snd.at[3], e_rcv.at[3], up),
    ]

    def cols(p):
        c, lo, width, _ = PARTS[p]
        return pl.ds(CLS[c][0] + lo, width)

    H = ROWS // 2

    def a2a(p):
        k = 6 * p
        cc = cols(p)
        return [
            remote(frag.at[zo, pl.ds(0, H), cc], rl.at[0, :, cc], a_snd.at[k], a_rcv.at[k], up),
            remote(frag.at[zo, pl.ds(H, H), cc], rl.at[1, :, cc], a_snd.at[k + 1], a_rcv.at[k + 1], down),
            remote(frag.at[zu, :, cc], fb.at[1, :, cc], a_snd.at[k + 2], a_rcv.at[k + 2], up),
            remote(frag.at[zd, :, cc], fb.at[2, :, cc], a_snd.at[k + 3], a_rcv.at[k + 3], down),
            remote(rl.at[0, :, cc], fb.at[3, pl.ds(0, H), cc], a_snd.at[k + 4], a_rcv.at[k + 4], up),
            remote(rl.at[1, :, cc], fb.at[3, pl.ds(H, H), cc], a_snd.at[k + 5], a_rcv.at[k + 5], down),
        ]

    for m in e_cp[:3]:
        go(m)
    mine = pl.ds(pl.multiple_of(core * TOK, TOK), TOK)
    t_cp = remote(tokens, tok.at[mine, :], t_snd.at[0], t_rcv.at[0], other)
    l_tk = pltpu.make_async_copy(tokens, tok.at[mine, :], loc.at[5])

    def prepare():
        for s in (1, 2, 3):
            e_cp[s].wait_recv()
            expand(s)
        l_fr.wait()
        l_bs.wait()
        l_ms.wait()

    def encode(p):
        c, sub, width, _ = PARTS[p]
        lo = CLS[c][0] + sub
        row0 = pl.multiple_of(rep * ROWS, ROWS)

        def step(t, carry):
            rr = pl.ds(pl.multiple_of(t * SLAB, SLAB), SLAB)
            wr = pl.ds(pl.multiple_of(row0 + t * SLAB, SLAB), SLAB)
            fr = pl.ds(pl.multiple_of(off + t * SLAB, 16), SLAB)
            g = gn[fr, :]
            for k in range(width // 128):
                cc = pl.ds(lo + 128 * k, 128)
                b = bs[rr, cc]
                total = jnp.zeros((SLAB, 128), F32)
                for s in range(4):
                    v = (b - fb[s, rr, cc].astype(F32)) * iv[s, fr, cc].astype(F32)
                    m = jnp.abs(v)
                    level = jnp.zeros_like(m)
                    for mid, val in THRESH:
                        level = jnp.where(m >= mid, val, level)
                    total = total + jnp.where(v < 0.0, -level, level) * sc[s, fr, cc].astype(F32)
                grad = total * 0.25
                nm = MOMENTUM_COEF * ms[rr, cc] + grad
                nb = b - OUTER_RATE * (grad + MOMENTUM_COEF * nm)
                gr[rr, cc] = grad
                W[c][pos["y"], pos["x"], wr, pl.ds(sub + 128 * k, 128)] = (nb * g).astype(BF16)
            return carry

        lax.fori_loop(0, ROWS // SLAB, step, 0)

    def place(p, **at):
        half = at.pop("half", None)
        xs, ys = at.get("x", slice(None)), at.get("y", slice(None))
        if "z" in at:
            r0, n = at["z"] * ROWS, ROWS
        else:
            r0, n = 0, FROWS
        if half is not None:
            n = n // 2
            r0 = r0 + half * n
        if not isinstance(r0, int):
            r0 = pl.multiple_of(r0, 96)
        c, lo, width, _ = PARTS[p]
        return W[c].at[ys, xs, pl.ds(r0, n), pl.ds(lo, width)]

    M = {}
    OFF = (0, 1, -1, 2)
    used = [0]

    def both(*pair):
        out = []
        for j, s in enumerate((1, -1)):
            axis, ref = pair[j]
            out.append(remote(ref, ref, g_snd.at[used[0]], g_rcv.at[used[0]], nbr(axis, s)))
            used[0] += 1
        return out

    def full(p, axis, **fixed):
        here = place(p, **fixed, **{axis: pos[axis]})
        return both((axis, here), (axis, here))

    def half(p, axis, **fixed):
        return both(
            *[(axis, place(p, **fixed, **{axis: mod4(pos[axis] - s), "half": j})) for j, s in enumerate((1, -1))]
        )

    for p in range(len(PARTS)):
        m = a2a(p)
        M["r", p], M["d", p], M["f", p] = m[:2], m[2:4], m[4:]
        a, b, l = PARTS[p][3]
        R, S = (a, b) if b == "z" else (b, a)
        at = {b: pos[b], l: pos[l]}
        M["1", p], M["1h", p] = full(p, a, **at), half(p, a, **at)
        for i in range(4):
            at = {a: mod4(pos[a] + OFF[i]), l: pos[l]}
            M["2", p, i], M["2h", p, i] = full(p, b, **at), half(p, b, **at)
            M["3", p, i] = full(p, l, **{R: pos[R], S: mod4(pos[S] + OFF[i])})
            M["3h", p, i] = half(p, l, **{R: mod4(pos[R] + OFF[i])})
            if i:
                M["3", p, 3 + i] = full(p, l, **{R: mod4(pos[R] + OFF[i])})

    def mm(c, count, coords):
        lo, width = CLS[c]
        cc = pl.ds(lo, width)

        def chunk(t, carry):
            yy, xx = coords(t)
            kk = pl.ds(pl.multiple_of((yy * 4 + xx) * FROWS, FROWS), FROWS)

            def block(m, carry):
                mr = pl.ds(pl.multiple_of(m * 256, 256), 256)
                acc[mr, cc] += jnp.dot(tok[mr, kk], W[c][yy, xx], preferred_element_type=F32)
                return carry

            return lax.fori_loop(0, 3, block, carry)

        lax.fori_loop(0, count, chunk, 0)

    def offset(i):
        return i + lax.div(i, 2) - 2 * lax.div(i, 3)

    def mm_near(c, i):
        if c == 1:
            yy = mod4(pos["y"] + OFF[i])
            mm(c, 3, lambda t: (yy, mod4(pos["x"] + offset(t))))
        else:
            xx = mod4(pos["x"] + OFF[i])
            mm(c, 3, lambda t: (mod4(pos["y"] + offset(t)), xx))

    def mm_far(c, i):
        if c == 1:
            mm(c, 1, lambda t: (mod4(pos["y"] + OFF[i]), mod4(pos["x"] + 2)))
        else:
            mm(c, 1, lambda t: (mod4(pos["y"] + 2), mod4(pos["x"] + OFF[i])))

    def mm_level(c, i):
        def coords(t):
            turn = lax.div(t, i + 1)
            iy = i * (1 - turn) + (t - i - 1) * turn
            ix = t * (1 - turn) + i * turn
            return mod4(pos["y"] + offset(iy)), mod4(pos["x"] + offset(ix))

        mm(c, 2 * i + 1, coords)

    def squares(i):
        rr = pl.ds(pl.multiple_of(core * TOK + i * 128, 128), 128)

        def step(t, s):
            for k in range(4):
                v = tok[rr, pl.ds(pl.multiple_of(t * 512 + k * 128, 128), 128)].astype(F32)
                s = s + v * v
            return s

        s = lax.fori_loop(0, D // 512, step, jnp.zeros((128, 128), F32))
        mean = jnp.sum(s, axis=1, keepdims=True) * (1.0 / D)
        ss[rr, :] = jnp.broadcast_to(lax.rsqrt(mean + 1e-05) * (D ** -0.5), (128, 128))

    s_cp = remote(ss.at[mine, :], ss.at[mine, :], t_snd.at[1], t_rcv.at[1], other)
    outs = []
    left = []
    seen = set()

    def once(name):
        new = name not in seen
        seen.add(name)
        return new

    for kind, *key in SCHEDULE:
        key = tuple(key)
        if kind == "S":
            for m in M[key]:
                m.start()
            left.append(key)
        elif kind == "W":
            if once("wait"):
                go(t_cp)
                l_tk.start()
                e_cp[0].wait_recv()
                go(e_cp[3])
            if key == ("d", 0):
                prepare()
            for m in M[key]:
                m.wait_recv()
        elif kind == "D":
            for m in M[key]:
                m.wait_send()
            left.remove(key)
        elif kind == "E":
            encode(*key)
            left_to_encode = len(PARTS) - 1 - key[0]
            if left_to_encode == 0:
                outs.append(pltpu.make_async_copy(gr, grad_out, o_sem.at[0]))
                outs[0].start()
        elif key[0] == "sq":
            if once("own tokens"):
                l_tk.wait()
            squares(key[1])
            if key[1] == 2:
                go(s_cp)
        else:
            if once("all tokens"):
                t_cp.wait_recv()
            {"near": mm_near, "far": mm_far, "all": mm_level}[key[3]](key[1], key[2])
    s_cp.wait_recv()

    for m in range(3):
        mr = pl.ds(m * 256, 256)

        def scale(k, carry):
            cc = pl.ds(pl.multiple_of(k * 128, 128), 128)
            kv[mr, cc] = (acc[mr, cc] * ss[mr, :]).astype(BF16)
            return carry

        lax.fori_loop(0, KVW // 128, scale, 0)
        o = pltpu.make_async_copy(kv.at[mr, :], kv_out.at[mr, :], o_sem.at[1 + m])
        o.start()
        outs.append(o)
    for key in left:
        for m in M[key]:
            m.wait_send()
    for p in pending:
        p.wait_send()
    for o in outs:
        o.wait()


def body(tokens, norm_gain, fragment, exponents, base_weight, momentum):
    any_ = pl.BlockSpec(memory_space=pl.ANY)
    dma = pltpu.SemaphoreType.DMA
    vm = pltpu.VMEM
    grad, keys_values = pl.pallas_call(
        kernel,
        out_shape=(
            jax.ShapeDtypeStruct((ROWS, KVW), F32),
            jax.ShapeDtypeStruct((2 * TOK, KVW), BF16),
        ),
        in_specs=[any_] * 6,
        out_specs=[any_] * 2,
        scratch_shapes=[
            *[vm((4, 4, FROWS, width), BF16) for _, width in CLS],
            vm((2 * TOK, D), BF16),
            vm((2 * TOK, KVW), F32),
            vm((2 * TOK, KVW), BF16),
            vm((4, ROWS, KVW), BF16),
            vm((2, ROWS // 2, KVW), BF16),
            vm((ROWS, KVW), F32),
            vm((ROWS, KVW), F32),
            vm((ROWS, KVW), F32),
            vm((D // 128, 128), BF16),
            vm((D // 128, 128), F32),
            vm((256, 128), F32),
            vm((BLOCK, 4 * ROWS), jnp.int32),
            vm((BLOCK, 4 * ROWS), BF16),
            vm((4, BLOCK, 256), BF16),
            vm((BLOCK, 256), BF16),
            vm((4, 256, KVW), BF16),
            vm((4, 256, KVW), BF16),
            vm((2 * TOK, 128), F32),
            dma((6,)),
            dma((6 * len(PARTS),)),
            dma((6 * len(PARTS),)),
            dma((4,)),
            dma((4,)),
            dma((2,)),
            dma((2,)),
            dma((42 * len(PARTS),)),
            dma((42 * len(PARTS),)),
            dma((4,)),
        ],
        compiler_params=pltpu.CompilerParams(
            collective_id=0, has_side_effects=True, vmem_limit_bytes=62 * 1024 * 1024
        ),
        cost_estimate=pl.CostEstimate(flops=2 * 768 * 12288 * 1024, bytes_accessed=30_000_000, transcendentals=0),
    )(
        tokens,
        norm_gain.reshape(D // 128, 128),
        fragment.reshape(4, ROWS, KVW),
        exponents[0].T,
        base_weight,
        momentum,
    )
    new_momentum = MOMENTUM_COEF * momentum + grad
    new_base = base_weight - OUTER_RATE * (grad + MOMENTUM_COEF * new_momentum)
    return new_base, new_momentum, keys_values


def solution(mesh):
    in_specs = (
        P(("replica", "fsdp", "tensor"), None),
        P(),
        P("replica", "fsdp", "tensor"),
        P("replica", "fsdp", "tensor"),
        P(("fsdp", "replica"), "tensor"),
        P(("fsdp", "replica"), "tensor"),
    )
    out_specs = (
        P(("fsdp", "replica"), "tensor"),
        P(("fsdp", "replica"), "tensor"),
        P(("replica", "fsdp"), "tensor"),
    )
    return jax.shard_map(body, mesh=mesh, in_specs=in_specs, out_specs=out_specs, check_vma=False)
```

```python
import jax
import jax.numpy as jnp
from jax import lax
from jax.experimental import pallas as pl
from jax.experimental.pallas import tpu as pltpu
from jax.sharding import PartitionSpec as P

MESH = pl.DeviceIdType.MESH
F32, BF16 = jnp.float32, jnp.bfloat16
D, KVW, BLOCK, TOK = 12288, 1024, 32, 384
ROWS = 192
FROWS = 768
SLAB = 48
OUTER_RATE = 0.7
MOMENTUM_COEF = 0.9
CLS = ((0, 256), (256, 384), (640, 384))
PARTS = (
    (0, 0, 128, ("x", "y", "z")),
    (0, 128, 128, ("y", "x", "z")),
    (1, 0, 128, ("z", "y", "x")),
    (2, 0, 128, ("z", "x", "y")),
    (1, 128, 256, ("y", "z", "x")),
    (2, 128, 256, ("x", "z", "y")),
)

SCHEDULE = (
    ("S", "r", 0), ("S", "d", 0), ("S", "r", 1), ("S", "d", 1), ("W", "r", 0), ("S", "f", 0), ("S", "r", 2),
    ("W", "r", 1), ("S", "f", 1), ("S", "d", 2), ("S", "r", 3), ("W", "d", 0), ("W", "f", 0), ("E", 0), ("S", "1", 0),
    ("S", "2", 0, 0), ("D", "r", 0), ("W", "r", 2), ("S", "f", 2), ("S", "d", 3), ("W", "d", 1), ("W", "f", 1),
    ("E", 1), ("S", "2", 1, 0), ("S", "1", 1), ("D", "r", 1), ("D", "d", 0), ("W", "r", 3), ("S", "f", 3),
    ("S", "r", 4), ("W", "1", 0), ("S", "1h", 0), ("W", "2", 0, 0), ("S", "2h", 0, 0), ("S", "2", 0, 1),
    ("S", "2", 0, 2), ("D", "d", 1), ("D", "f", 0), ("S", "d", 4), ("W", "d", 2), ("W", "f", 2), ("E", 2),
    ("W", "2", 1, 0), ("S", "2h", 1, 0), ("W", "1", 1), ("S", "2", 1, 1), ("S", "1h", 1), ("S", "2", 1, 2),
    ("W", "1h", 0), ("S", "2", 0, 3), ("S", "2", 2, 0), ("S", "3", 2, 0), ("D", "r", 2), ("D", "f", 1), ("D", "d", 2),
    ("D", "r", 3), ("W", "r", 4), ("S", "f", 4), ("W", "d", 3), ("W", "f", 3), ("E", 3), ("S", "r", 5),
    ("S", "2", 3, 0), ("S", "3", 3, 0), ("D", "f", 2), ("S", "d", 5), ("D", "2", 0, 0), ("W", "2", 0, 1),
    ("S", "2h", 0, 1), ("S", "1", 2), ("D", "1", 0), ("W", "1h", 1), ("S", "2", 1, 3), ("D", "1", 1),
    ("W", "2", 0, 2), ("S", "2h", 0, 2), ("D", "d", 3), ("D", "f", 3), ("S", "1", 3), ("D", "2", 1, 0),
    ("D", "1h", 0), ("W", "2", 1, 1), ("S", "2h", 1, 1), ("W", "d", 4), ("W", "f", 4), ("E", 4), ("D", "2h", 0, 0),
    ("S", "1", 4), ("W", "2", 1, 2), ("S", "2h", 1, 2), ("S", "3", 4, 0), ("W", "2", 0, 3), ("S", "2h", 0, 3),
    ("W", "2", 2, 0), ("S", "2h", 2, 0), ("C", "tk", 0), ("D", "2h", 1, 0), ("W", "2", 3, 0), ("S", "2h", 3, 0),
    ("D", "r", 4), ("D", "d", 4), ("W", "r", 5), ("S", "f", 5), ("S", "2", 4, 0), ("C", "tk", 1), ("W", "2", 1, 3),
    ("S", "2h", 1, 3), ("D", "2", 0, 1), ("D", "2", 0, 2), ("D", "1h", 1), ("W", "1", 2), ("S", "2", 2, 1),
    ("S", "2", 2, 2), ("D", "2", 1, 1), ("W", "1", 3), ("S", "2", 3, 1), ("S", "2", 3, 2), ("D", "f", 4),
    ("S", "1h", 2), ("S", "1h", 3), ("S", "3", 3, 1), ("C", "tk", 2), ("D", "2", 1, 2), ("D", "3", 2, 0),
    ("S", "3", 2, 1), ("D", "r", 5), ("S", "3", 0, 0), ("D", "2", 0, 3), ("D", "2", 2, 0), ("S", "3", 3, 2),
    ("D", "2", 3, 0), ("D", "2h", 1, 1), ("S", "3", 2, 2), ("S", "3", 1, 0), ("C", "tk", 3), ("W", "d", 5),
    ("W", "f", 5), ("E", 5), ("D", "2h", 0, 1), ("D", "2h", 0, 2), ("D", "3", 3, 0), ("W", "1", 4), ("S", "1h", 4),
    ("D", "2", 1, 3), ("D", "2h", 1, 2), ("S", "1", 5), ("D", "1", 2), ("D", "1", 3), ("S", "2", 4, 1),
    ("D", "2h", 0, 3), ("D", "2h", 2, 0), ("W", "2", 2, 1), ("S", "2h", 2, 1), ("W", "2", 2, 2), ("S", "2h", 2, 2),
    ("W", "1h", 2), ("S", "2", 2, 3), ("D", "2h", 3, 0), ("W", "2", 3, 1), ("S", "2h", 3, 1), ("D", "d", 5),
    ("S", "2", 4, 2), ("D", "2h", 1, 3), ("W", "2", 3, 2), ("S", "2h", 3, 2), ("W", "1h", 3), ("S", "2", 3, 3),
    ("S", "2", 5, 0), ("S", "3", 5, 0), ("C", "tk", 4), ("C", "tk", 5), ("W", "2", 4, 0), ("S", "3", 4, 1),
    ("D", "1", 4), ("S", "3", 3, 3), ("D", "f", 5), ("D", "1h", 2), ("D", "1h", 3), ("S", "2h", 4, 0), ("W", "1h", 4),
    ("S", "2", 4, 3), ("C", "tk", 6), ("D", "2", 2, 1), ("D", "2", 2, 2), ("D", "3", 3, 1), ("W", "2", 2, 3),
    ("S", "2h", 2, 3), ("D", "3", 4, 0), ("D", "2", 3, 1), ("D", "2", 3, 2), ("S", "3", 4, 2), ("D", "3", 2, 1),
    ("W", "2", 3, 3), ("S", "2h", 3, 3), ("D", "3", 3, 2), ("S", "3", 3, 4), ("C", "tk", 7), ("D", "3", 2, 2),
    ("W", "1", 5), ("S", "1h", 5), ("D", "3", 0, 0), ("D", "2", 4, 0), ("D", "3", 1, 0), ("S", "2", 5, 1),
    ("W", "2", 4, 1), ("S", "2h", 4, 1), ("D", "2h", 3, 1), ("D", "2h", 3, 2), ("S", "3", 2, 3), ("D", "2h", 2, 1),
    ("D", "1h", 4), ("D", "2h", 2, 2), ("D", "2", 2, 3), ("W", "3", 3, 0), ("W", "3", 3, 1), ("W", "3", 3, 2),
    ("W", "3", 3, 3), ("S", "3h", 3, 0), ("S", "2", 5, 2), ("W", "2h", 4, 0), ("S", "3", 4, 3), ("D", "3", 3, 3),
    ("S", "3", 3, 5), ("W", "2", 4, 2), ("S", "2h", 4, 2), ("D", "2", 3, 3), ("D", "1", 5), ("S", "3", 2, 4),
    ("D", "2", 4, 1), ("W", "2", 5, 0), ("S", "2h", 5, 0), ("D", "2h", 4, 0), ("W", "1h", 5), ("S", "2", 5, 3),
    ("D", "2h", 2, 3), ("D", "3", 5, 0), ("S", "3", 5, 1), ("C", "sq", 0), ("D", "2", 4, 2), ("D", "2", 5, 0),
    ("W", "2", 4, 3), ("S", "2h", 4, 3), ("D", "2h", 3, 3), ("D", "3", 4, 1), ("D", "1h", 5), ("W", "2h", 4, 1),
    ("S", "3", 4, 4), ("S", "3", 5, 2), ("W", "3", 2, 0), ("W", "3", 2, 1), ("W", "3", 2, 2), ("W", "3", 2, 3),
    ("W", "3", 4, 0), ("W", "3", 4, 1), ("W", "3", 4, 2), ("W", "3", 4, 3), ("C", "mm", 1, 0, "near"),
    ("D", "2h", 4, 1), ("D", "2", 4, 3), ("W", "2", 5, 1), ("S", "2h", 5, 1), ("D", "3", 3, 4), ("D", "3h", 3, 0),
    ("W", "2h", 5, 0), ("S", "3", 5, 3), ("S", "3", 0, 1), ("W", "2", 5, 2), ("S", "2h", 5, 2), ("C", "sq", 1),
    ("W", "3", 3, 4), ("S", "3h", 3, 1), ("C", "sq", 2), ("D", "2h", 4, 2), ("S", "3", 1, 1), ("D", "2", 5, 1),
    ("W", "2", 5, 3), ("S", "2h", 5, 3), ("W", "2h", 3, 0), ("W", "2h", 3, 1), ("W", "2h", 3, 2), ("W", "2h", 3, 3),
    ("S", "3", 3, 6), ("D", "2h", 5, 0), ("S", "3", 0, 2), ("D", "3", 4, 2), ("D", "3", 2, 3), ("D", "3", 4, 3),
    ("D", "3", 2, 4), ("S", "3h", 2, 0), ("D", "2", 5, 2), ("S", "3", 1, 2), ("D", "2h", 4, 3), ("S", "3", 0, 3),
    ("S", "3h", 4, 0), ("S", "3", 1, 3), ("W", "3", 5, 0), ("W", "3", 5, 1), ("W", "3", 5, 2), ("W", "3", 5, 3),
    ("C", "mm", 2, 0, "near"), ("D", "3", 3, 5), ("D", "3", 5, 1), ("D", "3", 5, 2), ("W", "2h", 5, 1),
    ("S", "3", 5, 4), ("D", "2", 5, 3), ("D", "2h", 5, 1), ("S", "3", 0, 4), ("W", "3", 2, 4), ("W", "3", 4, 4),
    ("C", "mm", 1, 1, "near"), ("S", "3", 2, 5), ("D", "3", 0, 1), ("D", "2h", 5, 2), ("S", "3", 1, 4),
    ("W", "3h", 2, 0), ("W", "3h", 4, 0), ("C", "mm", 1, 0, "far"), ("D", "3", 4, 4), ("D", "3h", 2, 0),
    ("W", "2h", 4, 2), ("S", "3", 4, 5), ("D", "3", 5, 3), ("D", "3h", 3, 1), ("D", "3", 3, 6), ("S", "3h", 5, 0),
    ("D", "3", 1, 1), ("D", "2h", 5, 3), ("D", "3", 0, 2), ("D", "3", 1, 2), ("D", "3", 0, 3), ("D", "3", 1, 3),
    ("W", "3", 0, 0), ("W", "3", 0, 1), ("W", "3", 0, 2), ("W", "3", 0, 3), ("S", "3h", 0, 0), ("W", "3", 1, 0),
    ("W", "3", 1, 1), ("W", "3", 1, 2), ("W", "3", 1, 3), ("S", "3h", 1, 0), ("W", "2h", 5, 2), ("S", "3", 5, 5),
    ("S", "3", 0, 5), ("W", "3", 5, 4), ("C", "mm", 2, 1, "near"), ("D", "3h", 4, 0), ("S", "3h", 2, 1),
    ("D", "3", 0, 4), ("S", "3", 1, 5), ("W", "3h", 0, 0), ("W", "3h", 1, 0), ("C", "mm", 0, 0, "all"),
    ("D", "3", 2, 5), ("S", "3h", 4, 1), ("W", "3h", 3, 0), ("W", "3h", 5, 0), ("C", "mm", 2, 0, "far"),
    ("D", "3", 5, 4), ("S", "3h", 5, 1), ("D", "3", 1, 4), ("D", "3h", 0, 0), ("W", "3", 0, 4), ("S", "3h", 0, 1),
    ("W", "2h", 2, 0), ("W", "2h", 2, 1), ("W", "2h", 2, 2), ("W", "2h", 2, 3), ("S", "3", 2, 6), ("W", "3", 2, 5),
    ("W", "3", 4, 5), ("C", "mm", 1, 2, "near"), ("D", "3h", 1, 0), ("W", "3", 1, 4), ("S", "3h", 1, 1),
    ("D", "3h", 5, 0), ("W", "2h", 5, 3), ("S", "3", 5, 6), ("W", "2h", 0, 0), ("W", "2h", 0, 1), ("W", "2h", 0, 2),
    ("W", "2h", 0, 3), ("S", "3", 0, 6), ("D", "3", 4, 5), ("D", "3h", 2, 1), ("W", "2h", 4, 3), ("S", "3", 4, 6),
    ("W", "3", 3, 5), ("W", "3", 5, 5), ("C", "mm", 2, 2, "near"), ("W", "3h", 2, 1), ("W", "3h", 4, 1),
    ("C", "mm", 1, 1, "far"), ("D", "3", 0, 5), ("W", "2h", 1, 0), ("W", "2h", 1, 1), ("W", "2h", 1, 2),
    ("W", "2h", 1, 3), ("S", "3", 1, 6), ("W", "3h", 0, 1), ("W", "3h", 1, 1), ("C", "mm", 0, 1, "all"),
    ("W", "3h", 3, 1), ("W", "3h", 5, 1), ("C", "mm", 2, 1, "far"), ("D", "3", 5, 5), ("S", "3h", 3, 2),
    ("D", "3h", 0, 1), ("D", "3", 1, 5), ("W", "3", 0, 5), ("S", "3h", 0, 2), ("D", "3h", 4, 1), ("S", "3h", 2, 2),
    ("D", "3h", 5, 1), ("S", "3h", 5, 2), ("D", "3h", 1, 1), ("W", "3", 1, 5), ("S", "3h", 1, 2), ("D", "3", 2, 6),
    ("S", "3h", 4, 2), ("W", "3", 0, 6), ("S", "3h", 0, 3), ("W", "3", 3, 6), ("W", "3", 5, 6),
    ("C", "mm", 2, 3, "near"), ("S", "3h", 3, 3), ("D", "3", 0, 6), ("W", "3", 1, 6), ("S", "3h", 1, 3),
    ("W", "3", 2, 6), ("S", "3h", 2, 3), ("S", "3h", 5, 3), ("W", "3", 4, 6), ("C", "mm", 1, 3, "near"),
    ("D", "3", 4, 6), ("S", "3h", 4, 3), ("W", "3h", 0, 2), ("W", "3h", 1, 2), ("C", "mm", 0, 2, "all"),
    ("W", "3h", 0, 3), ("W", "3h", 1, 3), ("C", "mm", 0, 3, "all"), ("W", "3h", 2, 2), ("W", "3h", 4, 2),
    ("C", "mm", 1, 2, "far"), ("W", "3h", 2, 3), ("W", "3h", 4, 3), ("C", "mm", 1, 3, "far"), ("W", "3h", 3, 2),
    ("W", "3h", 5, 2), ("C", "mm", 2, 2, "far"), ("W", "3h", 3, 3), ("W", "3h", 5, 3), ("C", "mm", 2, 3, "far"),
)

THRESH = ((0.25, 0.5), (0.75, 1.0), (1.25, 1.5), (1.75, 2.0), (2.5, 3.0), (3.5, 4.0), (5.0, 6.0))


def mod4(v):
    return lax.rem(v + 8, 4)


def kernel(
    tokens, gain, frag, exps, base, mom,
    grad_out, kv_out,
    w0, w1, w2, tok, acc, kv, fb, rl, bs, ms, gr, gb, gf, gn, ex, eb, er, erl, sc, iv, ss,
    loc, a_snd, a_rcv, e_snd, e_rcv, t_snd, t_rcv, g_snd, g_rcv, o_sem,
):
    W = (w0, w1, w2)
    rep = lax.axis_index("replica")
    fs = lax.axis_index("fsdp")
    core = lax.axis_index("tensor")
    pos = {"x": lax.rem(fs, 4), "y": lax.div(fs, 4), "z": rep}

    def nbr(axis, step):
        c = dict(pos)
        c[axis] = mod4(pos[axis] + step)
        return (c["z"], c["y"] * 4 + c["x"], core)

    other = (rep, fs, 1 - core)

    def remote(src, dst, ss_, rs_, dev):
        return pltpu.make_async_remote_copy(
            src_ref=src, dst_ref=dst, send_sem=ss_, recv_sem=rs_, device_id=dev, device_id_type=MESH
        )

    pending = []

    def go(copy):
        copy.start()
        pending.append(copy)

    barrier = pltpu.get_barrier_semaphore()
    peers = [nbr(a, s) for a in "xyz" for s in (1, -1)] + [other]
    for p in peers:
        pl.semaphore_signal(barrier, inc=1, device_id=p, device_id_type=MESH)

    l_ex = pltpu.make_async_copy(exps, ex, loc.at[0])
    l_ex.start()
    l_fr = pltpu.make_async_copy(frag.at[rep], fb.at[0], loc.at[1])
    l_fr.start()
    l_bs = pltpu.make_async_copy(base, bs, loc.at[2])
    l_bs.start()
    l_ms = pltpu.make_async_copy(mom, ms, loc.at[3])
    l_ms.start()
    l_gn = pltpu.make_async_copy(gain, gb, loc.at[4])
    l_gn.start()

    pl.semaphore_wait(barrier, len(peers))

    up, down = nbr("z", 1), nbr("z", -1)
    zu, zd, zo = mod4(rep + 1), mod4(rep - 1), mod4(rep + 2)

    def window(d):
        return eb.at[:, pl.ds(pl.multiple_of(128 * lax.div(3 * d, 2), 128), 256)]

    off = 64 * lax.rem(rep, 2)

    def expand(slot):
        e = (window(rep)[...] if slot == 0 else er[slot]).astype(F32)
        j = lax.broadcasted_iota(jnp.int32, (BLOCK, KVW), 0)
        n = lax.broadcasted_iota(jnp.int32, (BLOCK, KVW), 1)
        pick = jnp.where(j == lax.div(n, BLOCK), 1.0, 0.0).astype(BF16)
        for ref, sign in ((sc, 1.0), (iv, -1.0)):
            small = jnp.exp2(sign * e).astype(BF16)
            full = lax.dot_general(small, pick, (((0,), (0,)), ((), ())), preferred_element_type=F32)
            ref[slot] = full.astype(BF16)

    e_cp = [
        remote(window(zo), erl, e_snd.at[0], e_rcv.at[0], up),
        remote(window(zu), er.at[1], e_snd.at[1], e_rcv.at[1], up),
        remote(window(zd), er.at[2], e_snd.at[2], e_rcv.at[2], down),
        remote(erl, er.at[3], e_snd.at[3], e_rcv.at[3], up),
    ]

    def cols(p):
        c, lo, width, _ = PARTS[p]
        return pl.ds(CLS[c][0] + lo, width)

    H = ROWS // 2

    def a2a(p):
        k = 6 * p
        cc = cols(p)
        return [
            remote(frag.at[zo, pl.ds(0, H), cc], rl.at[0, :, cc], a_snd.at[k], a_rcv.at[k], up),
            remote(frag.at[zo, pl.ds(H, H), cc], rl.at[1, :, cc], a_snd.at[k + 1], a_rcv.at[k + 1], down),
            remote(frag.at[zu, :, cc], fb.at[1, :, cc], a_snd.at[k + 2], a_rcv.at[k + 2], up),
            remote(frag.at[zd, :, cc], fb.at[2, :, cc], a_snd.at[k + 3], a_rcv.at[k + 3], down),
            remote(rl.at[0, :, cc], fb.at[3, pl.ds(0, H), cc], a_snd.at[k + 4], a_rcv.at[k + 4], up),
            remote(rl.at[1, :, cc], fb.at[3, pl.ds(H, H), cc], a_snd.at[k + 5], a_rcv.at[k + 5], down),
        ]

    mine = pl.ds(pl.multiple_of(core * TOK, TOK), TOK)
    t_cp, l_tk = [], []
    for i in range(8):
        src = tokens.at[pl.ds(i * SLAB, SLAB), :]
        dst = tok.at[pl.ds(pl.multiple_of(core * TOK + i * SLAB, SLAB), SLAB), :]
        t_cp.append(remote(src, dst, t_snd.at[i], t_rcv.at[i], other))
        l_tk.append(pltpu.make_async_copy(src, dst, loc.at[5 + i]))

    def early():
        l_ex.wait()
        eb[...] = ex[...].astype(F32).astype(BF16)
        for m in e_cp[:3]:
            go(m)
        expand(0)
        l_gn.wait()
        gf[...] = gb[...].astype(F32)
        first = 6 * fs + lax.div(3 * rep, 2)
        i = lax.broadcasted_iota(jnp.int32, (128, 128), 0)
        l = lax.broadcasted_iota(jnp.int32, (128, 128), 1)
        for h in range(2):
            row = jnp.broadcast_to(gf[pl.ds(first + h, 1), :], (128, 128))
            column = jnp.sum(jnp.where(i == l, row, 0.0), axis=1, keepdims=True)
            gn[pl.ds(128 * h, 128), :] = jnp.broadcast_to(column, (128, 128))
        e_cp[0].wait_recv()
        go(e_cp[3])

    def prepare():
        for s in (1, 2, 3):
            e_cp[s].wait_recv()
            expand(s)
        l_fr.wait()
        l_bs.wait()
        l_ms.wait()

    def encode(p):
        c, sub, width, _ = PARTS[p]
        lo = CLS[c][0] + sub
        row0 = pl.multiple_of(rep * ROWS, ROWS)

        def step(t, carry):
            rr = pl.ds(pl.multiple_of(t * SLAB, SLAB), SLAB)
            wr = pl.ds(pl.multiple_of(row0 + t * SLAB, SLAB), SLAB)
            fr = pl.ds(pl.multiple_of(off + t * SLAB, 16), SLAB)
            g = gn[fr, :]
            for k in range(width // 128):
                cc = pl.ds(lo + 128 * k, 128)
                b = bs[rr, cc]
                total = jnp.zeros((SLAB, 128), F32)
                for s in range(4):
                    v = (b - fb[s, rr, cc].astype(F32)) * iv[s, fr, cc].astype(F32)
                    m = jnp.abs(v)
                    level = jnp.zeros_like(m)
                    for mid, val in THRESH:
                        level = jnp.where(m >= mid, val, level)
                    total = total + jnp.where(v < 0.0, -level, level) * sc[s, fr, cc].astype(F32)
                grad = total * 0.25
                nm = MOMENTUM_COEF * ms[rr, cc] + grad
                nb = b - OUTER_RATE * (grad + MOMENTUM_COEF * nm)
                gr[rr, cc] = grad
                W[c][pos["y"], pos["x"], wr, pl.ds(sub + 128 * k, 128)] = (nb * g).astype(BF16)
            return carry

        lax.fori_loop(0, ROWS // SLAB, step, 0)

    def place(p, **at):
        half = at.pop("half", None)
        xs, ys = at.get("x", slice(None)), at.get("y", slice(None))
        if "z" in at:
            r0, n = at["z"] * ROWS, ROWS
        else:
            r0, n = 0, FROWS
        if half is not None:
            n = n // 2
            r0 = r0 + half * n
        if not isinstance(r0, int):
            r0 = pl.multiple_of(r0, 96)
        c, lo, width, _ = PARTS[p]
        return W[c].at[ys, xs, pl.ds(r0, n), pl.ds(lo, width)]

    M = {}
    OFF = (0, 1, -1, 2)
    used = [0]

    def both(*pair):
        out = []
        for j, s in enumerate((1, -1)):
            axis, ref = pair[j]
            out.append(remote(ref, ref, g_snd.at[used[0]], g_rcv.at[used[0]], nbr(axis, s)))
            used[0] += 1
        return out

    def full(p, axis, **fixed):
        here = place(p, **fixed, **{axis: pos[axis]})
        return both((axis, here), (axis, here))

    def half(p, axis, **fixed):
        return both(
            *[(axis, place(p, **fixed, **{axis: mod4(pos[axis] - s), "half": j})) for j, s in enumerate((1, -1))]
        )

    for p in range(len(PARTS)):
        m = a2a(p)
        M["r", p], M["d", p], M["f", p] = m[:2], m[2:4], m[4:]
        a, b, l = PARTS[p][3]
        R, S = (a, b) if b == "z" else (b, a)
        at = {b: pos[b], l: pos[l]}
        M["1", p], M["1h", p] = full(p, a, **at), half(p, a, **at)
        for i in range(4):
            at = {a: mod4(pos[a] + OFF[i]), l: pos[l]}
            M["2", p, i], M["2h", p, i] = full(p, b, **at), half(p, b, **at)
            M["3", p, i] = full(p, l, **{R: pos[R], S: mod4(pos[S] + OFF[i])})
            M["3h", p, i] = half(p, l, **{R: mod4(pos[R] + OFF[i])})
            if i:
                M["3", p, 3 + i] = full(p, l, **{R: mod4(pos[R] + OFF[i])})

    def mm(c, count, coords):
        lo, width = CLS[c]
        cc = pl.ds(lo, width)

        def chunk(t, carry):
            yy, xx = coords(t)
            kk = pl.ds(pl.multiple_of((yy * 4 + xx) * FROWS, FROWS), FROWS)

            def block(m, carry):
                mr = pl.ds(pl.multiple_of(m * 256, 256), 256)
                acc[mr, cc] += jnp.dot(tok[mr, kk], W[c][yy, xx], preferred_element_type=F32)
                return carry

            return lax.fori_loop(0, 3, block, carry)

        lax.fori_loop(0, count, chunk, 0)

    def offset(i):
        return i + lax.div(i, 2) - 2 * lax.div(i, 3)

    def mm_near(c, i):
        if c == 1:
            yy = mod4(pos["y"] + OFF[i])
            mm(c, 3, lambda t: (yy, mod4(pos["x"] + offset(t))))
        else:
            xx = mod4(pos["x"] + OFF[i])
            mm(c, 3, lambda t: (mod4(pos["y"] + offset(t)), xx))

    def mm_far(c, i):
        if c == 1:
            mm(c, 1, lambda t: (mod4(pos["y"] + OFF[i]), mod4(pos["x"] + 2)))
        else:
            mm(c, 1, lambda t: (mod4(pos["y"] + 2), mod4(pos["x"] + OFF[i])))

    def mm_level(c, i):
        def coords(t):
            turn = lax.div(t, i + 1)
            iy = i * (1 - turn) + (t - i - 1) * turn
            ix = t * (1 - turn) + i * turn
            return mod4(pos["y"] + offset(iy)), mod4(pos["x"] + offset(ix))

        mm(c, 2 * i + 1, coords)

    def squares(i):
        rr = pl.ds(pl.multiple_of(core * TOK + i * 128, 128), 128)

        def step(t, s):
            for k in range(4):
                v = tok[rr, pl.ds(pl.multiple_of(t * 512 + k * 128, 128), 128)].astype(F32)
                s = s + v * v
            return s

        s = lax.fori_loop(0, D // 512, step, jnp.zeros((128, 128), F32))
        mean = jnp.sum(s, axis=1, keepdims=True) * (1.0 / D)
        ss[rr, :] = jnp.broadcast_to(lax.rsqrt(mean + 1e-05) * (D ** -0.5), (128, 128))

    s_cp = remote(ss.at[mine, :], ss.at[mine, :], t_snd.at[8], t_rcv.at[8], other)
    outs = []
    left = []
    seen = set()

    def once(name):
        new = name not in seen
        seen.add(name)
        return new

    for kind, *key in SCHEDULE:
        key = tuple(key)
        if kind == "S":
            for m in M[key]:
                m.start()
            left.append(key)
        elif kind == "W":
            if once("wait"):
                early()
            if key == ("d", 0):
                prepare()
            for m in M[key]:
                m.wait_recv()
        elif kind == "D":
            for m in M[key]:
                m.wait_send()
            left.remove(key)
        elif kind == "E":
            encode(*key)
            left_to_encode = len(PARTS) - 1 - key[0]
            if left_to_encode == 0:
                outs.append(pltpu.make_async_copy(gr, grad_out, o_sem.at[0]))
                outs[0].start()
        elif key[0] == "tk":
            l_tk[key[1]].start()
            go(t_cp[key[1]])
            if once("total"):
                acc[...] = jnp.zeros_like(acc)
        elif key[0] == "sq":
            if once("own tokens"):
                for t in l_tk:
                    t.wait()
            squares(key[1])
            if key[1] == 2:
                go(s_cp)
        else:
            if once("all tokens"):
                for t in t_cp:
                    t.wait_recv()
            {"near": mm_near, "far": mm_far, "all": mm_level}[key[3]](key[1], key[2])
    s_cp.wait_recv()

    for m in range(3):
        mr = pl.ds(m * 256, 256)

        def scale(k, carry):
            cc = pl.ds(pl.multiple_of(k * 128, 128), 128)
            kv[mr, cc] = (acc[mr, cc] * ss[mr, :]).astype(BF16)
            return carry

        lax.fori_loop(0, KVW // 128, scale, 0)
        o = pltpu.make_async_copy(kv.at[mr, :], kv_out.at[mr, :], o_sem.at[1 + m])
        o.start()
        outs.append(o)
    for key in left:
        for m in M[key]:
            m.wait_send()
    for p in pending:
        p.wait_send()
    for o in outs:
        o.wait()


def body(tokens, norm_gain, fragment, exponents, base_weight, momentum):
    any_ = pl.BlockSpec(memory_space=pl.ANY)
    dma = pltpu.SemaphoreType.DMA
    vm = pltpu.VMEM
    grad, keys_values = pl.pallas_call(
        kernel,
        out_shape=(
            jax.ShapeDtypeStruct((ROWS, KVW), F32),
            jax.ShapeDtypeStruct((2 * TOK, KVW), BF16),
        ),
        in_specs=[any_] * 6,
        out_specs=[any_] * 2,
        scratch_shapes=[
            *[vm((4, 4, FROWS, width), BF16) for _, width in CLS],
            vm((2 * TOK, D), BF16),
            vm((2 * TOK, KVW), F32),
            vm((2 * TOK, KVW), BF16),
            vm((4, ROWS, KVW), BF16),
            vm((2, ROWS // 2, KVW), BF16),
            vm((ROWS, KVW), F32),
            vm((ROWS, KVW), F32),
            vm((ROWS, KVW), F32),
            vm((D // 128, 128), BF16),
            vm((D // 128, 128), F32),
            vm((256, 128), F32),
            vm((BLOCK, 4 * ROWS), jnp.int32),
            vm((BLOCK, 4 * ROWS), BF16),
            vm((4, BLOCK, 256), BF16),
            vm((BLOCK, 256), BF16),
            vm((4, 256, KVW), BF16),
            vm((4, 256, KVW), BF16),
            vm((2 * TOK, 128), F32),
            dma((13,)),
            dma((6 * len(PARTS),)),
            dma((6 * len(PARTS),)),
            dma((4,)),
            dma((4,)),
            dma((9,)),
            dma((9,)),
            dma((42 * len(PARTS),)),
            dma((42 * len(PARTS),)),
            dma((4,)),
        ],
        compiler_params=pltpu.CompilerParams(
            collective_id=0, has_side_effects=True, vmem_limit_bytes=62 * 1024 * 1024
        ),
        cost_estimate=pl.CostEstimate(flops=2 * 768 * 12288 * 1024, bytes_accessed=30_000_000, transcendentals=0),
    )(
        tokens,
        norm_gain.reshape(D // 128, 128),
        fragment.reshape(4, ROWS, KVW),
        exponents[0].T,
        base_weight,
        momentum,
    )
    new_momentum = MOMENTUM_COEF * momentum + grad
    new_base = base_weight - OUTER_RATE * (grad + MOMENTUM_COEF * new_momentum)
    return new_base, new_momentum, keys_values


def solution(mesh):
    in_specs = (
        P(("replica", "fsdp", "tensor"), None),
        P(),
        P("replica", "fsdp", "tensor"),
        P("replica", "fsdp", "tensor"),
        P(("fsdp", "replica"), "tensor"),
        P(("fsdp", "replica"), "tensor"),
    )
    out_specs = (
        P(("fsdp", "replica"), "tensor"),
        P(("fsdp", "replica"), "tensor"),
        P(("replica", "fsdp"), "tensor"),
    )
    return jax.shard_map(body, mesh=mesh, in_specs=in_specs, out_specs=out_specs, check_vma=False)
```

```python
import jax
import jax.numpy as jnp
from jax import lax
from jax.experimental import pallas as pl
from jax.experimental.pallas import tpu as pltpu
from jax.sharding import PartitionSpec as P

MESH = pl.DeviceIdType.MESH
F32, BF16 = jnp.float32, jnp.bfloat16
D, KVW, BLOCK, TOK = 12288, 1024, 32, 384
ROWS = 192
FROWS = 768
SLAB = 48
OUTER_RATE = 0.7
MOMENTUM_COEF = 0.9
CLS = ((0, 256), (256, 384), (640, 384))
PARTS = (
    (0, 0, 128, ("x", "y", "z")),
    (0, 128, 128, ("y", "x", "z")),
    (1, 0, 128, ("z", "y", "x")),
    (2, 0, 128, ("z", "x", "y")),
    (1, 128, 256, ("y", "z", "x")),
    (2, 128, 256, ("x", "z", "y")),
)

SCHEDULE = (
    ("S", "r", 0), ("S", "d", 0), ("S", "r", 1), ("D", "r", 0), ("S", "d", 1), ("D", "d", 0), ("D", "r", 1),
    ("W", "r", 0), ("S", "f", 0), ("S", "r", 2), ("W", "r", 1), ("S", "f", 1), ("D", "d", 1), ("S", "d", 2),
    ("W", "d", 0), ("W", "f", 0), ("E", 0), ("S", "1", 0), ("S", "2", 0, 0), ("D", "f", 0), ("D", "r", 2),
    ("D", "f", 1), ("D", "d", 2), ("W", "r", 2), ("S", "f", 2), ("S", "r", 3), ("W", "d", 1), ("W", "f", 1), ("E", 1),
    ("D", "1", 0), ("S", "2", 1, 0), ("D", "2", 0, 0), ("S", "1", 1), ("D", "f", 2), ("D", "r", 3), ("S", "d", 3),
    ("W", "1", 0), ("S", "1h", 0), ("W", "2", 0, 0), ("S", "2h", 0, 0), ("W", "r", 3), ("S", "f", 3),
    ("S", "2", 0, 1), ("S", "r", 4), ("S", "2", 0, 2), ("W", "d", 2), ("W", "f", 2), ("E", 2), ("D", "d", 3),
    ("D", "f", 3), ("S", "d", 4), ("D", "2", 1, 0), ("D", "1h", 0), ("W", "2", 1, 0), ("S", "2h", 1, 0),
    ("W", "1", 1), ("S", "2", 1, 1), ("D", "1", 1), ("D", "2h", 0, 0), ("S", "1h", 1), ("S", "2", 1, 2),
    ("W", "1h", 0), ("S", "2", 0, 3), ("S", "2", 2, 0), ("D", "2h", 1, 0), ("S", "3", 2, 0), ("W", "d", 3),
    ("W", "f", 3), ("E", 3), ("D", "r", 4), ("W", "r", 4), ("S", "f", 4), ("S", "2", 3, 0), ("D", "2", 0, 1),
    ("D", "2", 0, 2), ("S", "3", 3, 0), ("D", "1h", 1), ("W", "2", 0, 1), ("S", "2h", 0, 1), ("D", "d", 4),
    ("S", "r", 5), ("W", "2", 0, 2), ("S", "2h", 0, 2), ("D", "2", 1, 1), ("W", "1h", 1), ("S", "2", 1, 3),
    ("S", "d", 5), ("D", "f", 4), ("S", "1", 2), ("S", "1", 3), ("D", "2", 1, 2), ("W", "2", 1, 1), ("S", "2h", 1, 1),
    ("W", "d", 4), ("W", "f", 4), ("E", 4), ("D", "3", 2, 0), ("D", "2", 3, 0), ("D", "2h", 1, 1), ("W", "2", 1, 2),
    ("S", "2h", 1, 2), ("D", "2h", 0, 1), ("D", "2", 0, 3), ("D", "2", 2, 0), ("D", "2h", 0, 2), ("D", "3", 3, 0),
    ("S", "1", 4), ("W", "2", 0, 3), ("S", "2h", 0, 3), ("D", "2", 1, 3), ("D", "2h", 1, 2), ("W", "2", 3, 0),
    ("S", "2h", 3, 0), ("W", "2", 2, 0), ("S", "2h", 2, 0), ("W", "2", 1, 3), ("S", "2h", 1, 3), ("S", "3", 4, 0),
    ("C", "tk", 0), ("D", "r", 5), ("D", "1", 2), ("D", "1", 3), ("W", "r", 5), ("S", "f", 5), ("S", "2", 4, 0),
    ("C", "tk", 1), ("D", "2h", 0, 3), ("W", "1", 2), ("S", "2", 2, 1), ("D", "2h", 3, 0), ("D", "2h", 1, 3),
    ("W", "1", 3), ("S", "2", 3, 1), ("D", "2h", 2, 0), ("S", "2", 2, 2), ("S", "2", 3, 2), ("D", "d", 5),
    ("S", "1h", 2), ("S", "1h", 3), ("C", "tk", 2), ("S", "3", 3, 1), ("S", "3", 2, 1), ("S", "3", 0, 0),
    ("S", "3", 3, 2), ("C", "tk", 3), ("S", "3", 2, 2), ("D", "f", 5), ("D", "1h", 2), ("D", "1h", 3),
    ("S", "3", 1, 0), ("W", "d", 5), ("W", "f", 5), ("E", 5), ("D", "1", 4), ("D", "2", 2, 1), ("D", "2", 2, 2),
    ("W", "1", 4), ("S", "1h", 4), ("D", "2", 3, 1), ("D", "3", 4, 0), ("D", "2", 3, 2), ("S", "1", 5),
    ("S", "2", 4, 1), ("D", "3", 3, 1), ("D", "3", 3, 2), ("W", "2", 2, 1), ("S", "2h", 2, 1), ("W", "2", 2, 2),
    ("S", "2h", 2, 2), ("W", "1h", 2), ("S", "2", 2, 3), ("D", "3", 2, 1), ("D", "3", 2, 2), ("W", "2", 3, 1),
    ("S", "2h", 3, 1), ("D", "3", 0, 0), ("D", "2", 4, 0), ("D", "3", 1, 0), ("S", "2", 4, 2), ("W", "2", 3, 2),
    ("S", "2h", 3, 2), ("W", "1h", 3), ("S", "2", 3, 3), ("W", "2", 4, 0), ("S", "2h", 4, 0), ("D", "1h", 4),
    ("S", "3", 5, 0), ("C", "tk", 4), ("S", "2", 5, 0), ("C", "tk", 5), ("D", "2h", 3, 1), ("S", "3", 4, 1),
    ("D", "2h", 2, 1), ("D", "2h", 2, 2), ("S", "3", 3, 3), ("C", "tk", 6), ("W", "1h", 4), ("S", "2", 4, 3),
    ("D", "2", 2, 3), ("W", "2", 2, 3), ("S", "2h", 2, 3), ("D", "2h", 3, 2), ("S", "3", 4, 2), ("C", "tk", 7),
    ("D", "1", 5), ("D", "2", 3, 3), ("W", "1", 5), ("S", "1h", 5), ("W", "2", 3, 3), ("S", "2h", 3, 3),
    ("D", "3", 3, 3), ("D", "2h", 2, 3), ("S", "3", 3, 4), ("D", "2h", 4, 0), ("D", "2", 4, 1), ("S", "2", 5, 1),
    ("S", "3", 2, 3), ("W", "2", 4, 1), ("S", "2h", 4, 1), ("D", "3", 5, 0), ("W", "3", 3, 0), ("W", "3", 3, 1),
    ("W", "3", 3, 2), ("W", "3", 3, 3), ("S", "3h", 3, 0), ("D", "2h", 3, 3), ("W", "2h", 4, 0), ("S", "3", 4, 3),
    ("D", "2", 4, 2), ("S", "2", 5, 2), ("S", "3", 3, 5), ("D", "3", 4, 1), ("D", "1h", 5), ("S", "3", 2, 4),
    ("D", "2", 5, 0), ("W", "2", 4, 2), ("S", "2h", 4, 2), ("W", "2", 5, 0), ("S", "2h", 5, 0), ("W", "1h", 5),
    ("S", "2", 5, 3), ("C", "sq", 0), ("C", "sq", 1), ("D", "3", 3, 4), ("D", "3h", 3, 0), ("S", "3", 5, 1),
    ("D", "3", 4, 2), ("D", "3", 2, 3), ("D", "3", 4, 3), ("W", "2h", 4, 1), ("S", "3", 4, 4), ("D", "2h", 4, 1),
    ("D", "2", 4, 3), ("W", "2", 4, 3), ("S", "2h", 4, 3), ("W", "3", 2, 0), ("W", "3", 2, 1), ("W", "3", 2, 2),
    ("W", "3", 2, 3), ("W", "3", 4, 0), ("W", "3", 4, 1), ("W", "3", 4, 2), ("W", "3", 4, 3),
    ("C", "mm", 1, 0, "near"), ("D", "2", 5, 1), ("D", "2h", 4, 2), ("D", "2h", 5, 0), ("W", "2", 5, 1),
    ("S", "2h", 5, 1), ("D", "3", 3, 5), ("D", "3", 5, 1), ("S", "3", 5, 2), ("C", "sq", 2), ("D", "2", 5, 2),
    ("S", "3", 0, 1), ("W", "2h", 5, 0), ("S", "3", 5, 3), ("D", "2h", 4, 3), ("W", "2", 5, 2), ("S", "2h", 5, 2),
    ("S", "3", 1, 1), ("W", "3", 3, 4), ("S", "3h", 3, 1), ("D", "2", 5, 3), ("S", "3", 0, 2), ("D", "2h", 5, 1),
    ("W", "2", 5, 3), ("S", "2h", 5, 3), ("D", "3", 5, 2), ("W", "2h", 5, 1), ("S", "3", 5, 4), ("D", "3", 2, 4),
    ("S", "3h", 2, 0), ("D", "3", 0, 1), ("S", "3", 1, 2), ("D", "2h", 5, 2), ("S", "3", 0, 3), ("S", "3h", 4, 0),
    ("S", "3", 1, 3), ("W", "3", 5, 0), ("W", "3", 5, 1), ("W", "3", 5, 2), ("W", "3", 5, 3),
    ("C", "mm", 2, 0, "near"), ("D", "3", 1, 1), ("D", "3", 0, 2), ("D", "2h", 5, 3), ("S", "3", 0, 4),
    ("W", "3", 2, 4), ("W", "3", 4, 4), ("C", "mm", 1, 1, "near"), ("D", "3", 4, 4), ("D", "3h", 2, 0),
    ("S", "3", 2, 5), ("D", "3", 1, 2), ("D", "3", 0, 3), ("D", "3", 1, 3), ("S", "3", 1, 4), ("D", "3", 5, 3),
    ("D", "3h", 3, 1), ("S", "3h", 5, 0), ("W", "3h", 2, 0), ("W", "3h", 4, 0), ("C", "mm", 1, 0, "far"),
    ("D", "3h", 4, 0), ("W", "2h", 4, 2), ("S", "3", 4, 5), ("D", "3", 0, 4), ("W", "3", 0, 0), ("W", "3", 0, 1),
    ("W", "3", 0, 2), ("W", "3", 0, 3), ("S", "3h", 0, 0), ("D", "3", 5, 4), ("W", "2h", 5, 2), ("S", "3", 5, 5),
    ("W", "3", 5, 4), ("C", "mm", 2, 1, "near"), ("W", "3", 1, 0), ("W", "3", 1, 1), ("W", "3", 1, 2),
    ("W", "3", 1, 3), ("S", "3h", 1, 0), ("D", "3", 1, 4), ("S", "3", 0, 5), ("W", "3h", 3, 0), ("W", "3h", 5, 0),
    ("C", "mm", 2, 0, "far"), ("D", "3", 2, 5), ("S", "3h", 2, 1), ("D", "3h", 0, 0), ("D", "3h", 1, 0),
    ("S", "3", 1, 5), ("D", "3h", 5, 0), ("S", "3h", 5, 1), ("S", "3h", 4, 1), ("W", "3h", 0, 0), ("W", "3h", 1, 0),
    ("C", "mm", 0, 0, "all"), ("W", "3", 2, 5), ("W", "3", 4, 5), ("C", "mm", 1, 2, "near"), ("D", "3", 0, 5),
    ("W", "3", 0, 4), ("S", "3h", 0, 1), ("D", "3", 5, 5), ("W", "2h", 3, 0), ("W", "2h", 3, 1), ("W", "2h", 3, 2),
    ("W", "2h", 3, 3), ("S", "3", 3, 6), ("D", "3", 4, 5), ("D", "3h", 2, 1), ("W", "2h", 2, 0), ("W", "2h", 2, 1),
    ("W", "2h", 2, 2), ("W", "2h", 2, 3), ("S", "3", 2, 6), ("W", "3", 1, 4), ("S", "3h", 1, 1), ("W", "3", 3, 5),
    ("W", "3", 5, 5), ("C", "mm", 2, 2, "near"), ("D", "3", 1, 5), ("W", "2h", 0, 0), ("W", "2h", 0, 1),
    ("W", "2h", 0, 2), ("W", "2h", 0, 3), ("S", "3", 0, 6), ("D", "3h", 5, 1), ("W", "2h", 5, 3), ("S", "3", 5, 6),
    ("D", "3h", 4, 1), ("W", "2h", 4, 3), ("S", "3", 4, 6), ("W", "3h", 2, 1), ("W", "3h", 4, 1),
    ("C", "mm", 1, 1, "far"), ("W", "3h", 3, 1), ("W", "3h", 5, 1), ("C", "mm", 2, 1, "far"), ("W", "3h", 0, 1),
    ("W", "3h", 1, 1), ("C", "mm", 0, 1, "all"), ("D", "3h", 0, 1), ("D", "3h", 1, 1), ("W", "2h", 1, 0),
    ("W", "2h", 1, 1), ("W", "2h", 1, 2), ("W", "2h", 1, 3), ("S", "3", 1, 6), ("D", "3", 0, 6), ("W", "3", 0, 5),
    ("S", "3h", 0, 2), ("D", "3", 3, 6), ("S", "3h", 3, 2), ("D", "3", 2, 6), ("S", "3h", 2, 2), ("W", "3", 1, 5),
    ("S", "3h", 1, 2), ("S", "3h", 5, 2), ("S", "3h", 4, 2), ("D", "3", 1, 6), ("W", "3", 0, 6), ("S", "3h", 0, 3),
    ("W", "3", 2, 6), ("W", "3", 4, 6), ("C", "mm", 1, 3, "near"), ("D", "3h", 0, 2), ("W", "3", 1, 6),
    ("S", "3h", 1, 3), ("D", "3", 5, 6), ("D", "3h", 3, 2), ("W", "3", 3, 6), ("S", "3h", 3, 3), ("D", "3", 4, 6),
    ("D", "3h", 2, 2), ("S", "3h", 2, 3), ("W", "3", 5, 6), ("C", "mm", 2, 3, "near"), ("D", "3h", 5, 2),
    ("S", "3h", 5, 3), ("D", "3h", 4, 2), ("S", "3h", 4, 3), ("W", "3h", 0, 2), ("W", "3h", 1, 2),
    ("C", "mm", 0, 2, "all"), ("W", "3h", 0, 3), ("W", "3h", 1, 3), ("C", "mm", 0, 3, "all"), ("W", "3h", 2, 2),
    ("W", "3h", 4, 2), ("C", "mm", 1, 2, "far"), ("W", "3h", 2, 3), ("W", "3h", 4, 3), ("C", "mm", 1, 3, "far"),
    ("W", "3h", 3, 2), ("W", "3h", 5, 2), ("C", "mm", 2, 2, "far"), ("W", "3h", 3, 3), ("W", "3h", 5, 3),
    ("C", "mm", 2, 3, "far"), ("C", "fin", 1), ("C", "fin", 2), ("C", "fin", 0),
)

THRESH = ((0.25, 0.5), (0.75, 1.0), (1.25, 1.5), (1.75, 2.0), (2.5, 3.0), (3.5, 4.0), (5.0, 6.0))


def mod4(v):
    return lax.rem(v + 8, 4)


def kernel(
    tokens, gain, frag, exps, base, mom,
    grad_out, kv_out,
    w0, w1, w2, tok, acc, kv, fv, fb, rl, bs, ms, gr, gb, gf, gn, ex, eb, er, erl, sc, iv, ss,
    loc, a_snd, a_rcv, e_snd, e_rcv, t_snd, t_rcv, g_snd, g_rcv, o_sem,
):
    W = (w0, w1, w2)
    rep = lax.axis_index("replica")
    fs = lax.axis_index("fsdp")
    core = lax.axis_index("tensor")
    pos = {"x": lax.rem(fs, 4), "y": lax.div(fs, 4), "z": rep}

    def nbr(axis, step):
        c = dict(pos)
        c[axis] = mod4(pos[axis] + step)
        return (c["z"], c["y"] * 4 + c["x"], core)

    other = (rep, fs, 1 - core)

    def remote(src, dst, ss_, rs_, dev):
        return pltpu.make_async_remote_copy(
            src_ref=src, dst_ref=dst, send_sem=ss_, recv_sem=rs_, device_id=dev, device_id_type=MESH
        )

    pending = []

    def go(copy):
        copy.start()
        pending.append(copy)

    barrier = pltpu.get_barrier_semaphore()
    peers = [nbr(a, s) for a in "xyz" for s in (1, -1)] + [other]
    for p in peers:
        pl.semaphore_signal(barrier, inc=1, device_id=p, device_id_type=MESH)

    l_ex = pltpu.make_async_copy(exps, ex, loc.at[0])
    l_ex.start()
    l_fr = pltpu.make_async_copy(frag, fv, loc.at[1])
    l_fr.start()
    l_bs = pltpu.make_async_copy(base, bs, loc.at[2])
    l_bs.start()
    l_ms = pltpu.make_async_copy(mom, ms, loc.at[3])
    l_ms.start()
    l_gn = pltpu.make_async_copy(gain, gb, loc.at[4])
    l_gn.start()

    pl.semaphore_wait(barrier, len(peers))
    l_fr.wait()

    up, down = nbr("z", 1), nbr("z", -1)
    zu, zd, zo = mod4(rep + 1), mod4(rep - 1), mod4(rep + 2)

    def window(d):
        return eb.at[:, pl.ds(pl.multiple_of(128 * lax.div(3 * d, 2), 128), 256)]

    off = 64 * lax.rem(rep, 2)

    def expand(p):
        c, sub, width, _ = PARTS[p]
        lo = CLS[c][0] + sub
        j = lax.broadcasted_iota(jnp.int32, (BLOCK, width), 0)
        n = lax.broadcasted_iota(jnp.int32, (BLOCK, width), 1)
        pick = jnp.where(j == lax.div(n + lo, BLOCK), 1.0, 0.0).astype(BF16)
        for slot in range(4):
            e = (window(rep)[...] if slot == 0 else er[slot]).astype(F32)
            for ref, sign in ((sc, 1.0), (iv, -1.0)):
                small = jnp.exp2(sign * e).astype(BF16)
                full = lax.dot_general(small, pick, (((0,), (0,)), ((), ())), preferred_element_type=F32)
                ref[slot, :, pl.ds(lo, width)] = full.astype(BF16)

    e_cp = [
        remote(window(zo), erl, e_snd.at[0], e_rcv.at[0], up),
        remote(window(zu), er.at[1], e_snd.at[1], e_rcv.at[1], up),
        remote(window(zd), er.at[2], e_snd.at[2], e_rcv.at[2], down),
        remote(erl, er.at[3], e_snd.at[3], e_rcv.at[3], up),
    ]

    def cols(p):
        c, lo, width, _ = PARTS[p]
        return pl.ds(CLS[c][0] + lo, width)

    H = ROWS // 2

    def a2a(p):
        k = 6 * p
        cc = cols(p)
        return [
            remote(fv.at[zo, pl.ds(0, H), cc], rl.at[0, :, cc], a_snd.at[k], a_rcv.at[k], up),
            remote(fv.at[zo, pl.ds(H, H), cc], rl.at[1, :, cc], a_snd.at[k + 1], a_rcv.at[k + 1], down),
            remote(fv.at[zu, :, cc], fb.at[1, :, cc], a_snd.at[k + 2], a_rcv.at[k + 2], up),
            remote(fv.at[zd, :, cc], fb.at[2, :, cc], a_snd.at[k + 3], a_rcv.at[k + 3], down),
            remote(rl.at[0, :, cc], fb.at[3, pl.ds(0, H), cc], a_snd.at[k + 4], a_rcv.at[k + 4], up),
            remote(rl.at[1, :, cc], fb.at[3, pl.ds(H, H), cc], a_snd.at[k + 5], a_rcv.at[k + 5], down),
        ]

    mine = pl.ds(pl.multiple_of(core * TOK, TOK), TOK)
    t_cp, l_tk = [], []
    for i in range(8):
        src = tokens.at[pl.ds(i * SLAB, SLAB), :]
        dst = tok.at[pl.ds(pl.multiple_of(core * TOK + i * SLAB, SLAB), SLAB), :]
        t_cp.append(remote(src, dst, t_snd.at[i], t_rcv.at[i], other))
        l_tk.append(pltpu.make_async_copy(src, dst, loc.at[5 + i]))

    def early():
        l_ex.wait()
        eb[...] = ex[...].astype(F32).astype(BF16)
        for m in e_cp[:3]:
            go(m)
        l_gn.wait()
        gf[...] = gb[...].astype(F32)
        first = 6 * fs + lax.div(3 * rep, 2)
        i = lax.broadcasted_iota(jnp.int32, (128, 128), 0)
        l = lax.broadcasted_iota(jnp.int32, (128, 128), 1)
        for h in range(2):
            row = jnp.broadcast_to(gf[pl.ds(first + h, 1), :], (128, 128))
            column = jnp.sum(jnp.where(i == l, row, 0.0), axis=1, keepdims=True)
            gn[pl.ds(128 * h, 128), :] = jnp.broadcast_to(column, (128, 128))
        e_cp[0].wait_recv()
        go(e_cp[3])

    def prepare():
        for s in (1, 2, 3):
            e_cp[s].wait_recv()
        l_bs.wait()
        l_ms.wait()

    def encode(p):
        c, sub, width, _ = PARTS[p]
        lo = CLS[c][0] + sub
        row0 = pl.multiple_of(rep * ROWS, ROWS)

        def step(t, carry):
            rr = pl.ds(pl.multiple_of(t * SLAB, SLAB), SLAB)
            wr = pl.ds(pl.multiple_of(row0 + t * SLAB, SLAB), SLAB)
            fr = pl.ds(pl.multiple_of(off + t * SLAB, 16), SLAB)
            g = gn[fr, :]
            for k in range(width // 128):
                cc = pl.ds(lo + 128 * k, 128)
                b = bs[rr, cc]
                total = jnp.zeros((SLAB, 128), F32)
                for s in range(4):
                    v = (b - (fv[rep, rr, cc] if s == 0 else fb[s, rr, cc]).astype(F32)) * iv[s, fr, cc].astype(F32)
                    m = jnp.abs(v)
                    level = jnp.zeros_like(m)
                    for mid, val in THRESH:
                        level = jnp.where(m >= mid, val, level)
                    total = total + jnp.where(v < 0.0, -level, level) * sc[s, fr, cc].astype(F32)
                grad = total * 0.25
                nm = MOMENTUM_COEF * ms[rr, cc] + grad
                nb = b - OUTER_RATE * (grad + MOMENTUM_COEF * nm)
                gr[rr, cc] = grad
                W[c][pos["y"], pos["x"], wr, pl.ds(sub + 128 * k, 128)] = (nb * g).astype(BF16)
            return carry

        lax.fori_loop(0, ROWS // SLAB, step, 0)

    def place(p, **at):
        half = at.pop("half", None)
        xs, ys = at.get("x", slice(None)), at.get("y", slice(None))
        if "z" in at:
            r0, n = at["z"] * ROWS, ROWS
        else:
            r0, n = 0, FROWS
        if half is not None:
            n = n // 2
            r0 = r0 + half * n
        if not isinstance(r0, int):
            r0 = pl.multiple_of(r0, 96)
        c, lo, width, _ = PARTS[p]
        return W[c].at[ys, xs, pl.ds(r0, n), pl.ds(lo, width)]

    M = {}
    OFF = (0, 1, -1, 2)
    used = [0]

    def both(*pair):
        out = []
        for j, s in enumerate((1, -1)):
            axis, ref = pair[j]
            out.append(remote(ref, ref, g_snd.at[used[0]], g_rcv.at[used[0]], nbr(axis, s)))
            used[0] += 1
        return out

    def full(p, axis, **fixed):
        here = place(p, **fixed, **{axis: pos[axis]})
        return both((axis, here), (axis, here))

    def half(p, axis, **fixed):
        return both(
            *[(axis, place(p, **fixed, **{axis: mod4(pos[axis] - s), "half": j})) for j, s in enumerate((1, -1))]
        )

    for p in range(len(PARTS)):
        m = a2a(p)
        M["r", p], M["d", p], M["f", p] = m[:2], m[2:4], m[4:]
        a, b, l = PARTS[p][3]
        R, S = (a, b) if b == "z" else (b, a)
        at = {b: pos[b], l: pos[l]}
        M["1", p], M["1h", p] = full(p, a, **at), half(p, a, **at)
        for i in range(4):
            at = {a: mod4(pos[a] + OFF[i]), l: pos[l]}
            M["2", p, i], M["2h", p, i] = full(p, b, **at), half(p, b, **at)
            M["3", p, i] = full(p, l, **{R: pos[R], S: mod4(pos[S] + OFF[i])})
            M["3h", p, i] = half(p, l, **{R: mod4(pos[R] + OFF[i])})
            if i:
                M["3", p, 3 + i] = full(p, l, **{R: mod4(pos[R] + OFF[i])})

    def mm(c, count, coords):
        lo, width = CLS[c]
        cc = pl.ds(lo, width)

        def chunk(t, carry):
            yy, xx = coords(t)
            kk = pl.ds(pl.multiple_of((yy * 4 + xx) * FROWS, FROWS), FROWS)

            def block(m, carry):
                mr = pl.ds(pl.multiple_of(m * 256, 256), 256)
                acc[mr, cc] += jnp.dot(tok[mr, kk], W[c][yy, xx], preferred_element_type=F32)
                return carry

            return lax.fori_loop(0, 3, block, carry)

        lax.fori_loop(0, count, chunk, 0)

    def offset(i):
        return i + lax.div(i, 2) - 2 * lax.div(i, 3)

    def mm_near(c, i):
        if c == 1:
            yy = mod4(pos["y"] + OFF[i])
            mm(c, 3, lambda t: (yy, mod4(pos["x"] + offset(t))))
        else:
            xx = mod4(pos["x"] + OFF[i])
            mm(c, 3, lambda t: (mod4(pos["y"] + offset(t)), xx))

    def mm_far(c, i):
        if c == 1:
            mm(c, 1, lambda t: (mod4(pos["y"] + OFF[i]), mod4(pos["x"] + 2)))
        else:
            mm(c, 1, lambda t: (mod4(pos["y"] + 2), mod4(pos["x"] + OFF[i])))

    same = len({p[3] for p in PARTS if p[0] == 0}) == 1

    def mm_row(c, i):
        by_y = PARTS[[p[0] for p in PARTS].index(0)][3][1] == "y"
        at = mod4(pos["y" if by_y else "x"] + OFF[i])
        mm(c, 4, (lambda t: (at, t)) if by_y else (lambda t: (t, at)))

    def mm_level(c, i):
        def coords(t):
            turn = lax.div(t, i + 1)
            iy = i * (1 - turn) + (t - i - 1) * turn
            ix = t * (1 - turn) + i * turn
            return mod4(pos["y"] + offset(iy)), mod4(pos["x"] + offset(ix))

        mm(c, 2 * i + 1, coords)

    def squares(i):
        rr = pl.ds(pl.multiple_of(core * TOK + i * 128, 128), 128)

        def step(t, s):
            for k in range(4):
                v = tok[rr, pl.ds(pl.multiple_of(t * 512 + k * 128, 128), 128)].astype(F32)
                s = s + v * v
            return s

        s = lax.fori_loop(0, D // 512, step, jnp.zeros((128, 128), F32))
        mean = jnp.sum(s, axis=1, keepdims=True) * (1.0 / D)
        ss[rr, :] = jnp.broadcast_to(lax.rsqrt(mean + 1e-05) * (D ** -0.5), (128, 128))

    def finish(c):
        lo, width = CLS[c]
        cc = pl.ds(lo, width)

        def scale(m, carry):
            mr = pl.ds(pl.multiple_of(m * 64, 64), 64)
            for k in range(width // 128):
                at = pl.ds(lo + 128 * k, 128)
                kv[mr, at] = (acc[mr, at] * ss[mr, :]).astype(BF16)
            return carry

        lax.fori_loop(0, 2 * TOK // 64, scale, 0)
        outs.append(pltpu.make_async_copy(kv.at[:, cc], kv_out.at[:, cc], o_sem.at[1 + c]))
        outs[-1].start()

    s_cp = remote(ss.at[mine, :], ss.at[mine, :], t_snd.at[8], t_rcv.at[8], other)
    outs = []
    left = []
    late = []
    seen = set()

    def once(name):
        new = name not in seen
        seen.add(name)
        return new

    for kind, *key in SCHEDULE:
        key = tuple(key)
        if kind == "S":
            for m in M[key]:
                m.start()
            left.append(key)
        elif kind == "W":
            if once("wait"):
                early()
            if key[0] == "d":
                if once("prepare"):
                    prepare()
                expand(key[1])
            for m in M[key]:
                m.wait_recv()
        elif kind == "D":

            @pl.when(core == 1)
            def _():
                for m in M[key]:
                    m.wait_send()

            left.remove(key)
            late.append(key)
        elif kind == "E":
            encode(*key)
            left_to_encode = len(PARTS) - 1 - key[0]
            if left_to_encode == 0:
                outs.append(pltpu.make_async_copy(gr, grad_out, o_sem.at[0]))
                outs[0].start()
        elif key[0] == "tk":
            l_tk[key[1]].start()
            go(t_cp[key[1]])
            if once("total"):
                acc[...] = jnp.zeros_like(acc)
        elif key[0] == "sq":
            if once("own tokens"):
                for t in l_tk:
                    t.wait()
            squares(key[1])
            if key[1] == 2:
                go(s_cp)
        elif key[0] == "fin":
            if once("factors"):
                s_cp.wait_recv()
            finish(key[1])
        else:
            if once("all tokens"):
                for t in t_cp:
                    t.wait_recv()
            {"near": mm_near, "far": mm_far, "all": mm_row if same else mm_level}[key[3]](key[1], key[2])
    for key in left:
        for m in M[key]:
            m.wait_send()

    @pl.when(core == 0)
    def _():
        for key in late:
            for m in M[key]:
                m.wait_send()

    for p in pending:
        p.wait_send()
    for o in outs:
        o.wait()


def write_kernel(grad, base, mom, kv, nb_out, nm_out, kv_out, gr, bs, ms, ks, in_sem, out_sem, kv_in, kv_sem):
    loads, stores, moves = [], [], []
    for q in range(4):
        rr = pl.ds(q * SLAB, SLAB)
        for i, (src, dst) in enumerate(((grad, gr), (base, bs), (mom, ms))):
            loads.append(pltpu.make_async_copy(src.at[rr, :], dst.at[rr, :], in_sem.at[3 * q + i]))
            loads[-1].start()
    for q in range(4):
        rr = pl.ds(q * 192, 192)
        moves.append(pltpu.make_async_copy(kv.at[rr, :], ks.at[rr, :], kv_in.at[q]))
        moves[-1].start()
    for q in range(4):
        rr = pl.ds(q * SLAB, SLAB)
        for i in range(3):
            loads[3 * q + i].wait()
        g = gr[rr, :]
        nm = MOMENTUM_COEF * ms[rr, :] + g
        ms[rr, :] = nm
        bs[rr, :] = bs[rr, :] - OUTER_RATE * (g + MOMENTUM_COEF * nm)
        stores.append(pltpu.make_async_copy(bs.at[rr, :], nb_out.at[rr, :], out_sem.at[2 * q]))
        stores.append(pltpu.make_async_copy(ms.at[rr, :], nm_out.at[rr, :], out_sem.at[2 * q + 1]))
        stores[-2].start()
        stores[-1].start()
    for q in range(4):
        rr = pl.ds(q * 192, 192)
        moves[q].wait()
        stores.append(pltpu.make_async_copy(ks.at[rr, :], kv_out.at[rr, :], kv_sem.at[q]))
        stores[-1].start()
    for copy in stores:
        copy.wait()


def body(tokens, norm_gain, fragment, exponents, base_weight, momentum):
    any_ = pl.BlockSpec(memory_space=pl.ANY)
    dma = pltpu.SemaphoreType.DMA
    vm = pltpu.VMEM
    grad, keys_values = pl.pallas_call(
        kernel,
        out_shape=(
            jax.ShapeDtypeStruct((ROWS, KVW), F32),
            jax.ShapeDtypeStruct((2 * TOK, KVW), BF16),
        ),
        in_specs=[any_] * 6,
        out_specs=[any_] * 2,
        scratch_shapes=[
            *[vm((4, 4, FROWS, width), BF16) for _, width in CLS],
            vm((2 * TOK, D), BF16),
            vm((2 * TOK, KVW), F32),
            vm((2 * TOK, KVW), BF16),
            vm((4, ROWS, KVW), BF16),
            vm((4, ROWS, KVW), BF16),
            vm((2, ROWS // 2, KVW), BF16),
            vm((ROWS, KVW), F32),
            vm((ROWS, KVW), F32),
            vm((ROWS, KVW), F32),
            vm((D // 128, 128), BF16),
            vm((D // 128, 128), F32),
            vm((256, 128), F32),
            vm((BLOCK, 4 * ROWS), jnp.int32),
            vm((BLOCK, 4 * ROWS), BF16),
            vm((4, BLOCK, 256), BF16),
            vm((BLOCK, 256), BF16),
            vm((4, 256, KVW), BF16),
            vm((4, 256, KVW), BF16),
            vm((2 * TOK, 128), F32),
            dma((13,)),
            dma((6 * len(PARTS),)),
            dma((6 * len(PARTS),)),
            dma((4,)),
            dma((4,)),
            dma((9,)),
            dma((9,)),
            dma((42 * len(PARTS),)),
            dma((42 * len(PARTS),)),
            dma((4,)),
        ],
        compiler_params=pltpu.CompilerParams(
            collective_id=0, has_side_effects=True, vmem_limit_bytes=62 * 1024 * 1024
        ),
        cost_estimate=pl.CostEstimate(flops=2 * 768 * 12288 * 1024, bytes_accessed=30_000_000, transcendentals=0),
    )(
        tokens,
        norm_gain.reshape(D // 128, 128),
        fragment.reshape(4, ROWS, KVW),
        exponents[0].T,
        base_weight,
        momentum,
    )
    return pl.pallas_call(
        write_kernel,
        out_shape=(
            jax.ShapeDtypeStruct((ROWS, KVW), F32),
            jax.ShapeDtypeStruct((ROWS, KVW), F32),
            jax.ShapeDtypeStruct((2 * TOK, KVW), BF16),
        ),
        in_specs=[any_] * 4,
        out_specs=[any_] * 3,
        scratch_shapes=[vm((ROWS, KVW), F32)] * 3
        + [vm((2 * TOK, KVW), BF16), dma((12,)), dma((8,)), dma((4,)), dma((4,))],
        compiler_params=pltpu.CompilerParams(vmem_limit_bytes=62 * 1024 * 1024),
        cost_estimate=pl.CostEstimate(flops=6 * ROWS * KVW, bytes_accessed=7_000_000, transcendentals=0),
    )(grad, base_weight, momentum, keys_values)


def solution(mesh):
    in_specs = (
        P(("replica", "fsdp", "tensor"), None),
        P(),
        P("replica", "fsdp", "tensor"),
        P("replica", "fsdp", "tensor"),
        P(("fsdp", "replica"), "tensor"),
        P(("fsdp", "replica"), "tensor"),
    )
    out_specs = (
        P(("fsdp", "replica"), "tensor"),
        P(("fsdp", "replica"), "tensor"),
        P(("replica", "fsdp"), "tensor"),
    )
    return jax.shard_map(body, mesh=mesh, in_specs=in_specs, out_specs=out_specs, check_vma=False)
```

```python
import jax
import jax.numpy as jnp
from jax import lax
from jax.experimental import pallas as pl
from jax.experimental.pallas import tpu as pltpu
from jax.sharding import PartitionSpec as P

MESH = pl.DeviceIdType.MESH
F32, BF16 = jnp.float32, jnp.bfloat16
D, KVW, BLOCK, TOK = 12288, 1024, 32, 384
ROWS = 192
FROWS = 768
SLAB = 48
OUTER_RATE = 0.7
MOMENTUM_COEF = 0.9
CLS = ((0, 256), (256, 384), (640, 384))
PARTS = (
    (0, 0, 128, ("x", "y", "z")),
    (0, 128, 128, ("y", "x", "z")),
    (1, 0, 128, ("z", "y", "x")),
    (2, 0, 128, ("z", "x", "y")),
    (1, 128, 256, ("y", "z", "x")),
    (2, 128, 256, ("x", "z", "y")),
)

SCHEDULE = (
    ("S", "r", 0), ("S", "d", 0), ("S", "r", 1), ("S", "d", 1), ("W", "r", 0), ("S", "f", 0), ("S", "r", 2),
    ("W", "r", 1), ("S", "f", 1), ("S", "d", 2), ("S", "r", 3), ("W", "d", 0), ("W", "f", 0), ("E", 0), ("S", "1", 0),
    ("S", "2", 0, 0), ("D", "r", 0), ("W", "r", 2), ("S", "f", 2), ("S", "d", 3), ("W", "d", 1), ("W", "f", 1),
    ("E", 1), ("S", "2", 1, 0), ("S", "1", 1), ("D", "d", 0), ("D", "r", 1), ("W", "r", 3), ("S", "f", 3),
    ("S", "r", 4), ("W", "1", 0), ("S", "1h", 0), ("W", "2", 0, 0), ("S", "2h", 0, 0), ("S", "2", 0, 1),
    ("S", "2", 0, 2), ("D", "d", 1), ("D", "f", 0), ("S", "d", 4), ("W", "d", 2), ("W", "f", 2), ("E", 2),
    ("W", "2", 1, 0), ("S", "2h", 1, 0), ("W", "1", 1), ("S", "2", 1, 1), ("S", "1h", 1), ("S", "2", 1, 2),
    ("W", "1h", 0), ("S", "2", 0, 3), ("S", "2", 2, 0), ("D", "r", 2), ("D", "f", 1), ("D", "d", 2), ("D", "r", 3),
    ("W", "r", 4), ("S", "f", 4), ("S", "3", 2, 0), ("W", "d", 3), ("W", "f", 3), ("E", 3), ("S", "r", 5),
    ("D", "1", 0), ("S", "2", 3, 0), ("D", "2", 0, 0), ("S", "3", 3, 0), ("D", "f", 2), ("S", "d", 5), ("D", "d", 3),
    ("S", "1", 2), ("W", "2", 0, 1), ("S", "2h", 0, 1), ("W", "2", 0, 2), ("S", "2h", 0, 2), ("W", "1h", 1),
    ("S", "2", 1, 3), ("D", "f", 3), ("S", "1", 3), ("D", "2", 1, 0), ("W", "2", 1, 1), ("S", "2h", 1, 1),
    ("W", "d", 4), ("W", "f", 4), ("E", 4), ("D", "1", 1), ("D", "2h", 0, 0), ("S", "1", 4), ("D", "1h", 0),
    ("W", "2", 1, 2), ("S", "2h", 1, 2), ("W", "2", 0, 3), ("S", "2h", 0, 3), ("W", "2", 2, 0), ("S", "2h", 2, 0),
    ("D", "2h", 1, 0), ("S", "3", 4, 0), ("C", "tk", 0), ("W", "2", 3, 0), ("S", "2h", 3, 0), ("D", "r", 4),
    ("D", "d", 4), ("W", "r", 5), ("S", "f", 5), ("S", "2", 4, 0), ("W", "2", 1, 3), ("S", "2h", 1, 3),
    ("D", "2", 0, 1), ("D", "2", 0, 2), ("D", "1h", 1), ("W", "1", 2), ("S", "2", 2, 1), ("S", "2", 2, 2),
    ("D", "2", 1, 1), ("W", "1", 3), ("S", "2", 3, 1), ("D", "f", 4), ("S", "1h", 2), ("S", "2", 3, 2),
    ("S", "1h", 3), ("C", "tk", 1), ("C", "tk", 2), ("S", "3", 3, 1), ("D", "r", 5), ("S", "3", 0, 0),
    ("D", "2", 1, 2), ("D", "3", 2, 0), ("S", "3", 2, 1), ("D", "2", 0, 3), ("D", "2", 2, 0), ("S", "3", 3, 2),
    ("S", "3", 1, 0), ("D", "2", 3, 0), ("D", "2h", 1, 1), ("S", "3", 2, 2), ("C", "tk", 3), ("D", "2h", 0, 1),
    ("D", "2h", 0, 2), ("D", "3", 3, 0), ("W", "1h", 2), ("S", "2", 2, 3), ("W", "d", 5), ("W", "f", 5), ("E", 5),
    ("D", "1", 2), ("D", "1", 3), ("W", "1", 4), ("S", "2", 4, 1), ("D", "2", 1, 3), ("D", "2h", 1, 2),
    ("D", "2h", 3, 0), ("S", "1", 5), ("D", "2h", 0, 3), ("D", "2h", 2, 0), ("S", "1h", 4), ("W", "2", 2, 1),
    ("S", "2h", 2, 1), ("W", "2", 2, 2), ("S", "2h", 2, 2), ("D", "d", 5), ("S", "2", 4, 2), ("D", "2h", 1, 3),
    ("W", "2", 3, 1), ("S", "2h", 3, 1), ("W", "2", 3, 2), ("S", "2h", 3, 2), ("W", "1h", 3), ("S", "2", 3, 3),
    ("W", "2", 4, 0), ("S", "2h", 4, 0), ("S", "3", 5, 0), ("S", "2", 5, 0), ("W", "2", 2, 3), ("S", "2h", 2, 3),
    ("C", "tk", 4), ("C", "tk", 5), ("S", "3", 4, 1), ("D", "2", 2, 1), ("D", "1", 4), ("S", "3", 3, 3),
    ("C", "tk", 6), ("D", "1h", 2), ("D", "f", 5), ("D", "1h", 3), ("W", "1h", 4), ("S", "2", 4, 3), ("D", "2", 3, 1),
    ("D", "2", 3, 2), ("D", "3", 4, 0), ("S", "3", 4, 2), ("C", "tk", 7), ("D", "3", 2, 1), ("D", "3", 2, 2),
    ("W", "2", 3, 3), ("S", "2h", 3, 3), ("W", "1", 5), ("S", "1h", 5), ("D", "3", 0, 0), ("D", "2", 4, 0),
    ("D", "3", 1, 0), ("S", "2", 5, 1), ("D", "2", 2, 2), ("D", "3", 3, 1), ("D", "3", 3, 2), ("D", "2", 2, 3),
    ("S", "3", 3, 4), ("W", "2", 4, 1), ("S", "2h", 4, 1), ("D", "2h", 3, 1), ("S", "3", 2, 3), ("S", "2", 5, 2),
    ("D", "2h", 3, 2), ("W", "2h", 4, 0), ("S", "3", 4, 3), ("D", "2h", 2, 1), ("D", "2h", 2, 2), ("D", "1h", 4),
    ("D", "2h", 2, 3), ("W", "3", 3, 0), ("W", "3", 3, 1), ("W", "3", 3, 2), ("W", "3", 3, 3), ("S", "3h", 3, 0),
    ("D", "2", 4, 1), ("D", "2h", 4, 0), ("W", "2", 4, 2), ("S", "2h", 4, 2), ("D", "2", 3, 3), ("D", "1", 5),
    ("S", "3", 2, 4), ("D", "3", 3, 3), ("D", "3", 5, 0), ("W", "2", 5, 0), ("S", "3", 5, 1), ("S", "2h", 5, 0),
    ("D", "2", 4, 2), ("W", "1h", 5), ("S", "2", 5, 3), ("S", "3", 5, 2), ("C", "sq", 0), ("D", "2", 5, 0),
    ("W", "2", 4, 3), ("S", "2h", 4, 3), ("D", "2h", 3, 3), ("D", "3", 4, 1), ("D", "1h", 5), ("W", "2h", 4, 1),
    ("S", "3", 4, 4), ("S", "3", 3, 5), ("W", "3", 2, 0), ("W", "3", 2, 1), ("W", "3", 2, 2), ("W", "3", 2, 3),
    ("W", "3", 4, 0), ("W", "3", 4, 1), ("W", "3", 4, 2), ("W", "3", 4, 3), ("C", "mm", 1, 0, "near"),
    ("D", "2h", 4, 1), ("D", "2", 4, 3), ("W", "2", 5, 1), ("S", "2h", 5, 1), ("S", "3", 0, 1), ("C", "sq", 1),
    ("W", "2", 5, 2), ("S", "2h", 5, 2), ("D", "3", 3, 4), ("D", "3h", 3, 0), ("W", "2h", 5, 0), ("S", "3", 5, 3),
    ("C", "sq", 2), ("S", "3", 1, 1), ("W", "3", 3, 4), ("S", "3h", 3, 1), ("D", "2", 5, 1), ("D", "2h", 4, 2),
    ("S", "3", 0, 2), ("W", "2", 5, 3), ("S", "2h", 5, 3), ("D", "3", 4, 2), ("D", "3", 2, 3), ("D", "3", 4, 3),
    ("D", "3", 2, 4), ("S", "3h", 2, 0), ("D", "3", 5, 1), ("D", "3", 5, 2), ("W", "2h", 5, 1), ("S", "3", 5, 4),
    ("D", "2h", 5, 0), ("D", "2", 5, 2), ("S", "3", 1, 2), ("D", "2h", 4, 3), ("S", "3", 0, 3), ("S", "3h", 4, 0),
    ("S", "3", 1, 3), ("D", "2", 5, 3), ("S", "3", 0, 4), ("W", "3", 5, 0), ("W", "3", 5, 1), ("W", "3", 5, 2),
    ("W", "3", 5, 3), ("C", "mm", 2, 0, "near"), ("W", "3", 2, 4), ("W", "3", 4, 4), ("C", "mm", 1, 1, "near"),
    ("S", "3", 2, 5), ("D", "2h", 5, 1), ("D", "3", 0, 1), ("D", "2h", 5, 2), ("S", "3", 1, 4), ("D", "3", 3, 5),
    ("D", "3", 5, 3), ("D", "3h", 3, 1), ("S", "3h", 5, 0), ("W", "3h", 2, 0), ("W", "3h", 4, 0),
    ("C", "mm", 1, 0, "far"), ("D", "3", 4, 4), ("D", "3h", 2, 0), ("W", "2h", 4, 2), ("S", "3", 4, 5),
    ("D", "3", 1, 1), ("D", "3", 0, 2), ("D", "2h", 5, 3), ("D", "3", 1, 2), ("D", "3", 0, 3), ("D", "3", 1, 3),
    ("W", "3", 0, 0), ("W", "3", 0, 1), ("W", "3", 0, 2), ("W", "3", 0, 3), ("S", "3h", 0, 0), ("W", "2h", 5, 2),
    ("S", "3", 5, 5), ("W", "3", 5, 4), ("C", "mm", 2, 1, "near"), ("W", "3", 1, 0), ("W", "3", 1, 1),
    ("W", "3", 1, 2), ("W", "3", 1, 3), ("S", "3h", 1, 0), ("S", "3", 0, 5), ("W", "3h", 3, 0), ("W", "3h", 5, 0),
    ("C", "mm", 2, 0, "far"), ("D", "3h", 4, 0), ("S", "3h", 2, 1), ("D", "3", 0, 4), ("S", "3", 1, 5),
    ("W", "3h", 0, 0), ("W", "3h", 1, 0), ("C", "mm", 0, 0, "all"), ("D", "3", 2, 5), ("S", "3h", 4, 1),
    ("D", "3", 5, 4), ("D", "3h", 5, 0), ("S", "3h", 5, 1), ("D", "3", 1, 4), ("D", "3h", 0, 0), ("W", "3", 0, 4),
    ("S", "3h", 0, 1), ("W", "3", 2, 5), ("W", "3", 4, 5), ("C", "mm", 1, 2, "near"), ("W", "2h", 2, 0),
    ("W", "2h", 2, 1), ("W", "2h", 2, 2), ("W", "2h", 2, 3), ("S", "3", 2, 6), ("W", "2h", 3, 0), ("W", "2h", 3, 1),
    ("W", "2h", 3, 2), ("W", "2h", 3, 3), ("S", "3", 3, 6), ("D", "3h", 1, 0), ("W", "3", 1, 4), ("S", "3h", 1, 1),
    ("W", "3", 3, 5), ("W", "3", 5, 5), ("C", "mm", 2, 2, "near"), ("D", "3", 0, 5), ("W", "2h", 0, 0),
    ("W", "2h", 0, 1), ("W", "2h", 0, 2), ("W", "2h", 0, 3), ("S", "3", 0, 6), ("D", "3", 4, 5), ("D", "3h", 2, 1),
    ("W", "2h", 4, 3), ("S", "3", 4, 6), ("D", "3", 5, 5), ("W", "2h", 5, 3), ("S", "3", 5, 6), ("W", "3h", 2, 1),
    ("W", "3h", 4, 1), ("C", "mm", 1, 1, "far"), ("W", "3h", 3, 1), ("W", "3h", 5, 1), ("C", "mm", 2, 1, "far"),
    ("W", "3h", 0, 1), ("W", "3h", 1, 1), ("C", "mm", 0, 1, "all"), ("D", "3h", 0, 1), ("W", "2h", 1, 0),
    ("W", "2h", 1, 1), ("W", "2h", 1, 2), ("W", "2h", 1, 3), ("S", "3", 1, 6), ("D", "3", 1, 5), ("D", "3h", 1, 1),
    ("W", "3", 0, 5), ("S", "3h", 0, 2), ("D", "3h", 4, 1), ("D", "3", 2, 6), ("S", "3h", 2, 2), ("D", "3h", 5, 1),
    ("D", "3", 3, 6), ("S", "3h", 3, 2), ("W", "3", 1, 5), ("S", "3h", 1, 2), ("S", "3h", 4, 2), ("S", "3h", 5, 2),
    ("D", "3", 0, 6), ("W", "3", 0, 6), ("S", "3h", 0, 3), ("W", "3", 1, 6), ("S", "3h", 1, 3), ("W", "3", 2, 6),
    ("S", "3h", 2, 3), ("W", "3", 3, 6), ("S", "3h", 3, 3), ("W", "3", 4, 6), ("C", "mm", 1, 3, "near"),
    ("S", "3h", 4, 3), ("W", "3", 5, 6), ("S", "3h", 5, 3), ("C", "mm", 2, 3, "near"), ("W", "3h", 0, 2),
    ("W", "3h", 1, 2), ("C", "mm", 0, 2, "all"), ("W", "3h", 0, 3), ("W", "3h", 1, 3), ("C", "mm", 0, 3, "all"),
    ("W", "3h", 2, 2), ("W", "3h", 4, 2), ("C", "mm", 1, 2, "far"), ("W", "3h", 2, 3), ("W", "3h", 4, 3),
    ("C", "mm", 1, 3, "far"), ("W", "3h", 3, 2), ("W", "3h", 5, 2), ("C", "mm", 2, 2, "far"), ("W", "3h", 3, 3),
    ("W", "3h", 5, 3), ("C", "mm", 2, 3, "far"), ("C", "fin", 1), ("C", "fin", 2), ("C", "fin", 0),
)

THRESH = ((0.25, 0.5), (0.75, 1.0), (1.25, 1.5), (1.75, 2.0), (2.5, 3.0), (3.5, 4.0), (5.0, 6.0))


class Message:
    def __init__(self, whole, copies):
        self.copies = copies
        self.wait_recv, self.wait_send = whole.wait_recv, whole.wait_send

    def start(self):
        for copy in self.copies:
            copy.start()


def mod4(v):
    return lax.rem(v + 8, 4)


def kernel(
    tokens, gain, frag, exps, base, mom,
    grad_out, kv_out,
    w0, w1, w2, tok, acc, kv, fv, fb, rl, bs, ms, gr, gb, gf, gn, ex, eb, er, erl, sc, iv, ss,
    loc, a_snd, a_rcv, e_snd, e_rcv, t_snd, t_rcv, g_snd, g_rcv, o_sem,
):
    W = (w0, w1, w2)
    rep = lax.axis_index("replica")
    fs = lax.axis_index("fsdp")
    core = lax.axis_index("tensor")
    pos = {"x": lax.rem(fs, 4), "y": lax.div(fs, 4), "z": rep}

    def nbr(axis, step):
        c = dict(pos)
        c[axis] = mod4(pos[axis] + step)
        return (c["z"], c["y"] * 4 + c["x"], core)

    other = (rep, fs, 1 - core)

    def remote(src, dst, ss_, rs_, dev):
        return pltpu.make_async_remote_copy(
            src_ref=src, dst_ref=dst, send_sem=ss_, recv_sem=rs_, device_id=dev, device_id_type=MESH
        )

    pending = []

    def go(copy):
        copy.start()
        pending.append(copy)

    barrier = pltpu.get_barrier_semaphore()
    peers = [nbr(a, s) for a in "xyz" for s in (1, -1)] + [other]
    for p in peers:
        pl.semaphore_signal(barrier, inc=1, device_id=p, device_id_type=MESH)

    l_ex = pltpu.make_async_copy(exps, ex, loc.at[0])
    l_ex.start()
    l_fr = pltpu.make_async_copy(frag, fv, loc.at[1])
    l_fr.start()
    l_bs = pltpu.make_async_copy(base, bs, loc.at[2])
    l_bs.start()
    l_ms = pltpu.make_async_copy(mom, ms, loc.at[3])
    l_ms.start()
    l_gn = pltpu.make_async_copy(gain, gb, loc.at[4])
    l_gn.start()

    pl.semaphore_wait(barrier, len(peers))
    l_fr.wait()

    up, down = nbr("z", 1), nbr("z", -1)
    zu, zd, zo = mod4(rep + 1), mod4(rep - 1), mod4(rep + 2)

    def window(d):
        return eb.at[:, pl.ds(pl.multiple_of(128 * lax.div(3 * d, 2), 128), 256)]

    off = 64 * lax.rem(rep, 2)

    def expand(p):
        c, sub, width, _ = PARTS[p]
        lo = CLS[c][0] + sub
        j = lax.broadcasted_iota(jnp.int32, (BLOCK, width), 0)
        n = lax.broadcasted_iota(jnp.int32, (BLOCK, width), 1)
        pick = jnp.where(j == lax.div(n + lo, BLOCK), 1.0, 0.0).astype(BF16)
        for slot in range(4):
            e = (window(rep)[...] if slot == 0 else er[slot]).astype(F32)
            for ref, sign in ((sc, 1.0), (iv, -1.0)):
                small = jnp.exp2(sign * e).astype(BF16)
                full = lax.dot_general(small, pick, (((0,), (0,)), ((), ())), preferred_element_type=F32)
                ref[slot, :, pl.ds(lo, width)] = full.astype(BF16)

    e_cp = [
        remote(window(zo), erl, e_snd.at[0], e_rcv.at[0], up),
        remote(window(zu), er.at[1], e_snd.at[1], e_rcv.at[1], up),
        remote(window(zd), er.at[2], e_snd.at[2], e_rcv.at[2], down),
        remote(erl, er.at[3], e_snd.at[3], e_rcv.at[3], up),
    ]

    def cols(p):
        c, lo, width, _ = PARTS[p]
        return pl.ds(CLS[c][0] + lo, width)

    H = ROWS // 2

    def a2a(p):
        k = 6 * p
        cc = cols(p)
        return [
            remote(fv.at[zo, pl.ds(0, H), cc], rl.at[0, :, cc], a_snd.at[k], a_rcv.at[k], up),
            remote(fv.at[zo, pl.ds(H, H), cc], rl.at[1, :, cc], a_snd.at[k + 1], a_rcv.at[k + 1], down),
            remote(fv.at[zu, :, cc], fb.at[1, :, cc], a_snd.at[k + 2], a_rcv.at[k + 2], up),
            remote(fv.at[zd, :, cc], fb.at[2, :, cc], a_snd.at[k + 3], a_rcv.at[k + 3], down),
            remote(rl.at[0, :, cc], fb.at[3, pl.ds(0, H), cc], a_snd.at[k + 4], a_rcv.at[k + 4], up),
            remote(rl.at[1, :, cc], fb.at[3, pl.ds(H, H), cc], a_snd.at[k + 5], a_rcv.at[k + 5], down),
        ]

    mine = pl.ds(pl.multiple_of(core * TOK, TOK), TOK)
    t_cp, l_tk = [], []
    for i in range(8):
        src = tokens.at[pl.ds(i * SLAB, SLAB), :]
        dst = tok.at[pl.ds(pl.multiple_of(core * TOK + i * SLAB, SLAB), SLAB), :]
        t_cp.append(remote(src, dst, t_snd.at[i], t_rcv.at[i], other))
        l_tk.append(pltpu.make_async_copy(src, dst, loc.at[5 + i]))

    def early():
        l_ex.wait()
        eb[...] = ex[...].astype(F32).astype(BF16)
        for m in e_cp[:3]:
            go(m)
        l_gn.wait()
        gf[...] = gb[...].astype(F32)
        first = 6 * fs + lax.div(3 * rep, 2)
        i = lax.broadcasted_iota(jnp.int32, (128, 128), 0)
        l = lax.broadcasted_iota(jnp.int32, (128, 128), 1)
        for h in range(2):
            row = jnp.broadcast_to(gf[pl.ds(first + h, 1), :], (128, 128))
            column = jnp.sum(jnp.where(i == l, row, 0.0), axis=1, keepdims=True)
            gn[pl.ds(128 * h, 128), :] = jnp.broadcast_to(column, (128, 128))
        e_cp[0].wait_recv()
        go(e_cp[3])

    def prepare():
        for s in (1, 2, 3):
            e_cp[s].wait_recv()
        l_bs.wait()
        l_ms.wait()

    def encode(p):
        c, sub, width, _ = PARTS[p]
        lo = CLS[c][0] + sub
        row0 = pl.multiple_of(rep * ROWS, ROWS)

        def step(t, carry):
            rr = pl.ds(pl.multiple_of(t * SLAB, SLAB), SLAB)
            wr = pl.ds(pl.multiple_of(row0 + t * SLAB, SLAB), SLAB)
            fr = pl.ds(pl.multiple_of(off + t * SLAB, 16), SLAB)
            g = gn[fr, :]
            for k in range(width // 128):
                cc = pl.ds(lo + 128 * k, 128)
                b = bs[rr, cc]
                total = jnp.zeros((SLAB, 128), F32)
                for s in range(4):
                    v = (b - (fv[rep, rr, cc] if s == 0 else fb[s, rr, cc]).astype(F32)) * iv[s, fr, cc].astype(F32)
                    m = jnp.abs(v)
                    level = jnp.zeros_like(m)
                    for mid, val in THRESH:
                        level = jnp.where(m >= mid, val, level)
                    total = total + jnp.where(v < 0.0, -level, level) * sc[s, fr, cc].astype(F32)
                grad = total * 0.25
                nm = MOMENTUM_COEF * ms[rr, cc] + grad
                nb = b - OUTER_RATE * (grad + MOMENTUM_COEF * nm)
                gr[rr, cc] = grad
                W[c][pos["y"], pos["x"], wr, pl.ds(sub + 128 * k, 128)] = (nb * g).astype(BF16)
            return carry

        lax.fori_loop(0, ROWS // SLAB, step, 0)

    def place(p, **at):
        half = at.pop("half", None)
        xs, ys = at.get("x", slice(None)), at.get("y", slice(None))
        if "z" in at:
            r0, n = at["z"] * ROWS, ROWS
        else:
            r0, n = 0, FROWS
        if half is not None:
            n = n // 2
            r0 = r0 + half * n
        if not isinstance(r0, int):
            r0 = pl.multiple_of(r0, 96)
        c, lo, width, _ = PARTS[p]
        cc = pl.ds(lo, width)
        if isinstance(ys, slice) or isinstance(xs, slice):
            pieces = [(t, xs) if isinstance(ys, slice) else (ys, t) for t in range(4)]
            pieces = [W[c].at[yy, xx, pl.ds(r0, n), cc] for yy, xx in pieces]
        else:
            step = n // 4 if n > ROWS else n // 2
            starts = [r0 + t * step for t in range(n // step)]
            if not isinstance(r0, int):
                starts = [pl.multiple_of(t, SLAB) for t in starts]
            pieces = [W[c].at[ys, xs, pl.ds(t, step), cc] for t in starts]
        return W[c].at[ys, xs, pl.ds(r0, n), cc], pieces

    M = {}
    OFF = (0, 1, -1, 2)
    used = [0]

    def both(*pair):
        out = []
        for j, s in enumerate((1, -1)):
            axis, (ref, pieces) = pair[j]
            sems = g_snd.at[used[0]], g_rcv.at[used[0]], nbr(axis, s)
            out.append(Message(remote(ref, ref, *sems), [remote(r, r, *sems) for r in pieces]))
            used[0] += 1
        return out

    def full(p, axis, **fixed):
        here = place(p, **fixed, **{axis: pos[axis]})
        return both((axis, here), (axis, here))

    def half(p, axis, **fixed):
        return both(
            *[(axis, place(p, **fixed, **{axis: mod4(pos[axis] - s), "half": j})) for j, s in enumerate((1, -1))]
        )

    for p in range(len(PARTS)):
        m = a2a(p)
        M["r", p], M["d", p], M["f", p] = m[:2], m[2:4], m[4:]
        a, b, l = PARTS[p][3]
        R, S = (a, b) if b == "z" else (b, a)
        at = {b: pos[b], l: pos[l]}
        M["1", p], M["1h", p] = full(p, a, **at), half(p, a, **at)
        for i in range(4):
            at = {a: mod4(pos[a] + OFF[i]), l: pos[l]}
            M["2", p, i], M["2h", p, i] = full(p, b, **at), half(p, b, **at)
            M["3", p, i] = full(p, l, **{R: pos[R], S: mod4(pos[S] + OFF[i])})
            M["3h", p, i] = half(p, l, **{R: mod4(pos[R] + OFF[i])})
            if i:
                M["3", p, 3 + i] = full(p, l, **{R: mod4(pos[R] + OFF[i])})

    def mm(c, count, coords):
        lo, width = CLS[c]
        cc = pl.ds(lo, width)

        def chunk(t, carry):
            yy, xx = coords(t)
            kk = pl.ds(pl.multiple_of((yy * 4 + xx) * FROWS, FROWS), FROWS)

            def block(m, carry):
                mr = pl.ds(pl.multiple_of(m * 256, 256), 256)
                acc[mr, cc] += jnp.dot(tok[mr, kk], W[c][yy, xx], preferred_element_type=F32)
                return carry

            return lax.fori_loop(0, 3, block, carry)

        lax.fori_loop(0, count, chunk, 0)

    def offset(i):
        return i + lax.div(i, 2) - 2 * lax.div(i, 3)

    def mm_near(c, i):
        if c == 1:
            yy = mod4(pos["y"] + OFF[i])
            mm(c, 3, lambda t: (yy, mod4(pos["x"] + offset(t))))
        else:
            xx = mod4(pos["x"] + OFF[i])
            mm(c, 3, lambda t: (mod4(pos["y"] + offset(t)), xx))

    def mm_far(c, i):
        if c == 1:
            mm(c, 1, lambda t: (mod4(pos["y"] + OFF[i]), mod4(pos["x"] + 2)))
        else:
            mm(c, 1, lambda t: (mod4(pos["y"] + 2), mod4(pos["x"] + OFF[i])))

    same = len({p[3] for p in PARTS if p[0] == 0}) == 1

    def mm_row(c, i):
        by_y = PARTS[[p[0] for p in PARTS].index(0)][3][1] == "y"
        at = mod4(pos["y" if by_y else "x"] + OFF[i])
        mm(c, 4, (lambda t: (at, t)) if by_y else (lambda t: (t, at)))

    def mm_level(c, i):
        def coords(t):
            turn = lax.div(t, i + 1)
            iy = i * (1 - turn) + (t - i - 1) * turn
            ix = t * (1 - turn) + i * turn
            return mod4(pos["y"] + offset(iy)), mod4(pos["x"] + offset(ix))

        mm(c, 2 * i + 1, coords)

    def squares(i):
        rr = pl.ds(pl.multiple_of(core * TOK + i * 128, 128), 128)

        def step(t, s):
            for k in range(4):
                v = tok[rr, pl.ds(pl.multiple_of(t * 512 + k * 128, 128), 128)].astype(F32)
                s = s + v * v
            return s

        s = lax.fori_loop(0, D // 512, step, jnp.zeros((128, 128), F32))
        mean = jnp.sum(s, axis=1, keepdims=True) * (1.0 / D)
        ss[rr, :] = jnp.broadcast_to(lax.rsqrt(mean + 1e-05) * (D ** -0.5), (128, 128))

    def finish(c):
        lo, width = CLS[c]
        cc = pl.ds(lo, width)

        def scale(m, carry):
            mr = pl.ds(pl.multiple_of(m * 64, 64), 64)
            for k in range(width // 128):
                at = pl.ds(lo + 128 * k, 128)
                kv[mr, at] = (acc[mr, at] * ss[mr, :]).astype(BF16)
            return carry

        lax.fori_loop(0, 2 * TOK // 64, scale, 0)
        outs.append(pltpu.make_async_copy(kv.at[:, cc], kv_out.at[:, cc], o_sem.at[1 + c]))
        outs[-1].start()

    s_cp = remote(ss.at[mine, :], ss.at[mine, :], t_snd.at[8], t_rcv.at[8], other)
    outs = []
    left = []
    seen = set()

    def once(name):
        new = name not in seen
        seen.add(name)
        return new

    for kind, *key in SCHEDULE:
        key = tuple(key)
        if kind == "S":
            for m in M[key]:
                m.start()
            left.append(key)
        elif kind == "W":
            if once("wait"):
                early()
            if key[0] == "d":
                if once("prepare"):
                    prepare()
                expand(key[1])
            for m in M[key]:
                m.wait_recv()
        elif kind == "D":
            for m in M[key]:
                m.wait_send()
            left.remove(key)
        elif kind == "E":
            encode(*key)
            left_to_encode = len(PARTS) - 1 - key[0]
            if left_to_encode == 0:
                outs.append(pltpu.make_async_copy(gr, grad_out, o_sem.at[0]))
                outs[0].start()
        elif key[0] == "tk":
            l_tk[key[1]].start()
            go(t_cp[key[1]])
            if once("total"):
                acc[...] = jnp.zeros_like(acc)
        elif key[0] == "sq":
            if once("own tokens"):
                for t in l_tk:
                    t.wait()
            squares(key[1])
            if key[1] == 2:
                go(s_cp)
        elif key[0] == "fin":
            if once("factors"):
                s_cp.wait_recv()
            finish(key[1])
        else:
            if once("all tokens"):
                for t in t_cp:
                    t.wait_recv()
            {"near": mm_near, "far": mm_far, "all": mm_row if same else mm_level}[key[3]](key[1], key[2])
    for key in left:
        for m in M[key]:
            m.wait_send()

    for p in pending:
        p.wait_send()
    for o in outs:
        o.wait()


def write_kernel(grad, base, mom, kv, nb_out, nm_out, kv_out, gr, bs, ms, ks, in_sem, out_sem, kv_in, kv_sem):
    loads, stores, moves = [], [], []
    for q in range(4):
        rr = pl.ds(q * SLAB, SLAB)
        for i, (src, dst) in enumerate(((grad, gr), (base, bs), (mom, ms))):
            loads.append(pltpu.make_async_copy(src.at[rr, :], dst.at[rr, :], in_sem.at[3 * q + i]))
            loads[-1].start()
    for q in range(4):
        rr = pl.ds(q * 192, 192)
        moves.append(pltpu.make_async_copy(kv.at[rr, :], ks.at[rr, :], kv_in.at[q]))
        moves[-1].start()
    for q in range(4):
        rr = pl.ds(q * SLAB, SLAB)
        for i in range(3):
            loads[3 * q + i].wait()
        g = gr[rr, :]
        nm = MOMENTUM_COEF * ms[rr, :] + g
        ms[rr, :] = nm
        bs[rr, :] = bs[rr, :] - OUTER_RATE * (g + MOMENTUM_COEF * nm)
        stores.append(pltpu.make_async_copy(bs.at[rr, :], nb_out.at[rr, :], out_sem.at[2 * q]))
        stores.append(pltpu.make_async_copy(ms.at[rr, :], nm_out.at[rr, :], out_sem.at[2 * q + 1]))
        stores[-2].start()
        stores[-1].start()
    for q in range(4):
        rr = pl.ds(q * 192, 192)
        moves[q].wait()
        stores.append(pltpu.make_async_copy(ks.at[rr, :], kv_out.at[rr, :], kv_sem.at[q]))
        stores[-1].start()
    for copy in stores:
        copy.wait()


def body(tokens, norm_gain, fragment, exponents, base_weight, momentum):
    any_ = pl.BlockSpec(memory_space=pl.ANY)
    dma = pltpu.SemaphoreType.DMA
    vm = pltpu.VMEM
    grad, keys_values = pl.pallas_call(
        kernel,
        out_shape=(
            jax.ShapeDtypeStruct((ROWS, KVW), F32),
            jax.ShapeDtypeStruct((2 * TOK, KVW), BF16),
        ),
        in_specs=[any_] * 6,
        out_specs=[any_] * 2,
        scratch_shapes=[
            *[vm((4, 4, FROWS, width), BF16) for _, width in CLS],
            vm((2 * TOK, D), BF16),
            vm((2 * TOK, KVW), F32),
            vm((2 * TOK, KVW), BF16),
            vm((4, ROWS, KVW), BF16),
            vm((4, ROWS, KVW), BF16),
            vm((2, ROWS // 2, KVW), BF16),
            vm((ROWS, KVW), F32),
            vm((ROWS, KVW), F32),
            vm((ROWS, KVW), F32),
            vm((D // 128, 128), BF16),
            vm((D // 128, 128), F32),
            vm((256, 128), F32),
            vm((BLOCK, 4 * ROWS), jnp.int32),
            vm((BLOCK, 4 * ROWS), BF16),
            vm((4, BLOCK, 256), BF16),
            vm((BLOCK, 256), BF16),
            vm((4, 256, KVW), BF16),
            vm((4, 256, KVW), BF16),
            vm((2 * TOK, 128), F32),
            dma((13,)),
            dma((6 * len(PARTS),)),
            dma((6 * len(PARTS),)),
            dma((4,)),
            dma((4,)),
            dma((9,)),
            dma((9,)),
            dma((42 * len(PARTS),)),
            dma((42 * len(PARTS),)),
            dma((4,)),
        ],
        compiler_params=pltpu.CompilerParams(
            collective_id=0, has_side_effects=True, vmem_limit_bytes=62 * 1024 * 1024
        ),
        cost_estimate=pl.CostEstimate(flops=2 * 768 * 12288 * 1024, bytes_accessed=30_000_000, transcendentals=0),
    )(
        tokens,
        norm_gain.reshape(D // 128, 128),
        fragment.reshape(4, ROWS, KVW),
        exponents[0].T,
        base_weight,
        momentum,
    )
    return pl.pallas_call(
        write_kernel,
        out_shape=(
            jax.ShapeDtypeStruct((ROWS, KVW), F32),
            jax.ShapeDtypeStruct((ROWS, KVW), F32),
            jax.ShapeDtypeStruct((2 * TOK, KVW), BF16),
        ),
        in_specs=[any_] * 4,
        out_specs=[any_] * 3,
        scratch_shapes=[vm((ROWS, KVW), F32)] * 3
        + [vm((2 * TOK, KVW), BF16), dma((12,)), dma((8,)), dma((4,)), dma((4,))],
        compiler_params=pltpu.CompilerParams(vmem_limit_bytes=62 * 1024 * 1024),
        cost_estimate=pl.CostEstimate(flops=6 * ROWS * KVW, bytes_accessed=7_000_000, transcendentals=0),
    )(grad, base_weight, momentum, keys_values)


def solution(mesh):
    in_specs = (
        P(("replica", "fsdp", "tensor"), None),
        P(),
        P("replica", "fsdp", "tensor"),
        P("replica", "fsdp", "tensor"),
        P(("fsdp", "replica"), "tensor"),
        P(("fsdp", "replica"), "tensor"),
    )
    out_specs = (
        P(("fsdp", "replica"), "tensor"),
        P(("fsdp", "replica"), "tensor"),
        P(("replica", "fsdp"), "tensor"),
    )
    return jax.shard_map(body, mesh=mesh, in_specs=in_specs, out_specs=out_specs, check_vma=False)
```

```python
import jax
import jax.numpy as jnp
from jax import lax
from jax.experimental import pallas as pl
from jax.experimental.pallas import tpu as pltpu
from jax.sharding import PartitionSpec as P

MESH = pl.DeviceIdType.MESH
F32, BF16 = jnp.float32, jnp.bfloat16
D, KVW, BLOCK, TOK = 12288, 1024, 32, 384
ROWS = 192
FROWS = 768
SLAB = 48
OUTER_RATE = 0.7
MOMENTUM_COEF = 0.9
CLS = ((0, 256), (256, 384), (640, 384))
PARTS = (
    (0, 128, 128, ("y", "x", "z")),
    (0, 0, 128, ("x", "y", "z")),
    (2, 0, 128, ("z", "x", "y")),
    (1, 0, 128, ("z", "y", "x")),
    (1, 128, 256, ("y", "z", "x")),
    (2, 128, 256, ("x", "z", "y")),
)

SCHEDULE = (
    ("S", "r", 0), ("S", "d", 0), ("S", "r", 1), ("S", "d", 1), ("S", "r", 2), ("W", "r", 0), ("S", "f", 0),
    ("S", "d", 2), ("W", "r", 1), ("S", "f", 1), ("S", "r", 3), ("S", "d", 3), ("W", "d", 0), ("W", "f", 0), ("E", 0),
    ("S", "2", 0, 0), ("S", "1", 0), ("D", "r", 0), ("W", "r", 2), ("S", "f", 2), ("D", "r", 1), ("S", "r", 4),
    ("W", "d", 1), ("W", "f", 1), ("E", 1), ("S", "1", 1), ("S", "2", 1, 0), ("D", "d", 0), ("W", "r", 3),
    ("S", "f", 3), ("S", "d", 4), ("W", "2", 0, 0), ("S", "2h", 0, 0), ("W", "1", 0), ("S", "1h", 0),
    ("S", "2", 0, 1), ("S", "2", 0, 2), ("W", "d", 2), ("W", "f", 2), ("E", 2), ("W", "1", 1), ("S", "2", 1, 1),
    ("D", "r", 2), ("D", "d", 1), ("D", "f", 0), ("D", "f", 1), ("W", "r", 4), ("S", "f", 4), ("W", "2", 1, 0),
    ("S", "2h", 1, 0), ("S", "1h", 1), ("D", "r", 3), ("D", "d", 2), ("S", "r", 5), ("S", "2", 1, 2), ("W", "1h", 0),
    ("S", "2", 0, 3), ("D", "d", 3), ("S", "d", 5), ("S", "2", 2, 0), ("S", "1", 2), ("S", "3", 2, 0), ("W", "d", 3),
    ("W", "f", 3), ("E", 3), ("D", "1", 0), ("S", "2", 3, 0), ("D", "2", 0, 0), ("W", "2", 0, 1), ("S", "2h", 0, 1),
    ("W", "2", 0, 2), ("S", "2h", 0, 2), ("W", "2", 1, 1), ("S", "2h", 1, 1), ("W", "1h", 1), ("S", "2", 1, 3),
    ("D", "f", 2), ("D", "r", 4), ("S", "1", 3), ("D", "1", 1), ("S", "3", 3, 0), ("W", "d", 4), ("W", "f", 4),
    ("E", 4), ("D", "2h", 0, 0), ("W", "2", 0, 3), ("S", "2h", 0, 3), ("D", "2", 1, 0), ("D", "1h", 0), ("S", "1", 4),
    ("W", "2", 2, 0), ("S", "2h", 2, 0), ("D", "f", 3), ("D", "d", 4), ("W", "r", 5), ("S", "f", 5), ("W", "1", 2),
    ("S", "2", 2, 1), ("S", "1h", 2), ("D", "2", 0, 1), ("D", "2", 0, 2), ("S", "2", 2, 2), ("S", "2", 4, 0),
    ("D", "2", 1, 1), ("D", "2h", 1, 0), ("W", "2", 1, 2), ("S", "2h", 1, 2), ("W", "2", 3, 0), ("S", "2h", 3, 0),
    ("D", "1h", 1), ("S", "3", 4, 0), ("W", "1", 3), ("S", "2", 3, 1), ("D", "f", 4), ("S", "1h", 3),
    ("W", "2", 1, 3), ("S", "2h", 1, 3), ("S", "2", 3, 2), ("S", "3", 0, 0), ("C", "tk", 0), ("S", "3", 3, 1),
    ("C", "tk", 1), ("D", "2", 0, 3), ("W", "1h", 2), ("S", "2", 2, 3), ("D", "r", 5), ("S", "3", 1, 0),
    ("D", "2", 1, 2), ("S", "3", 2, 1), ("W", "d", 5), ("W", "f", 5), ("E", 5), ("D", "1", 2), ("S", "2", 5, 0),
    ("D", "3", 2, 0), ("D", "2h", 1, 1), ("D", "2", 3, 0), ("W", "1h", 3), ("S", "2", 3, 3), ("D", "2", 2, 0),
    ("D", "2h", 0, 1), ("D", "2h", 0, 2), ("D", "3", 3, 0), ("D", "2h", 0, 3), ("S", "1", 5), ("W", "2", 2, 1),
    ("S", "2h", 2, 1), ("D", "2", 1, 3), ("W", "1", 4), ("S", "1h", 4), ("D", "1", 3), ("D", "d", 5),
    ("S", "2", 4, 1), ("D", "2h", 2, 0), ("W", "2", 2, 2), ("S", "2h", 2, 2), ("S", "2", 4, 2), ("S", "3", 5, 0),
    ("C", "tk", 2), ("C", "tk", 3), ("W", "2", 3, 1), ("S", "2h", 3, 1), ("S", "3", 3, 2), ("C", "tk", 4),
    ("W", "2", 3, 2), ("S", "2h", 3, 2), ("D", "2", 2, 1), ("W", "2", 2, 3), ("S", "2h", 2, 3), ("D", "1h", 2),
    ("D", "f", 5), ("W", "2", 4, 0), ("S", "2h", 4, 0), ("D", "2", 2, 2), ("S", "3", 4, 1), ("D", "2h", 1, 2),
    ("D", "2h", 3, 0), ("S", "3", 2, 2), ("C", "tk", 5), ("D", "1", 4), ("D", "2h", 1, 3), ("S", "3", 2, 3),
    ("W", "2", 3, 3), ("S", "2h", 3, 3), ("D", "3", 3, 1), ("S", "3", 4, 2), ("D", "1h", 3), ("D", "3", 0, 0),
    ("S", "3", 0, 1), ("W", "1h", 4), ("S", "2", 4, 3), ("D", "2", 3, 1), ("D", "2", 3, 2), ("S", "3", 2, 4),
    ("C", "tk", 6), ("D", "2", 2, 3), ("D", "3", 4, 0), ("S", "3", 3, 3), ("D", "2h", 2, 1), ("W", "1", 5),
    ("S", "1h", 5), ("D", "2", 4, 0), ("D", "3", 1, 0), ("W", "2", 5, 0), ("S", "2h", 5, 0), ("S", "2", 5, 1),
    ("S", "2", 5, 2), ("C", "tk", 7), ("D", "2h", 2, 2), ("W", "2h", 4, 0), ("S", "3", 4, 3), ("W", "2", 4, 1),
    ("S", "2h", 4, 1), ("D", "3", 2, 1), ("D", "2", 3, 3), ("D", "2h", 3, 1), ("D", "1h", 4), ("D", "2h", 3, 2),
    ("S", "3", 5, 1), ("W", "2", 4, 2), ("S", "2h", 4, 2), ("D", "2h", 2, 3), ("D", "3", 3, 2), ("S", "3", 3, 4),
    ("S", "3", 5, 2), ("C", "sq", 0), ("D", "2", 5, 0), ("D", "2h", 4, 0), ("D", "2", 4, 1), ("W", "1h", 5),
    ("S", "2", 5, 3), ("D", "2h", 3, 3), ("D", "3", 2, 2), ("D", "3", 2, 3), ("D", "3", 5, 0), ("S", "3", 2, 5),
    ("C", "sq", 1), ("D", "1", 5), ("D", "3", 4, 1), ("S", "3", 3, 5), ("C", "sq", 2), ("W", "3", 3, 0),
    ("W", "3", 3, 1), ("W", "3", 3, 2), ("W", "3", 3, 3), ("W", "3", 4, 0), ("W", "3", 4, 1), ("W", "3", 4, 2),
    ("W", "3", 4, 3), ("C", "mm", 1, 0, "near"), ("D", "2", 4, 2), ("D", "3", 0, 1), ("D", "2h", 5, 0),
    ("W", "2", 4, 3), ("S", "2h", 4, 3), ("W", "2h", 5, 0), ("S", "3", 5, 3), ("W", "2", 5, 1), ("S", "2h", 5, 1),
    ("W", "2", 5, 2), ("S", "2h", 5, 2), ("D", "3", 3, 3), ("D", "3", 4, 2), ("D", "1h", 5), ("D", "3", 4, 3),
    ("W", "2h", 4, 1), ("S", "3", 4, 4), ("D", "3", 2, 4), ("W", "2h", 2, 0), ("W", "2h", 2, 1), ("W", "2h", 2, 2),
    ("W", "2h", 2, 3), ("S", "3", 2, 6), ("W", "2", 5, 3), ("S", "2h", 5, 3), ("D", "2h", 4, 1), ("S", "3", 1, 1),
    ("D", "2h", 4, 2), ("D", "2", 4, 3), ("S", "3", 0, 2), ("S", "3", 1, 2), ("D", "3", 5, 1), ("D", "3", 5, 2),
    ("W", "3", 2, 0), ("W", "3", 2, 1), ("W", "3", 2, 2), ("W", "3", 2, 3), ("S", "3h", 2, 0), ("D", "2", 5, 1),
    ("D", "2", 5, 2), ("S", "3", 0, 3), ("D", "2", 5, 3), ("S", "3", 1, 3), ("W", "3", 5, 0), ("W", "3", 5, 1),
    ("W", "3", 5, 2), ("W", "3", 5, 3), ("C", "mm", 2, 0, "near"), ("D", "3", 2, 5), ("W", "2h", 5, 1),
    ("S", "3", 5, 4), ("D", "2h", 4, 3), ("S", "3", 0, 4), ("D", "3", 3, 4), ("D", "3", 3, 5), ("W", "2h", 4, 2),
    ("S", "3", 4, 5), ("D", "2h", 5, 1), ("D", "2h", 5, 2), ("S", "3", 1, 4), ("W", "3", 3, 4), ("W", "3", 4, 4),
    ("C", "mm", 1, 1, "near"), ("D", "3", 5, 3), ("D", "3", 2, 6), ("D", "3h", 2, 0), ("W", "2h", 5, 2),
    ("S", "3", 5, 5), ("D", "2h", 5, 3), ("D", "3", 1, 1), ("D", "3", 0, 2), ("D", "3", 1, 2), ("D", "3", 0, 3),
    ("D", "3", 1, 3), ("S", "3", 0, 5), ("W", "2h", 3, 0), ("W", "2h", 3, 1), ("W", "2h", 3, 2), ("W", "2h", 3, 3),
    ("S", "3", 3, 6), ("S", "3", 1, 5), ("D", "3", 4, 4), ("W", "2h", 4, 3), ("S", "3", 4, 6), ("W", "3", 2, 4),
    ("W", "3", 5, 4), ("C", "mm", 2, 1, "near"), ("W", "2h", 5, 3), ("S", "3", 5, 6), ("D", "3", 0, 4),
    ("W", "2h", 0, 0), ("W", "2h", 0, 1), ("W", "2h", 0, 2), ("W", "2h", 0, 3), ("S", "3", 0, 6), ("W", "3", 3, 5),
    ("W", "3", 4, 5), ("C", "mm", 1, 2, "near"), ("D", "3", 1, 4), ("W", "2h", 1, 0), ("W", "2h", 1, 1),
    ("W", "2h", 1, 2), ("W", "2h", 1, 3), ("S", "3", 1, 6), ("D", "3", 4, 5), ("S", "3h", 3, 0), ("W", "3", 2, 5),
    ("W", "3", 5, 5), ("C", "mm", 2, 2, "near"), ("D", "3", 3, 6), ("S", "3h", 4, 0), ("D", "3", 5, 4),
    ("S", "3h", 5, 0), ("D", "3", 0, 5), ("W", "3", 0, 0), ("W", "3", 0, 1), ("W", "3", 0, 2), ("W", "3", 0, 3),
    ("S", "3h", 0, 0), ("D", "3", 1, 5), ("W", "3", 1, 0), ("W", "3", 1, 1), ("W", "3", 1, 2), ("W", "3", 1, 3),
    ("S", "3h", 1, 0), ("S", "3h", 3, 1), ("D", "3", 5, 5), ("S", "3h", 2, 1), ("W", "3", 3, 6), ("W", "3", 4, 6),
    ("C", "mm", 1, 3, "near"), ("D", "3", 0, 6), ("W", "3", 0, 4), ("S", "3h", 0, 1), ("S", "3h", 4, 1),
    ("S", "3h", 5, 1), ("W", "3", 1, 4), ("S", "3h", 1, 1), ("W", "3", 2, 6), ("W", "3", 5, 6),
    ("C", "mm", 2, 3, "near"), ("W", "3", 0, 5), ("S", "3h", 0, 2), ("D", "3", 4, 6), ("D", "3h", 3, 0),
    ("S", "3h", 3, 2), ("W", "3h", 0, 0), ("W", "3h", 1, 0), ("C", "mm", 0, 0, "all"), ("W", "3h", 3, 0),
    ("W", "3h", 4, 0), ("C", "mm", 1, 0, "far"), ("D", "3", 5, 6), ("S", "3h", 2, 2), ("D", "3", 1, 6),
    ("D", "3h", 0, 0), ("W", "3", 1, 5), ("S", "3h", 1, 2), ("S", "3h", 4, 2), ("W", "3h", 2, 0), ("W", "3h", 5, 0),
    ("C", "mm", 2, 0, "far"), ("S", "3h", 5, 2), ("D", "3h", 1, 0), ("W", "3", 0, 6), ("S", "3h", 0, 3),
    ("W", "3h", 0, 1), ("W", "3h", 1, 1), ("C", "mm", 0, 1, "all"), ("W", "3", 1, 6), ("S", "3h", 1, 3),
    ("W", "3h", 2, 1), ("W", "3h", 5, 1), ("C", "mm", 2, 1, "far"), ("D", "3h", 4, 0), ("D", "3h", 3, 1),
    ("S", "3h", 3, 3), ("W", "3h", 3, 1), ("W", "3h", 4, 1), ("C", "mm", 1, 1, "far"), ("D", "3h", 2, 1),
    ("D", "3h", 5, 0), ("S", "3h", 2, 3), ("S", "3h", 4, 3), ("S", "3h", 5, 3), ("W", "3h", 0, 2), ("W", "3h", 1, 2),
    ("C", "mm", 0, 2, "all"), ("W", "3h", 0, 3), ("W", "3h", 1, 3), ("C", "mm", 0, 3, "all"), ("C", "fin", 0),
    ("W", "3h", 3, 2), ("W", "3h", 4, 2), ("C", "mm", 1, 2, "far"), ("W", "3h", 2, 2), ("W", "3h", 5, 2),
    ("C", "mm", 2, 2, "far"), ("W", "3h", 3, 3), ("W", "3h", 4, 3), ("C", "mm", 1, 3, "far"), ("C", "fin", 1),
    ("W", "3h", 2, 3), ("W", "3h", 5, 3), ("C", "mm", 2, 3, "far"), ("C", "fin", 2),
)

THRESH = ((0.25, 0.5), (0.75, 1.0), (1.25, 1.5), (1.75, 2.0), (2.5, 3.0), (3.5, 4.0), (5.0, 6.0))


def mod4(v):
    return lax.rem(v + 8, 4)


def kernel(
    tokens, gain, frag, exps, base, mom,
    nb, nm, kv,
    w0, w1, w2, tok, acc, fv, fb, rl, bs, ms, gb, gf, gn, ex, eb, er, erl, sc, iv, ss,
    loc, a_snd, a_rcv, e_snd, e_rcv, t_snd, t_rcv, g_snd, g_rcv,
):
    W = (w0, w1, w2)
    rep = lax.axis_index("replica")
    fs = lax.axis_index("fsdp")
    core = lax.axis_index("tensor")
    pos = {"x": lax.rem(fs, 4), "y": lax.div(fs, 4), "z": rep}

    def nbr(axis, step):
        c = dict(pos)
        c[axis] = mod4(pos[axis] + step)
        return (c["z"], c["y"] * 4 + c["x"], core)

    other = (rep, fs, 1 - core)

    def remote(src, dst, ss_, rs_, dev):
        return pltpu.make_async_remote_copy(
            src_ref=src, dst_ref=dst, send_sem=ss_, recv_sem=rs_, device_id=dev, device_id_type=MESH
        )

    pending = []

    def go(copy):
        copy.start()
        pending.append(copy)

    barrier = pltpu.get_barrier_semaphore()
    peers = [nbr(a, s) for a in "xyz" for s in (1, -1)] + [other]
    for p in peers:
        pl.semaphore_signal(barrier, inc=1, device_id=p, device_id_type=MESH)

    l_ex = pltpu.make_async_copy(exps, ex, loc.at[0])
    l_ex.start()
    l_fr = pltpu.make_async_copy(frag, fv, loc.at[1])
    l_fr.start()
    l_bs = pltpu.make_async_copy(base, bs, loc.at[2])
    l_bs.start()
    l_ms = pltpu.make_async_copy(mom, ms, loc.at[3])
    l_ms.start()
    l_gn = pltpu.make_async_copy(gain, gb, loc.at[4])
    l_gn.start()

    pl.semaphore_wait(barrier, len(peers))
    l_fr.wait()

    up, down = nbr("z", 1), nbr("z", -1)
    zu, zd, zo = mod4(rep + 1), mod4(rep - 1), mod4(rep + 2)

    def window(d):
        return eb.at[:, pl.ds(pl.multiple_of(128 * lax.div(3 * d, 2), 128), 256)]

    off = 64 * lax.rem(rep, 2)

    def expand(lo, width):
        j = lax.broadcasted_iota(jnp.int32, (BLOCK, width), 0)
        n = lax.broadcasted_iota(jnp.int32, (BLOCK, width), 1)
        pick = jnp.where(j == lax.div(n + lo, BLOCK), 1.0, 0.0).astype(BF16)
        for slot in range(4):
            e = (window(rep)[...] if slot == 0 else er[slot]).astype(F32)
            for ref, sign in ((sc, 1.0), (iv, -1.0)):
                small = jnp.exp2(sign * e).astype(BF16)
                full = lax.dot_general(small, pick, (((0,), (0,)), ((), ())), preferred_element_type=F32)
                ref[slot, :, pl.ds(lo, width)] = full.astype(BF16)

    e_cp = [
        remote(window(zo), erl, e_snd.at[0], e_rcv.at[0], up),
        remote(window(zu), er.at[1], e_snd.at[1], e_rcv.at[1], up),
        remote(window(zd), er.at[2], e_snd.at[2], e_rcv.at[2], down),
        remote(erl, er.at[3], e_snd.at[3], e_rcv.at[3], up),
    ]

    def cols(p):
        c, lo, width, _ = PARTS[p]
        return pl.ds(CLS[c][0] + lo, width)

    H = ROWS // 2

    def a2a(p):
        k = 6 * p
        cc = cols(p)
        return [
            remote(fv.at[zo, pl.ds(0, H), cc], rl.at[0, :, cc], a_snd.at[k], a_rcv.at[k], up),
            remote(fv.at[zo, pl.ds(H, H), cc], rl.at[1, :, cc], a_snd.at[k + 1], a_rcv.at[k + 1], down),
            remote(fv.at[zu, :, cc], fb.at[1, :, cc], a_snd.at[k + 2], a_rcv.at[k + 2], up),
            remote(fv.at[zd, :, cc], fb.at[2, :, cc], a_snd.at[k + 3], a_rcv.at[k + 3], down),
            remote(rl.at[0, :, cc], fb.at[3, pl.ds(0, H), cc], a_snd.at[k + 4], a_rcv.at[k + 4], up),
            remote(rl.at[1, :, cc], fb.at[3, pl.ds(H, H), cc], a_snd.at[k + 5], a_rcv.at[k + 5], down),
        ]

    mine = pl.ds(pl.multiple_of(core * TOK, TOK), TOK)
    t_cp, l_tk = [], []
    for i in range(8):
        src = tokens.at[pl.ds(i * SLAB, SLAB), :]
        dst = tok.at[pl.ds(pl.multiple_of(core * TOK + i * SLAB, SLAB), SLAB), :]
        t_cp.append(remote(src, dst, t_snd.at[i], t_rcv.at[i], other))
        l_tk.append(pltpu.make_async_copy(src, dst, loc.at[5 + i]))

    def early():
        l_ex.wait()
        eb[...] = ex[...].astype(F32).astype(BF16)
        for m in e_cp[:3]:
            go(m)
        l_gn.wait()
        gf[...] = gb[...].astype(F32)
        first = 6 * fs + lax.div(3 * rep, 2)
        i = lax.broadcasted_iota(jnp.int32, (128, 128), 0)
        l = lax.broadcasted_iota(jnp.int32, (128, 128), 1)
        for h in range(2):
            row = jnp.broadcast_to(gf[pl.ds(first + h, 1), :], (128, 128))
            column = jnp.sum(jnp.where(i == l, row, 0.0), axis=1, keepdims=True)
            gn[pl.ds(128 * h, 128), :] = jnp.broadcast_to(column, (128, 128))
        e_cp[0].wait_recv()
        go(e_cp[3])

    def prepare():
        for s in (1, 2, 3):
            e_cp[s].wait_recv()
        l_bs.wait()
        l_ms.wait()

    def encode(p):
        c, sub, width, _ = PARTS[p]
        lo = CLS[c][0] + sub
        row0 = pl.multiple_of(rep * ROWS, ROWS)

        def step(t, carry):
            rr = pl.ds(pl.multiple_of(t * SLAB, SLAB), SLAB)
            wr = pl.ds(pl.multiple_of(row0 + t * SLAB, SLAB), SLAB)
            fr = pl.ds(pl.multiple_of(off + t * SLAB, 16), SLAB)
            g = gn[fr, :]
            for k in range(width // 128):
                cc = pl.ds(lo + 128 * k, 128)
                b = bs[rr, cc]
                total = jnp.zeros((SLAB, 128), F32)
                for s in range(4):
                    v = (b - (fv[rep, rr, cc] if s == 0 else fb[s, rr, cc]).astype(F32)) * iv[s, fr, cc].astype(F32)
                    m = jnp.abs(v)
                    level = jnp.zeros_like(m)
                    for mid, val in THRESH:
                        level = jnp.where(m >= mid, val, level)
                    total = total + jnp.where(v < 0.0, -level, level) * sc[s, fr, cc].astype(F32)
                grad = total * 0.25
                moment = MOMENTUM_COEF * ms[rr, cc] + grad
                new = b - OUTER_RATE * (grad + MOMENTUM_COEF * moment)
                nm[rr, cc] = moment
                nb[rr, cc] = new
                W[c][pos["y"], pos["x"], wr, pl.ds(sub + 128 * k, 128)] = (new * g).astype(BF16)
            return carry

        lax.fori_loop(0, ROWS // SLAB, step, 0)

    def place(p, **at):
        half = at.pop("half", None)
        xs, ys = at.get("x", slice(None)), at.get("y", slice(None))
        if "z" in at:
            r0, n = at["z"] * ROWS, ROWS
        else:
            r0, n = 0, FROWS
        if half is not None:
            n = n // 2
            r0 = r0 + half * n
        if not isinstance(r0, int):
            r0 = pl.multiple_of(r0, 96)
        c, lo, width, _ = PARTS[p]
        return W[c].at[ys, xs, pl.ds(r0, n), pl.ds(lo, width)]

    M = {}
    OFF = (0, 1, -1, 2)
    used = [0]

    def both(*pair):
        out = []
        for j, s in enumerate((1, -1)):
            axis, ref = pair[j]
            out.append(remote(ref, ref, g_snd.at[used[0]], g_rcv.at[used[0]], nbr(axis, s)))
            used[0] += 1
        return out

    def full(p, axis, **fixed):
        here = place(p, **fixed, **{axis: pos[axis]})
        return both((axis, here), (axis, here))

    def half(p, axis, **fixed):
        return both(
            *[(axis, place(p, **fixed, **{axis: mod4(pos[axis] - s), "half": j})) for j, s in enumerate((1, -1))]
        )

    for p in range(len(PARTS)):
        m = a2a(p)
        M["r", p], M["d", p], M["f", p] = m[:2], m[2:4], m[4:]
        a, b, l = PARTS[p][3]
        R, S = (a, b) if b == "z" else (b, a)
        at = {b: pos[b], l: pos[l]}
        M["1", p], M["1h", p] = full(p, a, **at), half(p, a, **at)
        for i in range(4):
            at = {a: mod4(pos[a] + OFF[i]), l: pos[l]}
            M["2", p, i], M["2h", p, i] = full(p, b, **at), half(p, b, **at)
            M["3", p, i] = full(p, l, **{R: pos[R], S: mod4(pos[S] + OFF[i])})
            M["3h", p, i] = half(p, l, **{R: mod4(pos[R] + OFF[i])})
            if i:
                M["3", p, 3 + i] = full(p, l, **{R: mod4(pos[R] + OFF[i])})

    def mm(c, count, coords):
        lo, width = CLS[c]
        cc = pl.ds(lo, width)

        def chunk(t, carry):
            yy, xx = coords(t)
            kk = pl.ds(pl.multiple_of((yy * 4 + xx) * FROWS, FROWS), FROWS)

            def block(m, carry):
                mr = pl.ds(pl.multiple_of(m * 256, 256), 256)
                acc[mr, cc] += jnp.dot(tok[mr, kk], W[c][yy, xx], preferred_element_type=F32)
                return carry

            return lax.fori_loop(0, 3, block, carry)

        lax.fori_loop(0, count, chunk, 0)

    def offset(i):
        return i + lax.div(i, 2) - 2 * lax.div(i, 3)

    def mm_near(c, i):
        if c == 1:
            yy = mod4(pos["y"] + OFF[i])
            mm(c, 3, lambda t: (yy, mod4(pos["x"] + offset(t))))
        else:
            xx = mod4(pos["x"] + OFF[i])
            mm(c, 3, lambda t: (mod4(pos["y"] + offset(t)), xx))

    def mm_far(c, i):
        if c == 1:
            mm(c, 1, lambda t: (mod4(pos["y"] + OFF[i]), mod4(pos["x"] + 2)))
        else:
            mm(c, 1, lambda t: (mod4(pos["y"] + 2), mod4(pos["x"] + OFF[i])))

    same = len({p[3] for p in PARTS if p[0] == 0}) == 1

    def mm_row(c, i):
        by_y = PARTS[[p[0] for p in PARTS].index(0)][3][1] == "y"
        at = mod4(pos["y" if by_y else "x"] + OFF[i])
        mm(c, 4, (lambda t: (at, t)) if by_y else (lambda t: (t, at)))

    def mm_level(c, i):
        def coords(t):
            turn = lax.div(t, i + 1)
            iy = i * (1 - turn) + (t - i - 1) * turn
            ix = t * (1 - turn) + i * turn
            return mod4(pos["y"] + offset(iy)), mod4(pos["x"] + offset(ix))

        mm(c, 2 * i + 1, coords)

    def squares(i):
        rr = pl.ds(pl.multiple_of(core * TOK + i * 128, 128), 128)

        def step(t, s):
            for k in range(4):
                v = tok[rr, pl.ds(pl.multiple_of(t * 512 + k * 128, 128), 128)].astype(F32)
                s = s + v * v
            return s

        s = lax.fori_loop(0, D // 512, step, jnp.zeros((128, 128), F32))
        mean = jnp.sum(s, axis=1, keepdims=True) * (1.0 / D)
        ss[rr, :] = jnp.broadcast_to(lax.rsqrt(mean + 1e-05) * (D ** -0.5), (128, 128))

    def finish(c):
        lo, width = CLS[c]

        def scale(m, carry):
            mr = pl.ds(pl.multiple_of(m * 64, 64), 64)
            for k in range(width // 128):
                at = pl.ds(lo + 128 * k, 128)
                kv[mr, at] = (acc[mr, at] * ss[mr, :]).astype(BF16)
            return carry

        lax.fori_loop(0, 2 * TOK // 64, scale, 0)

    s_cp = remote(ss.at[mine, :], ss.at[mine, :], t_snd.at[8], t_rcv.at[8], other)
    left = []
    seen = set()

    def once(name):
        new = name not in seen
        seen.add(name)
        return new

    for kind, *key in SCHEDULE:
        key = tuple(key)
        if kind == "S":
            for m in M[key]:
                m.start()
            left.append(key)
        elif kind == "W":
            if once("wait"):
                early()
            if key[0] == "d":
                if once("prepare"):
                    prepare()
                c = PARTS[key[1]][0]
                if once(("factors", c)):
                    expand(*CLS[c])
            for m in M[key]:
                m.wait_recv()
        elif kind == "D":
            for m in M[key]:
                m.wait_send()
            left.remove(key)
        elif kind == "E":
            encode(*key)
        elif key[0] == "tk":
            l_tk[key[1]].start()
            go(t_cp[key[1]])
            if once("total"):
                acc[...] = jnp.zeros_like(acc)
        elif key[0] == "sq":
            if once("own tokens"):
                for t in l_tk:
                    t.wait()
            squares(key[1])
            if key[1] == 2:
                go(s_cp)
        elif key[0] == "fin":
            if once("factors"):
                s_cp.wait_recv()
            finish(key[1])
        else:
            if once("all tokens"):
                for t in t_cp:
                    t.wait_recv()
            {"near": mm_near, "far": mm_far, "all": mm_row if same else mm_level}[key[3]](key[1], key[2])
    for key in left:
        for m in M[key]:
            m.wait_send()

    for p in pending:
        p.wait_send()


def body(tokens, norm_gain, fragment, exponents, base_weight, momentum):
    any_ = pl.BlockSpec(memory_space=pl.ANY)
    dma = pltpu.SemaphoreType.DMA
    vm = pltpu.VMEM
    return pl.pallas_call(
        kernel,
        out_shape=(vm((ROWS, KVW), F32), vm((ROWS, KVW), F32), vm((2 * TOK, KVW), BF16)),
        in_specs=[any_] * 6,
        out_specs=[pl.BlockSpec(memory_space=vm)] * 3,
        scratch_shapes=[
            *[vm((4, 4, FROWS, width), BF16) for _, width in CLS],
            vm((2 * TOK, D), BF16),
            vm((2 * TOK, KVW), F32),
            vm((4, ROWS, KVW), BF16),
            vm((4, ROWS, KVW), BF16),
            vm((2, ROWS // 2, KVW), BF16),
            vm((ROWS, KVW), F32),
            vm((ROWS, KVW), F32),
            vm((D // 128, 128), BF16),
            vm((D // 128, 128), F32),
            vm((256, 128), F32),
            vm((BLOCK, 4 * ROWS), jnp.int32),
            vm((BLOCK, 4 * ROWS), BF16),
            vm((4, BLOCK, 256), BF16),
            vm((BLOCK, 256), BF16),
            vm((4, 256, KVW), BF16),
            vm((4, 256, KVW), BF16),
            vm((2 * TOK, 128), F32),
            dma((13,)),
            dma((6 * len(PARTS),)),
            dma((6 * len(PARTS),)),
            dma((4,)),
            dma((4,)),
            dma((9,)),
            dma((9,)),
            dma((42 * len(PARTS),)),
            dma((42 * len(PARTS),)),
        ],
        compiler_params=pltpu.CompilerParams(
            collective_id=0, has_side_effects=True, vmem_limit_bytes=59 * 1024 * 1024
        ),
        cost_estimate=pl.CostEstimate(flops=2 * 768 * 12288 * 1024, bytes_accessed=30_000_000, transcendentals=0),
    )(
        tokens,
        norm_gain.reshape(D // 128, 128),
        fragment.reshape(4, ROWS, KVW),
        exponents[0].T,
        base_weight,
        momentum,
    )


def solution(mesh):
    in_specs = (
        P(("replica", "fsdp", "tensor"), None),
        P(),
        P("replica", "fsdp", "tensor"),
        P("replica", "fsdp", "tensor"),
        P(("fsdp", "replica"), "tensor"),
        P(("fsdp", "replica"), "tensor"),
    )
    out_specs = (
        P(("fsdp", "replica"), "tensor"),
        P(("fsdp", "replica"), "tensor"),
        P(("replica", "fsdp"), "tensor"),
    )
    return jax.shard_map(body, mesh=mesh, in_specs=in_specs, out_specs=out_specs, check_vma=False)
```

```python
import jax
import jax.numpy as jnp
from jax import lax
from jax.experimental import pallas as pl
from jax.experimental.pallas import tpu as pltpu
from jax.sharding import PartitionSpec as P

MESH = pl.DeviceIdType.MESH
F32, BF16 = jnp.float32, jnp.bfloat16
D, KVW, BLOCK, TOK = 12288, 1024, 32, 384
ROWS = 192
FROWS = 768
SLAB = 48
OUTER_RATE = 0.7
MOMENTUM_COEF = 0.9
CLS = ((0, 256), (256, 384), (640, 384))
PARTS = (
    (0, 0, 128, ("x", "y", "z")),
    (0, 128, 128, ("y", "x", "z")),
    (1, 0, 128, ("z", "y", "x")),
    (2, 0, 128, ("z", "x", "y")),
    (2, 128, 256, ("x", "z", "y")),
    (1, 128, 256, ("y", "z", "x")),
)

DIRECT = 2
SCHEDULE = (
    ("S", "r", 0), ("S", "d", 0), ("S", "r", 1), ("S", "d", 1), ("S", "r", 2), ("S", "d", 2), ("D", "r", 0),
    ("S", "r", 3), ("D", "d", 0), ("S", "d", 3), ("D", "r", 1), ("D", "r", 2), ("S", "r", 4), ("W", "d", 0),
    ("W", "r", 0), ("E", 0), ("S", "1", 0), ("S", "2", 0, 0), ("D", "d", 1), ("D", "r", 3), ("W", "r", 2),
    ("S", "f", 2), ("D", "d", 2), ("S", "d", 4), ("W", "d", 1), ("W", "r", 1), ("E", 1), ("D", "1", 0),
    ("S", "2", 1, 0), ("D", "2", 0, 0), ("S", "1", 1), ("D", "d", 3), ("W", "r", 3), ("S", "f", 3), ("D", "r", 4),
    ("D", "f", 2), ("S", "r", 5), ("D", "2", 1, 0), ("W", "1", 0), ("S", "1h", 0), ("D", "1", 1), ("W", "2", 0, 0),
    ("S", "2h", 0, 0), ("S", "2", 0, 1), ("S", "2", 0, 2), ("D", "f", 3), ("W", "r", 4), ("S", "f", 4), ("W", "d", 2),
    ("W", "f", 2), ("E", 2), ("D", "1h", 0), ("W", "2", 1, 0), ("S", "2h", 1, 0), ("W", "1", 1), ("S", "2", 1, 1),
    ("D", "2h", 0, 0), ("S", "1h", 1), ("S", "2", 1, 2), ("W", "1h", 0), ("S", "2", 0, 3), ("S", "d", 5),
    ("S", "2", 2, 0), ("D", "r", 5), ("S", "1", 2), ("D", "2h", 1, 0), ("S", "3", 2, 0), ("W", "d", 3), ("W", "f", 3),
    ("E", 3), ("S", "2", 3, 0), ("D", "d", 4), ("S", "1", 3), ("D", "2", 0, 1), ("D", "2", 0, 2), ("S", "3", 3, 0),
    ("D", "1h", 1), ("W", "2", 0, 1), ("S", "2h", 0, 1), ("C", "tk", 0), ("W", "2", 0, 2), ("S", "2h", 0, 2),
    ("D", "f", 4), ("W", "r", 5), ("S", "f", 5), ("D", "2", 1, 1), ("D", "2", 1, 2), ("W", "1h", 1), ("S", "2", 1, 3),
    ("W", "d", 4), ("W", "f", 4), ("E", 4), ("D", "3", 2, 0), ("D", "2", 3, 0), ("S", "1", 4), ("D", "1", 2),
    ("D", "1", 3), ("S", "2", 4, 0), ("D", "2", 1, 3), ("W", "2", 1, 1), ("S", "2h", 1, 1), ("D", "2", 0, 3),
    ("D", "2", 2, 0), ("D", "2h", 0, 1), ("D", "2h", 0, 2), ("D", "3", 3, 0), ("W", "2", 0, 3), ("S", "2h", 0, 3),
    ("W", "2", 2, 0), ("S", "2h", 2, 0), ("W", "1", 2), ("S", "2", 2, 1), ("W", "2", 1, 2), ("S", "2h", 1, 2),
    ("D", "2h", 0, 3), ("S", "2", 2, 2), ("D", "2h", 1, 1), ("W", "2", 1, 3), ("S", "2h", 1, 3), ("D", "f", 5),
    ("D", "d", 5), ("S", "1h", 2), ("W", "2", 3, 0), ("S", "2h", 3, 0), ("W", "1", 3), ("S", "1h", 3),
    ("S", "2", 3, 1), ("S", "2", 3, 2), ("D", "2h", 2, 0), ("S", "3", 4, 0), ("S", "3", 0, 0), ("S", "3", 1, 0),
    ("W", "d", 5), ("W", "f", 5), ("E", 5), ("D", "2", 2, 1), ("D", "2", 2, 2), ("S", "1", 5), ("D", "1h", 2),
    ("D", "1h", 3), ("S", "2", 5, 0), ("D", "2h", 1, 2), ("D", "2h", 1, 3), ("D", "2h", 3, 0), ("S", "3", 5, 0),
    ("C", "tk", 1), ("W", "1h", 2), ("S", "2", 2, 3), ("C", "tk", 2), ("W", "2", 2, 1), ("S", "2h", 2, 1),
    ("C", "tk", 3), ("D", "1", 4), ("W", "1h", 3), ("S", "2", 3, 3), ("W", "2", 2, 2), ("S", "2h", 2, 2),
    ("D", "2", 4, 0), ("S", "3", 0, 1), ("C", "tk", 4), ("D", "2", 3, 1), ("S", "3", 2, 1), ("D", "3", 0, 0),
    ("D", "3", 1, 0), ("S", "3", 1, 1), ("D", "2", 3, 2), ("W", "1", 4), ("S", "1h", 4), ("W", "2", 4, 0),
    ("S", "2h", 4, 0), ("S", "3", 3, 1), ("S", "2", 4, 1), ("C", "tk", 5), ("W", "2", 3, 1), ("S", "2h", 3, 1),
    ("W", "2", 3, 2), ("S", "2h", 3, 2), ("D", "2h", 2, 1), ("S", "3", 4, 1), ("S", "2", 4, 2), ("S", "3", 2, 2),
    ("C", "tk", 6), ("D", "2h", 2, 2), ("D", "3", 4, 0), ("D", "2", 2, 3), ("S", "3", 3, 2), ("D", "2", 3, 3),
    ("S", "3", 2, 3), ("W", "2", 2, 3), ("S", "2h", 2, 3), ("D", "2h", 3, 1), ("W", "2", 3, 3), ("S", "2h", 3, 3),
    ("C", "tk", 7), ("D", "3", 3, 1), ("D", "1", 5), ("S", "3", 4, 2), ("D", "2h", 3, 2), ("D", "3", 2, 1),
    ("S", "3", 2, 4), ("D", "3", 0, 1), ("D", "3", 1, 1), ("D", "2h", 4, 0), ("D", "2", 5, 0), ("S", "3", 0, 2),
    ("W", "1", 5), ("S", "2", 5, 1), ("D", "2h", 2, 3), ("S", "1h", 5), ("W", "1h", 4), ("S", "2", 4, 3),
    ("D", "3", 3, 2), ("S", "3", 3, 3), ("W", "2h", 4, 0), ("S", "3", 4, 3), ("C", "sq", 0), ("D", "2", 4, 1),
    ("W", "2", 5, 0), ("S", "2h", 5, 0), ("D", "1h", 4), ("D", "3", 5, 0), ("D", "2h", 3, 3), ("D", "3", 2, 2),
    ("D", "3", 2, 3), ("S", "3", 5, 1), ("C", "sq", 1), ("D", "3", 0, 2), ("D", "2", 4, 2), ("W", "2", 4, 1),
    ("S", "2h", 4, 1), ("D", "3", 4, 1), ("D", "1h", 5), ("S", "3", 3, 4), ("S", "2", 5, 2), ("S", "3", 5, 2),
    ("C", "sq", 2), ("D", "3", 2, 4), ("S", "3", 2, 5), ("W", "2", 4, 2), ("S", "2h", 4, 2), ("W", "1h", 5),
    ("S", "2", 5, 3), ("D", "3", 3, 3), ("D", "3", 4, 2), ("D", "3", 4, 3), ("S", "3", 3, 5), ("W", "3", 3, 0),
    ("W", "3", 3, 1), ("W", "3", 3, 2), ("W", "3", 3, 3), ("W", "3", 4, 0), ("W", "3", 4, 1), ("W", "3", 4, 2),
    ("W", "3", 4, 3), ("C", "mm", 2, 0, "near"), ("D", "2h", 5, 0), ("D", "2", 5, 1), ("D", "2h", 4, 1),
    ("D", "2", 4, 3), ("D", "2h", 4, 2), ("W", "2", 5, 1), ("S", "2h", 5, 1), ("W", "2", 4, 3), ("S", "2h", 4, 3),
    ("D", "3", 5, 1), ("D", "3", 5, 2), ("W", "2h", 5, 0), ("S", "3", 5, 3), ("D", "3", 3, 4), ("W", "2h", 4, 1),
    ("S", "3", 4, 4), ("W", "2h", 2, 0), ("W", "2h", 2, 1), ("W", "2h", 2, 2), ("W", "2h", 2, 3), ("S", "3", 2, 6),
    ("S", "3", 1, 2), ("D", "2", 5, 2), ("S", "3", 0, 3), ("W", "2", 5, 2), ("S", "2h", 5, 2), ("S", "3", 1, 3),
    ("D", "3", 2, 5), ("D", "3", 5, 3), ("W", "3", 2, 0), ("W", "3", 2, 1), ("W", "3", 2, 2), ("W", "3", 2, 3),
    ("S", "3h", 2, 0), ("D", "2", 5, 3), ("D", "2h", 5, 1), ("D", "2h", 4, 3), ("S", "3", 0, 4), ("W", "2h", 5, 1),
    ("S", "3", 5, 4), ("W", "3", 5, 0), ("W", "3", 5, 1), ("W", "3", 5, 2), ("W", "3", 5, 3),
    ("C", "mm", 1, 0, "near"), ("D", "3", 1, 2), ("D", "3", 0, 3), ("D", "2h", 5, 2), ("D", "3", 1, 3),
    ("W", "2", 5, 3), ("S", "2h", 5, 3), ("D", "3", 3, 5), ("W", "2h", 4, 2), ("S", "3", 4, 5), ("S", "3", 1, 4),
    ("W", "3", 3, 4), ("W", "3", 4, 4), ("C", "mm", 2, 1, "near"), ("D", "2h", 5, 3), ("D", "3", 0, 4),
    ("S", "3", 0, 5), ("D", "3", 2, 6), ("D", "3h", 2, 0), ("W", "2h", 5, 2), ("S", "3", 5, 5), ("D", "3", 4, 4),
    ("W", "2h", 3, 0), ("W", "2h", 3, 1), ("W", "2h", 3, 2), ("W", "2h", 3, 3), ("S", "3", 3, 6), ("D", "3", 1, 4),
    ("S", "3", 1, 5), ("W", "3", 2, 4), ("W", "3", 5, 4), ("C", "mm", 1, 1, "near"), ("D", "3", 4, 5),
    ("W", "2h", 4, 3), ("S", "3", 4, 6), ("W", "2h", 0, 0), ("W", "2h", 0, 1), ("W", "2h", 0, 2), ("W", "2h", 0, 3),
    ("S", "3", 0, 6), ("D", "3", 5, 4), ("W", "2h", 5, 3), ("S", "3", 5, 6), ("W", "3", 3, 5), ("W", "3", 4, 5),
    ("C", "mm", 2, 2, "near"), ("D", "3", 0, 5), ("W", "2h", 1, 0), ("W", "2h", 1, 1), ("W", "2h", 1, 2),
    ("W", "2h", 1, 3), ("S", "3", 1, 6), ("D", "3", 3, 6), ("S", "3h", 3, 0), ("W", "3", 2, 5), ("W", "3", 5, 5),
    ("C", "mm", 1, 2, "near"), ("D", "3", 1, 5), ("D", "3", 0, 6), ("W", "3", 0, 0), ("W", "3", 0, 1),
    ("W", "3", 0, 2), ("W", "3", 0, 3), ("S", "3h", 0, 0), ("S", "3h", 4, 0), ("D", "3", 5, 5), ("S", "3h", 5, 0),
    ("W", "3", 1, 0), ("W", "3", 1, 1), ("W", "3", 1, 2), ("W", "3", 1, 3), ("S", "3h", 1, 0), ("W", "3", 0, 4),
    ("S", "3h", 0, 1), ("D", "3", 4, 6), ("D", "3h", 3, 0), ("S", "3h", 3, 1), ("D", "3", 5, 6), ("S", "3h", 2, 1),
    ("W", "3", 3, 6), ("W", "3", 4, 6), ("C", "mm", 2, 3, "near"), ("D", "3", 1, 6), ("D", "3h", 0, 0),
    ("W", "3", 1, 4), ("S", "3h", 1, 1), ("S", "3h", 4, 1), ("S", "3h", 5, 1), ("W", "3", 2, 6), ("W", "3", 5, 6),
    ("C", "mm", 1, 3, "near"), ("D", "3h", 1, 0), ("D", "3h", 0, 1), ("W", "3", 0, 5), ("S", "3h", 0, 2),
    ("W", "3h", 0, 0), ("W", "3h", 1, 0), ("C", "mm", 0, 0, "all"), ("W", "3", 1, 5), ("S", "3h", 1, 2),
    ("D", "3h", 4, 0), ("D", "3h", 3, 1), ("S", "3h", 3, 2), ("D", "3h", 5, 0), ("D", "3h", 2, 1), ("S", "3h", 2, 2),
    ("W", "3h", 2, 0), ("W", "3h", 5, 0), ("C", "mm", 1, 0, "far"), ("W", "3h", 3, 0), ("W", "3h", 4, 0),
    ("C", "mm", 2, 0, "far"), ("D", "3h", 1, 1), ("W", "3", 0, 6), ("S", "3h", 0, 3), ("S", "3h", 4, 2),
    ("S", "3h", 5, 2), ("W", "3h", 0, 1), ("W", "3h", 1, 1), ("C", "mm", 0, 1, "all"), ("D", "3h", 0, 2),
    ("W", "3", 1, 6), ("S", "3h", 1, 3), ("W", "3h", 3, 1), ("W", "3h", 4, 1), ("C", "mm", 2, 1, "far"),
    ("D", "3h", 4, 1), ("D", "3h", 3, 2), ("S", "3h", 3, 3), ("D", "3h", 5, 1), ("D", "3h", 2, 2), ("S", "3h", 2, 3),
    ("W", "3h", 2, 1), ("W", "3h", 5, 1), ("C", "mm", 1, 1, "far"), ("S", "3h", 4, 3), ("W", "3h", 0, 2),
    ("W", "3h", 1, 2), ("C", "mm", 0, 2, "all"), ("S", "3h", 5, 3), ("W", "3h", 0, 3), ("W", "3h", 1, 3),
    ("C", "mm", 0, 3, "all"), ("W", "3h", 2, 2), ("W", "3h", 5, 2), ("C", "mm", 1, 2, "far"), ("W", "3h", 3, 2),
    ("W", "3h", 4, 2), ("C", "mm", 2, 2, "far"), ("C", "fin", 0), ("W", "3h", 3, 3), ("W", "3h", 4, 3),
    ("C", "mm", 2, 3, "far"), ("W", "3h", 2, 3), ("W", "3h", 5, 3), ("C", "mm", 1, 3, "far"), ("C", "fin", 1),
    ("C", "fin", 2),
)

THRESH = ((0.25, 0.5), (0.75, 1.0), (1.25, 1.5), (1.75, 2.0), (2.5, 3.0), (3.5, 4.0), (5.0, 6.0))


def mod4(v):
    return lax.rem(v + 8, 4)


def kernel(
    tokens, gain, frag, exps, base, mom,
    nb, nm, kv,
    w0, w1, w2, tok, acc, fv, fb, rl, bs, ms, gb, gf, gn, ex, eb, er, erl, sc, iv, ss,
    loc, a_snd, a_rcv, e_snd, e_rcv, t_snd, t_rcv, g_snd, g_rcv,
):
    W = (w0, w1, w2)
    rep = lax.axis_index("replica")
    fs = lax.axis_index("fsdp")
    core = lax.axis_index("tensor")
    pos = {"x": lax.rem(fs, 4), "y": lax.div(fs, 4), "z": rep}

    def nbr(axis, step):
        c = dict(pos)
        c[axis] = mod4(pos[axis] + step)
        return (c["z"], c["y"] * 4 + c["x"], core)

    other = (rep, fs, 1 - core)

    def remote(src, dst, ss_, rs_, dev):
        return pltpu.make_async_remote_copy(
            src_ref=src, dst_ref=dst, send_sem=ss_, recv_sem=rs_, device_id=dev, device_id_type=MESH
        )

    seen = set()

    def once(name):
        new = name not in seen
        seen.add(name)
        return new

    pending = []

    def go(copy):
        copy.start()
        pending.append(copy)

    barrier = pltpu.get_barrier_semaphore()
    peers = [nbr(a, s) for a in "xyz" for s in (1, -1)] + [nbr("z", 2), other]
    for p in peers:
        pl.semaphore_signal(barrier, inc=1, device_id=p, device_id_type=MESH)

    l_ex = pltpu.make_async_copy(exps, ex, loc.at[0])
    l_ex.start()
    l_fr = pltpu.make_async_copy(frag, fv, loc.at[1])
    l_fr.start()
    l_bs = pltpu.make_async_copy(base, bs, loc.at[2])
    l_bs.start()
    l_ms = pltpu.make_async_copy(mom, ms, loc.at[3])
    l_ms.start()
    l_gn = pltpu.make_async_copy(gain, gb, loc.at[4])
    l_gn.start()

    pl.semaphore_wait(barrier, len(peers))
    l_fr.wait()

    up, down = nbr("z", 1), nbr("z", -1)
    zu, zd, zo = mod4(rep + 1), mod4(rep - 1), mod4(rep + 2)

    def window(d):
        return eb.at[:, pl.ds(pl.multiple_of(128 * lax.div(3 * d, 2), 128), 256)]

    off = 64 * lax.rem(rep, 2)

    def expand(lo, width):
        j = lax.broadcasted_iota(jnp.int32, (BLOCK, width), 0)
        n = lax.broadcasted_iota(jnp.int32, (BLOCK, width), 1)
        pick = jnp.where(j == lax.div(n + lo, BLOCK), 1.0, 0.0).astype(BF16)
        for slot in range(4):
            if slot == 3 and once("far exponents"):
                e_cp[3].wait_recv()
            e = (window(rep)[...] if slot == 0 else er[slot]).astype(F32)
            for ref, sign in ((sc, 1.0), (iv, -1.0)):
                small = jnp.exp2(sign * e).astype(BF16)
                full = lax.dot_general(small, pick, (((0,), (0,)), ((), ())), preferred_element_type=F32)
                ref[slot, :, pl.ds(lo, width)] = full.astype(BF16)

    e_cp = [
        remote(window(zo), erl, e_snd.at[0], e_rcv.at[0], up),
        remote(window(zu), er.at[1], e_snd.at[1], e_rcv.at[1], up),
        remote(window(zd), er.at[2], e_snd.at[2], e_rcv.at[2], down),
        remote(erl, er.at[3], e_snd.at[3], e_rcv.at[3], up),
    ]

    def cols(p):
        c, lo, width, _ = PARTS[p]
        return pl.ds(CLS[c][0] + lo, width)

    H = ROWS // 2

    def a2a(p):
        k = 6 * p
        cc = cols(p)
        return [
            remote(fv.at[zo, pl.ds(0, H), cc], rl.at[0, :, cc], a_snd.at[k], a_rcv.at[k], up),
            remote(fv.at[zo, pl.ds(H, H), cc], rl.at[1, :, cc], a_snd.at[k + 1], a_rcv.at[k + 1], down),
            remote(fv.at[zu, :, cc], fb.at[1, :, cc], a_snd.at[k + 2], a_rcv.at[k + 2], up),
            remote(fv.at[zd, :, cc], fb.at[2, :, cc], a_snd.at[k + 3], a_rcv.at[k + 3], down),
            remote(rl.at[0, :, cc], fb.at[3, pl.ds(0, H), cc], a_snd.at[k + 4], a_rcv.at[k + 4], up),
            remote(rl.at[1, :, cc], fb.at[3, pl.ds(H, H), cc], a_snd.at[k + 5], a_rcv.at[k + 5], down),
        ]

    mine = pl.ds(pl.multiple_of(core * TOK, TOK), TOK)
    t_cp, l_tk = [], []
    for i in range(8):
        src = tokens.at[pl.ds(i * SLAB, SLAB), :]
        dst = tok.at[pl.ds(pl.multiple_of(core * TOK + i * SLAB, SLAB), SLAB), :]
        t_cp.append(remote(src, dst, t_snd.at[i], t_rcv.at[i], other))
        l_tk.append(pltpu.make_async_copy(src, dst, loc.at[5 + i]))

    def early():
        l_ex.wait()
        eb[...] = ex[...].astype(F32).astype(BF16)
        for m in e_cp[:3]:
            go(m)
        l_gn.wait()
        gf[...] = gb[...].astype(F32)
        first = 6 * fs + lax.div(3 * rep, 2)
        i = lax.broadcasted_iota(jnp.int32, (128, 128), 0)
        l = lax.broadcasted_iota(jnp.int32, (128, 128), 1)
        for h in range(2):
            row = jnp.broadcast_to(gf[pl.ds(first + h, 1), :], (128, 128))
            column = jnp.sum(jnp.where(i == l, row, 0.0), axis=1, keepdims=True)
            gn[pl.ds(128 * h, 128), :] = jnp.broadcast_to(column, (128, 128))
        e_cp[0].wait_recv()
        go(e_cp[3])

    def prepare():
        for s in (1, 2):
            e_cp[s].wait_recv()
        l_bs.wait()
        l_ms.wait()

    def encode(p):
        c, sub, width, _ = PARTS[p]
        lo = CLS[c][0] + sub
        row0 = pl.multiple_of(rep * ROWS, ROWS)

        def step(t, carry):
            rr = pl.ds(pl.multiple_of(t * SLAB, SLAB), SLAB)
            wr = pl.ds(pl.multiple_of(row0 + t * SLAB, SLAB), SLAB)
            fr = pl.ds(pl.multiple_of(off + t * SLAB, 16), SLAB)
            g = gn[fr, :]
            for k in range(width // 128):
                cc = pl.ds(lo + 128 * k, 128)
                b = bs[rr, cc]
                total = jnp.zeros((SLAB, 128), F32)
                for s in range(4):
                    v = (b - (fv[rep, rr, cc] if s == 0 else fb[s, rr, cc]).astype(F32)) * iv[s, fr, cc].astype(F32)
                    m = jnp.abs(v)
                    level = jnp.zeros_like(m)
                    for mid, val in THRESH:
                        level = jnp.where(m >= mid, val, level)
                    total = total + jnp.where(v < 0.0, -level, level) * sc[s, fr, cc].astype(F32)
                grad = total * 0.25
                moment = MOMENTUM_COEF * ms[rr, cc] + grad
                new = b - OUTER_RATE * (grad + MOMENTUM_COEF * moment)
                nm[rr, cc] = moment
                nb[rr, cc] = new
                W[c][pos["y"], pos["x"], wr, pl.ds(sub + 128 * k, 128)] = (new * g).astype(BF16)
            return carry

        lax.fori_loop(0, ROWS // SLAB, step, 0)

    def place(p, **at):
        half = at.pop("half", None)
        xs, ys = at.get("x", slice(None)), at.get("y", slice(None))
        if "z" in at:
            r0, n = at["z"] * ROWS, ROWS
        else:
            r0, n = 0, FROWS
        if half is not None:
            n = n // 2
            r0 = r0 + half * n
        if not isinstance(r0, int):
            r0 = pl.multiple_of(r0, 96)
        c, lo, width, _ = PARTS[p]
        return W[c].at[ys, xs, pl.ds(r0, n), pl.ds(lo, width)]

    M = {}
    OFF = (0, 1, -1, 2)
    used = [0]

    def both(*pair):
        out = []
        for j, s in enumerate((1, -1)):
            axis, ref = pair[j]
            out.append(remote(ref, ref, g_snd.at[used[0]], g_rcv.at[used[0]], nbr(axis, s)))
            used[0] += 1
        return out

    def full(p, axis, **fixed):
        here = place(p, **fixed, **{axis: pos[axis]})
        return both((axis, here), (axis, here))

    def half(p, axis, **fixed):
        return both(
            *[(axis, place(p, **fixed, **{axis: mod4(pos[axis] - s), "half": j})) for j, s in enumerate((1, -1))]
        )

    for p in range(len(PARTS)):
        m = a2a(p)
        M["r", p], M["d", p], M["f", p] = m[:2], m[2:4], m[4:]
        if p < DIRECT:
            far = remote(fv.at[zo, :, cols(p)], fb.at[3, :, cols(p)], a_snd.at[6 * p], a_rcv.at[6 * p], nbr("z", 2))
            M["r", p] = [far]
        a, b, l = PARTS[p][3]
        R, S = (a, b) if b == "z" else (b, a)
        at = {b: pos[b], l: pos[l]}
        M["1", p], M["1h", p] = full(p, a, **at), half(p, a, **at)
        for i in range(4):
            at = {a: mod4(pos[a] + OFF[i]), l: pos[l]}
            M["2", p, i], M["2h", p, i] = full(p, b, **at), half(p, b, **at)
            M["3", p, i] = full(p, l, **{R: pos[R], S: mod4(pos[S] + OFF[i])})
            M["3h", p, i] = half(p, l, **{R: mod4(pos[R] + OFF[i])})
            if i:
                M["3", p, 3 + i] = full(p, l, **{R: mod4(pos[R] + OFF[i])})

    def mm(c, count, coords):
        lo, width = CLS[c]
        cc = pl.ds(lo, width)

        def chunk(t, carry):
            yy, xx = coords(t)
            kk = pl.ds(pl.multiple_of((yy * 4 + xx) * FROWS, FROWS), FROWS)

            def block(m, carry):
                mr = pl.ds(pl.multiple_of(m * TOK, TOK), TOK)
                acc[mr, cc] += jnp.dot(tok[mr, kk], W[c][yy, xx], preferred_element_type=F32)
                return carry

            return lax.fori_loop(0, 2, block, carry)

        lax.fori_loop(0, count, chunk, 0)

    def offset(i):
        return i + lax.div(i, 2) - 2 * lax.div(i, 3)

    def mm_near(c, i):
        if c == 1:
            yy = mod4(pos["y"] + OFF[i])
            mm(c, 3, lambda t: (yy, mod4(pos["x"] + offset(t))))
        else:
            xx = mod4(pos["x"] + OFF[i])
            mm(c, 3, lambda t: (mod4(pos["y"] + offset(t)), xx))

    def mm_far(c, i):
        if c == 1:
            mm(c, 1, lambda t: (mod4(pos["y"] + OFF[i]), mod4(pos["x"] + 2)))
        else:
            mm(c, 1, lambda t: (mod4(pos["y"] + 2), mod4(pos["x"] + OFF[i])))

    same = len({p[3] for p in PARTS if p[0] == 0}) == 1

    def mm_row(c, i):
        by_y = PARTS[[p[0] for p in PARTS].index(0)][3][1] == "y"
        at = mod4(pos["y" if by_y else "x"] + OFF[i])
        mm(c, 4, (lambda t: (at, t)) if by_y else (lambda t: (t, at)))

    def mm_level(c, i):
        def coords(t):
            turn = lax.div(t, i + 1)
            iy = i * (1 - turn) + (t - i - 1) * turn
            ix = t * (1 - turn) + i * turn
            return mod4(pos["y"] + offset(iy)), mod4(pos["x"] + offset(ix))

        mm(c, 2 * i + 1, coords)

    def squares(i):
        rr = pl.ds(pl.multiple_of(core * TOK + i * 128, 128), 128)

        def step(t, s):
            for k in range(4):
                v = tok[rr, pl.ds(pl.multiple_of(t * 512 + k * 128, 128), 128)].astype(F32)
                s = s + v * v
            return s

        s = lax.fori_loop(0, D // 512, step, jnp.zeros((128, 128), F32))
        mean = jnp.sum(s, axis=1, keepdims=True) * (1.0 / D)
        ss[rr, :] = jnp.broadcast_to(lax.rsqrt(mean + 1e-05) * (D ** -0.5), (128, 128))

    def finish(c):
        lo, width = CLS[c]

        def scale(m, carry):
            mr = pl.ds(pl.multiple_of(m * 64, 64), 64)
            for k in range(width // 128):
                at = pl.ds(lo + 128 * k, 128)
                kv[mr, at] = (acc[mr, at] * ss[mr, :]).astype(BF16)
            return carry

        lax.fori_loop(0, 2 * TOK // 64, scale, 0)

    s_cp = remote(ss.at[mine, :], ss.at[mine, :], t_snd.at[8], t_rcv.at[8], other)
    left = []
    for kind, *key in SCHEDULE:
        key = tuple(key)
        if kind == "S":
            for m in M[key]:
                m.start()
            left.append(key)
        elif kind == "W":
            if once("wait"):
                early()
            if key[0] == "d":
                if once("prepare"):
                    prepare()
                c = PARTS[key[1]][0]
                if once(("factors", c)):
                    expand(*CLS[c])
            for m in M[key]:
                m.wait_recv()
        elif kind == "D":
            for m in M[key]:
                m.wait_send()
            left.remove(key)
        elif kind == "E":
            encode(*key)
        elif key[0] == "tk":
            l_tk[key[1]].start()
            go(t_cp[key[1]])
            if once("total"):
                acc[...] = jnp.zeros_like(acc)
        elif key[0] == "sq":
            if once("own tokens"):
                for t in l_tk:
                    t.wait()
            squares(key[1])
            if key[1] == 2:
                go(s_cp)
        elif key[0] == "fin":
            if once("factors"):
                s_cp.wait_recv()
            finish(key[1])
        else:
            if once("all tokens"):
                for t in t_cp:
                    t.wait_recv()
            {"near": mm_near, "far": mm_far, "all": mm_row if same else mm_level}[key[3]](key[1], key[2])
    for key in left:
        for m in M[key]:
            m.wait_send()

    for p in pending:
        p.wait_send()


def body(tokens, norm_gain, fragment, exponents, base_weight, momentum):
    any_ = pl.BlockSpec(memory_space=pl.ANY)
    dma = pltpu.SemaphoreType.DMA
    vm = pltpu.VMEM
    return pl.pallas_call(
        kernel,
        out_shape=(vm((ROWS, KVW), F32), vm((ROWS, KVW), F32), vm((2 * TOK, KVW), BF16)),
        in_specs=[any_] * 6,
        out_specs=[pl.BlockSpec(memory_space=vm)] * 3,
        scratch_shapes=[
            *[vm((4, 4, FROWS, width), BF16) for _, width in CLS],
            vm((2 * TOK, D), BF16),
            vm((2 * TOK, KVW), F32),
            vm((4, ROWS, KVW), BF16),
            vm((4, ROWS, KVW), BF16),
            vm((2, ROWS // 2, KVW), BF16),
            vm((ROWS, KVW), F32),
            vm((ROWS, KVW), F32),
            vm((D // 128, 128), BF16),
            vm((D // 128, 128), F32),
            vm((256, 128), F32),
            vm((BLOCK, 4 * ROWS), jnp.int32),
            vm((BLOCK, 4 * ROWS), BF16),
            vm((4, BLOCK, 256), BF16),
            vm((BLOCK, 256), BF16),
            vm((4, 256, KVW), BF16),
            vm((4, 256, KVW), BF16),
            vm((2 * TOK, 128), F32),
            dma((13,)),
            dma((6 * len(PARTS),)),
            dma((6 * len(PARTS),)),
            dma((4,)),
            dma((4,)),
            dma((9,)),
            dma((9,)),
            dma((42 * len(PARTS),)),
            dma((42 * len(PARTS),)),
        ],
        compiler_params=pltpu.CompilerParams(
            collective_id=0, has_side_effects=True, vmem_limit_bytes=59 * 1024 * 1024
        ),
        cost_estimate=pl.CostEstimate(flops=2 * 768 * 12288 * 1024, bytes_accessed=30_000_000, transcendentals=0),
    )(
        tokens,
        norm_gain.reshape(D // 128, 128),
        fragment.reshape(4, ROWS, KVW),
        exponents[0].T,
        base_weight,
        momentum,
    )


def solution(mesh):
    in_specs = (
        P(("replica", "fsdp", "tensor"), None),
        P(),
        P("replica", "fsdp", "tensor"),
        P("replica", "fsdp", "tensor"),
        P(("fsdp", "replica"), "tensor"),
        P(("fsdp", "replica"), "tensor"),
    )
    out_specs = (
        P(("fsdp", "replica"), "tensor"),
        P(("fsdp", "replica"), "tensor"),
        P(("replica", "fsdp"), "tensor"),
    )
    return jax.shard_map(body, mesh=mesh, in_specs=in_specs, out_specs=out_specs, check_vma=False)
```

```python
import jax
import jax.numpy as jnp
from jax import lax
from jax.experimental import pallas as pl
from jax.experimental.pallas import tpu as pltpu
from jax.sharding import PartitionSpec as P

MESH = pl.DeviceIdType.MESH
F32, BF16 = jnp.float32, jnp.bfloat16
D, KVW, BLOCK, TOK = 12288, 1024, 32, 384
ROWS = 192
FROWS = 768
SLAB = 48
OUTER_RATE = 0.7
MOMENTUM_COEF = 0.9
CLS = ((0, 256), (256, 384), (640, 384))
PARTS = (
    (0, 0, 128, ("x", "y", "z")),
    (0, 128, 128, ("y", "x", "z")),
    (1, 0, 128, ("z", "y", "x")),
    (2, 0, 128, ("z", "x", "y")),
    (1, 128, 256, ("y", "z", "x")),
    (2, 128, 256, ("x", "z", "y")),
)

DIRECT = 2
SCHEDULE = (
    ("S", "r", 0), ("S", "d", 0), ("S", "r", 1), ("D", "r", 0), ("S", "d", 1), ("D", "d", 0), ("S", "r", 2),
    ("W", "d", 0), ("W", "r", 0), ("E", 0), ("S", "1", 0), ("S", "2", 0, 0), ("D", "r", 1), ("D", "d", 1),
    ("D", "r", 2), ("S", "d", 2), ("S", "r", 3), ("W", "d", 1), ("W", "r", 1), ("E", 1), ("D", "1", 0),
    ("S", "2", 1, 0), ("D", "2", 0, 0), ("S", "1", 1), ("W", "r", 2), ("S", "f", 2), ("D", "d", 2), ("D", "r", 3),
    ("S", "d", 3), ("W", "1", 0), ("S", "1h", 0), ("W", "2", 0, 0), ("S", "2h", 0, 0), ("S", "2", 0, 1),
    ("S", "2", 0, 2), ("D", "f", 2), ("W", "r", 3), ("S", "f", 3), ("S", "r", 4), ("W", "d", 2), ("W", "f", 2),
    ("E", 2), ("D", "2", 1, 0), ("D", "1h", 0), ("W", "2", 1, 0), ("S", "2h", 1, 0), ("D", "d", 3), ("D", "f", 3),
    ("S", "d", 4), ("W", "1", 1), ("S", "2", 1, 1), ("D", "1", 1), ("D", "2h", 0, 0), ("S", "1h", 1), ("W", "1h", 0),
    ("S", "2", 0, 3), ("D", "2h", 1, 0), ("S", "2", 1, 2), ("D", "2", 0, 1), ("D", "2", 0, 2), ("S", "2", 2, 0),
    ("S", "3", 2, 0), ("W", "d", 3), ("W", "f", 3), ("E", 3), ("D", "r", 4), ("W", "r", 4), ("S", "f", 4),
    ("D", "1h", 1), ("W", "2", 0, 1), ("S", "2h", 0, 1), ("D", "2", 1, 1), ("S", "2", 3, 0), ("W", "2", 0, 2),
    ("S", "2h", 0, 2), ("S", "3", 3, 0), ("D", "d", 4), ("S", "r", 5), ("W", "1h", 1), ("S", "2", 1, 3),
    ("W", "2", 1, 1), ("S", "2h", 1, 1), ("S", "d", 5), ("D", "f", 4), ("S", "1", 2), ("S", "1", 3), ("W", "d", 4),
    ("W", "f", 4), ("E", 4), ("D", "2", 0, 3), ("D", "2h", 0, 1), ("D", "2", 2, 0), ("D", "2h", 0, 2),
    ("D", "3", 3, 0), ("S", "1", 4), ("D", "2", 1, 2), ("D", "3", 2, 0), ("D", "2h", 1, 1), ("D", "2", 3, 0),
    ("D", "2", 1, 3), ("W", "2", 1, 2), ("S", "2h", 1, 2), ("W", "2", 0, 3), ("S", "2h", 0, 3), ("W", "2", 2, 0),
    ("S", "2h", 2, 0), ("D", "2h", 1, 2), ("W", "2", 3, 0), ("S", "2h", 3, 0), ("W", "2", 1, 3), ("S", "2h", 1, 3),
    ("S", "3", 4, 0), ("C", "tk", 0), ("C", "tk", 1), ("D", "r", 5), ("D", "1", 2), ("D", "1", 3), ("W", "r", 5),
    ("S", "f", 5), ("S", "2", 4, 0), ("D", "2h", 0, 3), ("D", "2h", 2, 0), ("W", "1", 2), ("S", "2", 2, 1),
    ("S", "2", 2, 2), ("D", "2h", 3, 0), ("D", "2h", 1, 3), ("W", "1", 3), ("S", "2", 3, 1), ("S", "2", 3, 2),
    ("S", "1h", 2), ("D", "d", 5), ("S", "1h", 3), ("S", "3", 3, 1), ("C", "tk", 2), ("D", "1", 4), ("S", "3", 3, 2),
    ("S", "3", 2, 1), ("W", "1", 4), ("S", "2", 4, 1), ("S", "1h", 4), ("S", "2", 4, 2), ("S", "3", 2, 2),
    ("C", "tk", 3), ("W", "d", 5), ("W", "f", 5), ("E", 5), ("D", "2", 2, 1), ("D", "2", 2, 2), ("W", "2", 2, 1),
    ("S", "2h", 2, 1), ("D", "2", 3, 1), ("D", "3", 4, 0), ("D", "2", 3, 2), ("S", "1", 5), ("D", "3", 3, 1),
    ("W", "2", 2, 2), ("S", "2h", 2, 2), ("W", "1h", 2), ("S", "2", 2, 3), ("D", "3", 2, 1), ("W", "2", 3, 1),
    ("S", "2h", 3, 1), ("D", "f", 5), ("D", "1h", 2), ("D", "1h", 3), ("S", "2", 5, 0), ("D", "3", 2, 2),
    ("W", "2", 3, 2), ("S", "2h", 3, 2), ("W", "1h", 3), ("S", "2", 3, 3), ("D", "3", 3, 2), ("D", "1h", 4),
    ("S", "3", 5, 0), ("C", "tk", 4), ("D", "2", 4, 0), ("W", "1h", 4), ("S", "2", 4, 3), ("C", "tk", 5),
    ("W", "2", 4, 0), ("S", "2h", 4, 0), ("D", "2h", 2, 1), ("D", "2h", 2, 2), ("S", "3", 3, 3), ("D", "2h", 3, 1),
    ("S", "3", 4, 1), ("C", "tk", 6), ("D", "2", 2, 3), ("W", "2", 2, 3), ("S", "2h", 2, 3), ("D", "2h", 3, 2),
    ("S", "3", 4, 2), ("D", "2", 4, 1), ("D", "2", 4, 2), ("W", "2", 4, 1), ("S", "2h", 4, 1), ("D", "2", 3, 3),
    ("D", "1", 5), ("W", "2", 3, 3), ("S", "2h", 3, 3), ("W", "2", 4, 2), ("S", "2h", 4, 2), ("D", "3", 3, 3),
    ("D", "2h", 2, 3), ("D", "3", 5, 0), ("S", "3", 3, 4), ("C", "tk", 7), ("W", "1", 5), ("S", "1h", 5),
    ("S", "2", 5, 1), ("D", "2h", 4, 0), ("S", "2", 5, 2), ("D", "2h", 3, 3), ("S", "3", 2, 3), ("S", "3", 3, 5),
    ("W", "2h", 4, 0), ("S", "3", 4, 3), ("D", "2", 5, 0), ("W", "2", 5, 0), ("S", "2h", 5, 0), ("D", "3", 4, 1),
    ("D", "1h", 5), ("S", "3", 2, 4), ("D", "2h", 4, 1), ("W", "1h", 5), ("S", "2", 5, 3), ("D", "2h", 4, 2),
    ("D", "2", 4, 3), ("W", "2", 4, 3), ("S", "2h", 4, 3), ("D", "3", 3, 4), ("S", "3", 5, 1), ("D", "3", 4, 2),
    ("D", "3", 2, 3), ("S", "3", 5, 2), ("D", "3", 4, 3), ("W", "2h", 4, 1), ("S", "3", 4, 4), ("S", "3", 0, 0),
    ("W", "3", 2, 0), ("W", "3", 2, 1), ("W", "3", 2, 2), ("W", "3", 2, 3), ("W", "3", 4, 0), ("W", "3", 4, 1),
    ("W", "3", 4, 2), ("W", "3", 4, 3), ("C", "mm", 1, 0, "near"), ("D", "2h", 5, 0), ("D", "2", 5, 1),
    ("D", "2", 5, 2), ("D", "2h", 4, 3), ("W", "2", 5, 1), ("S", "2h", 5, 1), ("W", "2", 5, 2), ("S", "2h", 5, 2),
    ("D", "3", 3, 5), ("D", "3", 5, 1), ("D", "3", 5, 2), ("W", "2h", 5, 0), ("S", "3", 5, 3), ("C", "sq", 0),
    ("W", "2h", 3, 0), ("W", "2h", 3, 1), ("W", "2h", 3, 2), ("W", "2h", 3, 3), ("S", "3", 3, 6), ("D", "3", 0, 0),
    ("D", "2", 5, 3), ("S", "3", 1, 0), ("S", "3", 0, 1), ("W", "2", 5, 3), ("S", "2h", 5, 3), ("C", "sq", 1),
    ("C", "sq", 2), ("D", "2h", 5, 1), ("D", "2h", 5, 2), ("S", "3", 1, 1), ("D", "3", 2, 4), ("D", "3", 5, 3),
    ("W", "2h", 5, 1), ("S", "3", 5, 4), ("S", "3", 0, 2), ("S", "3", 2, 5), ("S", "3", 1, 2), ("W", "3", 3, 0),
    ("W", "3", 3, 1), ("W", "3", 3, 2), ("W", "3", 3, 3), ("W", "3", 5, 0), ("W", "3", 5, 1), ("W", "3", 5, 2),
    ("W", "3", 5, 3), ("C", "mm", 2, 0, "near"), ("D", "3", 1, 0), ("D", "3", 0, 1), ("D", "2h", 5, 3),
    ("S", "3", 0, 3), ("S", "3", 1, 3), ("D", "3", 1, 1), ("S", "3", 0, 4), ("D", "3", 4, 4), ("W", "2h", 4, 2),
    ("S", "3", 4, 5), ("W", "3", 2, 4), ("W", "3", 4, 4), ("C", "mm", 1, 1, "near"), ("D", "3", 3, 6),
    ("D", "3", 0, 2), ("D", "3", 1, 2), ("W", "2h", 5, 2), ("S", "3", 5, 5), ("D", "3", 0, 3), ("D", "3", 1, 3),
    ("W", "3", 0, 0), ("W", "3", 0, 1), ("W", "3", 0, 2), ("W", "3", 0, 3), ("S", "3h", 0, 0), ("D", "3", 2, 5),
    ("W", "3", 1, 0), ("W", "3", 1, 1), ("W", "3", 1, 2), ("W", "3", 1, 3), ("S", "3h", 1, 0), ("D", "3", 0, 4),
    ("S", "3", 1, 4), ("W", "2h", 2, 0), ("W", "2h", 2, 1), ("W", "2h", 2, 2), ("W", "2h", 2, 3), ("S", "3", 2, 6),
    ("W", "3", 3, 4), ("W", "3", 5, 4), ("C", "mm", 2, 1, "near"), ("D", "3", 5, 4), ("D", "3h", 0, 0),
    ("W", "2h", 5, 3), ("S", "3", 5, 6), ("D", "3h", 1, 0), ("W", "3", 0, 4), ("S", "3h", 0, 1), ("D", "3", 4, 5),
    ("W", "2h", 4, 3), ("S", "3", 4, 6), ("W", "3", 2, 5), ("W", "3", 4, 5), ("C", "mm", 1, 2, "near"),
    ("S", "3", 0, 5), ("W", "3h", 0, 0), ("W", "3h", 1, 0), ("C", "mm", 0, 0, "all"), ("W", "3", 3, 5),
    ("W", "3", 5, 5), ("C", "mm", 2, 2, "near"), ("D", "3", 1, 4), ("D", "3h", 0, 1), ("W", "3", 1, 4),
    ("S", "3h", 1, 1), ("D", "3", 2, 6), ("D", "3", 5, 5), ("S", "3h", 3, 0), ("S", "3", 1, 5), ("S", "3h", 2, 0),
    ("S", "3h", 5, 0), ("S", "3h", 4, 0), ("D", "3", 0, 5), ("D", "3h", 1, 1), ("W", "3", 0, 5), ("S", "3h", 0, 2),
    ("W", "3h", 0, 1), ("W", "3h", 1, 1), ("C", "mm", 0, 1, "all"), ("D", "3", 5, 6), ("D", "3h", 3, 0),
    ("S", "3h", 3, 1), ("W", "2h", 0, 0), ("W", "2h", 0, 1), ("W", "2h", 0, 2), ("W", "2h", 0, 3), ("S", "3", 0, 6),
    ("D", "3", 4, 6), ("D", "3h", 2, 0), ("S", "3h", 2, 1), ("W", "3", 2, 6), ("W", "3", 4, 6),
    ("C", "mm", 1, 3, "near"), ("S", "3h", 5, 1), ("S", "3h", 4, 1), ("W", "3", 3, 6), ("W", "3", 5, 6),
    ("C", "mm", 2, 3, "near"), ("D", "3", 1, 5), ("D", "3h", 0, 2), ("W", "3", 1, 5), ("S", "3h", 1, 2),
    ("W", "3h", 2, 0), ("W", "3h", 4, 0), ("C", "mm", 1, 0, "far"), ("D", "3h", 5, 0), ("D", "3h", 3, 1),
    ("S", "3h", 3, 2), ("D", "3", 0, 6), ("W", "2h", 1, 0), ("W", "2h", 1, 1), ("W", "2h", 1, 2), ("W", "2h", 1, 3),
    ("S", "3", 1, 6), ("D", "3h", 4, 0), ("D", "3h", 2, 1), ("S", "3h", 2, 2), ("W", "3h", 3, 0), ("W", "3h", 5, 0),
    ("C", "mm", 2, 0, "far"), ("S", "3h", 5, 2), ("S", "3h", 4, 2), ("W", "3h", 2, 1), ("W", "3h", 4, 1),
    ("C", "mm", 1, 1, "far"), ("D", "3h", 1, 2), ("W", "3", 0, 6), ("S", "3h", 0, 3), ("W", "3h", 0, 2),
    ("W", "3h", 1, 2), ("C", "mm", 0, 2, "all"), ("D", "3h", 5, 1), ("D", "3h", 3, 2), ("S", "3h", 3, 3),
    ("D", "3h", 4, 1), ("D", "3h", 2, 2), ("S", "3h", 2, 3), ("W", "3h", 3, 1), ("W", "3h", 5, 1),
    ("C", "mm", 2, 1, "far"), ("D", "3", 1, 6), ("D", "3h", 0, 3), ("W", "3", 1, 6), ("S", "3h", 1, 3),
    ("D", "3h", 5, 2), ("S", "3h", 5, 3), ("D", "3h", 4, 2), ("S", "3h", 4, 3), ("W", "3h", 2, 2), ("W", "3h", 4, 2),
    ("C", "mm", 1, 2, "far"), ("W", "3h", 3, 2), ("W", "3h", 5, 2), ("C", "mm", 2, 2, "far"), ("W", "3h", 0, 3),
    ("W", "3h", 1, 3), ("C", "mm", 0, 3, "all"), ("W", "3h", 2, 3), ("W", "3h", 4, 3), ("C", "mm", 1, 3, "far"),
    ("W", "3h", 3, 3), ("W", "3h", 5, 3), ("C", "mm", 2, 3, "far"), ("C", "fin", 1), ("C", "fin", 2), ("C", "fin", 0),
    ("D", "3h", 1, 3), ("D", "3h", 3, 3), ("D", "3h", 2, 3), ("D", "3h", 5, 3), ("D", "3h", 4, 3),
)

THRESH = ((0.25, 0.5), (0.75, 1.0), (1.25, 1.5), (1.75, 2.0), (2.5, 3.0), (3.5, 4.0), (5.0, 6.0))


def mod4(v):
    return lax.rem(v + 8, 4)


def kernel(
    tokens, gain, frag, exps, base, mom,
    nb, nm, kv,
    w0, w1, w2, tok, acc, fv, fb, rl, bs, ms, gb, gf, gn, ex, eb, er, sc, iv, ss,
    loc, a_snd, a_rcv, e_snd, e_rcv, t_snd, t_rcv, g_snd, g_rcv,
):
    W = (w0, w1, w2)
    rep = lax.axis_index("replica")
    fs = lax.axis_index("fsdp")
    core = lax.axis_index("tensor")
    pos = {"x": lax.rem(fs, 4), "y": lax.div(fs, 4), "z": rep}

    def nbr(axis, step):
        c = dict(pos)
        c[axis] = mod4(pos[axis] + step)
        return (c["z"], c["y"] * 4 + c["x"], core)

    other = (rep, fs, 1 - core)

    def remote(src, dst, ss_, rs_, dev):
        return pltpu.make_async_remote_copy(
            src_ref=src, dst_ref=dst, send_sem=ss_, recv_sem=rs_, device_id=dev, device_id_type=MESH
        )

    seen = set()

    def once(name):
        new = name not in seen
        seen.add(name)
        return new

    pending = []

    def go(copy):
        copy.start()
        pending.append(copy)

    barrier = pltpu.get_barrier_semaphore()
    peers = [nbr(a, s) for a in "xyz" for s in (1, -1)] + [nbr("z", 2), other]
    for p in peers:
        pl.semaphore_signal(barrier, inc=1, device_id=p, device_id_type=MESH)

    l_ex = pltpu.make_async_copy(exps, ex, loc.at[0])
    l_ex.start()
    l_fr = pltpu.make_async_copy(frag, fv, loc.at[1])
    l_fr.start()
    l_bs = pltpu.make_async_copy(base, bs, loc.at[2])
    l_bs.start()
    l_ms = pltpu.make_async_copy(mom, ms, loc.at[3])
    l_ms.start()
    l_gn = pltpu.make_async_copy(gain, gb, loc.at[4])
    l_gn.start()

    pl.semaphore_wait(barrier, len(peers))
    l_fr.wait()

    up, down = nbr("z", 1), nbr("z", -1)
    zu, zd, zo = mod4(rep + 1), mod4(rep - 1), mod4(rep + 2)

    def window(d):
        return eb.at[:, pl.ds(pl.multiple_of(128 * lax.div(3 * d, 2), 128), 256)]

    off = 64 * lax.rem(rep, 2)

    def expand(lo, width):
        j = lax.broadcasted_iota(jnp.int32, (BLOCK, width), 0)
        n = lax.broadcasted_iota(jnp.int32, (BLOCK, width), 1)
        pick = jnp.where(j == lax.div(n + lo, BLOCK), 1.0, 0.0).astype(BF16)
        for slot in range(4):
            if slot == 3 and once("far exponents"):
                e_cp[0].wait_recv()
            e = (window(rep)[...] if slot == 0 else er[slot]).astype(F32)
            for ref, sign in ((sc, 1.0), (iv, -1.0)):
                small = jnp.exp2(sign * e).astype(BF16)
                full = lax.dot_general(small, pick, (((0,), (0,)), ((), ())), preferred_element_type=F32)
                ref[slot, :, pl.ds(lo, width)] = full.astype(BF16)

    e_cp = [
        remote(window(zo), er.at[3], e_snd.at[0], e_rcv.at[0], nbr("z", 2)),
        remote(window(zu), er.at[1], e_snd.at[1], e_rcv.at[1], up),
        remote(window(zd), er.at[2], e_snd.at[2], e_rcv.at[2], down),
    ]

    def cols(p):
        c, lo, width, _ = PARTS[p]
        return pl.ds(CLS[c][0] + lo, width)

    H = ROWS // 2

    def a2a(p):
        k = 6 * p
        cc = cols(p)
        return [
            remote(fv.at[zo, pl.ds(0, H), cc], rl.at[0, :, cc], a_snd.at[k], a_rcv.at[k], up),
            remote(fv.at[zo, pl.ds(H, H), cc], rl.at[1, :, cc], a_snd.at[k + 1], a_rcv.at[k + 1], down),
            remote(fv.at[zu, :, cc], fb.at[1, :, cc], a_snd.at[k + 2], a_rcv.at[k + 2], up),
            remote(fv.at[zd, :, cc], fb.at[2, :, cc], a_snd.at[k + 3], a_rcv.at[k + 3], down),
            remote(rl.at[0, :, cc], fb.at[3, pl.ds(0, H), cc], a_snd.at[k + 4], a_rcv.at[k + 4], up),
            remote(rl.at[1, :, cc], fb.at[3, pl.ds(H, H), cc], a_snd.at[k + 5], a_rcv.at[k + 5], down),
        ]

    mine = pl.ds(pl.multiple_of(core * TOK, TOK), TOK)
    t_cp, l_tk = [], []
    for i in range(8):
        src = tokens.at[pl.ds(i * SLAB, SLAB), :]
        dst = tok.at[pl.ds(pl.multiple_of(core * TOK + i * SLAB, SLAB), SLAB), :]
        t_cp.append(remote(src, dst, t_snd.at[i], t_rcv.at[i], other))
        l_tk.append(pltpu.make_async_copy(src, dst, loc.at[5 + i]))

    def early():
        l_ex.wait()
        eb[...] = ex[...].astype(F32).astype(BF16)
        for m in e_cp:
            go(m)
        l_gn.wait()
        gf[...] = gb[...].astype(F32)
        first = 6 * fs + lax.div(3 * rep, 2)
        i = lax.broadcasted_iota(jnp.int32, (128, 128), 0)
        l = lax.broadcasted_iota(jnp.int32, (128, 128), 1)
        for h in range(2):
            row = jnp.broadcast_to(gf[pl.ds(first + h, 1), :], (128, 128))
            column = jnp.sum(jnp.where(i == l, row, 0.0), axis=1, keepdims=True)
            gn[pl.ds(128 * h, 128), :] = jnp.broadcast_to(column, (128, 128))

    def prepare():
        for s in (1, 2):
            e_cp[s].wait_recv()
        l_bs.wait()
        l_ms.wait()

    def encode(p):
        c, sub, width, _ = PARTS[p]
        lo = CLS[c][0] + sub
        row0 = pl.multiple_of(rep * ROWS, ROWS)

        def step(t, carry):
            rr = pl.ds(pl.multiple_of(t * SLAB, SLAB), SLAB)
            wr = pl.ds(pl.multiple_of(row0 + t * SLAB, SLAB), SLAB)
            fr = pl.ds(pl.multiple_of(off + t * SLAB, 16), SLAB)
            g = gn[fr, :]
            for k in range(width // 128):
                cc = pl.ds(lo + 128 * k, 128)
                b = bs[rr, cc]
                total = jnp.zeros((SLAB, 128), F32)
                for s in range(4):
                    v = (b - (fv[rep, rr, cc] if s == 0 else fb[s, rr, cc]).astype(F32)) * iv[s, fr, cc].astype(F32)
                    m = jnp.abs(v)
                    level = jnp.zeros_like(m)
                    for mid, val in THRESH:
                        level = jnp.where(m >= mid, val, level)
                    total = total + jnp.where(v < 0.0, -level, level) * sc[s, fr, cc].astype(F32)
                grad = total * 0.25
                moment = MOMENTUM_COEF * ms[rr, cc] + grad
                new = b - OUTER_RATE * (grad + MOMENTUM_COEF * moment)
                nm[rr, cc] = moment
                nb[rr, cc] = new
                W[c][pos["y"], pos["x"], wr, pl.ds(sub + 128 * k, 128)] = (new * g).astype(BF16)
            return carry

        lax.fori_loop(0, ROWS // SLAB, step, 0)

    def place(p, **at):
        half = at.pop("half", None)
        xs, ys = at.get("x", slice(None)), at.get("y", slice(None))
        if "z" in at:
            r0, n = at["z"] * ROWS, ROWS
        else:
            r0, n = 0, FROWS
        if half is not None:
            n = n // 2
            r0 = r0 + half * n
        if not isinstance(r0, int):
            r0 = pl.multiple_of(r0, 96)
        c, lo, width, _ = PARTS[p]
        return W[c].at[ys, xs, pl.ds(r0, n), pl.ds(lo, width)]

    M = {}
    OFF = (0, 1, -1, 2)
    used = [0]

    def both(*pair):
        out = []
        for j, s in enumerate((1, -1)):
            axis, ref = pair[j]
            out.append(remote(ref, ref, g_snd.at[used[0]], g_rcv.at[used[0]], nbr(axis, s)))
            used[0] += 1
        return out

    def full(p, axis, **fixed):
        here = place(p, **fixed, **{axis: pos[axis]})
        return both((axis, here), (axis, here))

    def half(p, axis, **fixed):
        return both(
            *[(axis, place(p, **fixed, **{axis: mod4(pos[axis] - s), "half": j})) for j, s in enumerate((1, -1))]
        )

    for p in range(len(PARTS)):
        m = a2a(p)
        M["r", p], M["d", p], M["f", p] = m[:2], m[2:4], m[4:]
        if p < DIRECT:
            far = remote(fv.at[zo, :, cols(p)], fb.at[3, :, cols(p)], a_snd.at[6 * p], a_rcv.at[6 * p], nbr("z", 2))
            M["r", p] = [far]
        a, b, l = PARTS[p][3]
        R, S = (a, b) if b == "z" else (b, a)
        at = {b: pos[b], l: pos[l]}
        M["1", p], M["1h", p] = full(p, a, **at), half(p, a, **at)
        for i in range(4):
            at = {a: mod4(pos[a] + OFF[i]), l: pos[l]}
            M["2", p, i], M["2h", p, i] = full(p, b, **at), half(p, b, **at)
            M["3", p, i] = full(p, l, **{R: pos[R], S: mod4(pos[S] + OFF[i])})
            M["3h", p, i] = half(p, l, **{R: mod4(pos[R] + OFF[i])})
            if i:
                M["3", p, 3 + i] = full(p, l, **{R: mod4(pos[R] + OFF[i])})

    def mm(c, count, coords, last=False):
        lo, width = CLS[c]
        cc = pl.ds(lo, width)

        def chunk(t, carry):
            yy, xx = coords(t)
            kk = pl.ds(pl.multiple_of((yy * 4 + xx) * FROWS, FROWS), FROWS)

            def block(m, carry):
                mr = pl.ds(pl.multiple_of(m * TOK, TOK), TOK)
                total = acc[mr, cc] + jnp.dot(tok[mr, kk], W[c][yy, xx], preferred_element_type=F32)
                if last:
                    for k in range(width // 128):
                        part = total[:, 128 * k : 128 * (k + 1)] * ss[mr, :]
                        kv[mr, pl.ds(lo + 128 * k, 128)] = part.astype(BF16)
                else:
                    acc[mr, cc] = total
                return carry

            return lax.fori_loop(0, 2, block, carry)

        lax.fori_loop(0, count, chunk, 0)

    def offset(i):
        return i + lax.div(i, 2) - 2 * lax.div(i, 3)

    def mm_near(c, i):
        if c == 1:
            yy = mod4(pos["y"] + OFF[i])
            mm(c, 3, lambda t: (yy, mod4(pos["x"] + offset(t))))
        else:
            xx = mod4(pos["x"] + OFF[i])
            mm(c, 3, lambda t: (mod4(pos["y"] + offset(t)), xx))

    def mm_far(c, i, last):
        if c == 1:
            mm(c, 1, lambda t: (mod4(pos["y"] + OFF[i]), mod4(pos["x"] + 2)), last)
        else:
            mm(c, 1, lambda t: (mod4(pos["y"] + 2), mod4(pos["x"] + OFF[i])), last)

    same = len({p[3] for p in PARTS if p[0] == 0}) == 1

    def mm_row(c, i):
        by_y = PARTS[[p[0] for p in PARTS].index(0)][3][1] == "y"
        at = mod4(pos["y" if by_y else "x"] + OFF[i])
        mm(c, 4, (lambda t: (at, t)) if by_y else (lambda t: (t, at)))

    def mm_level(c, i):
        def coords(t):
            turn = lax.div(t, i + 1)
            iy = i * (1 - turn) + (t - i - 1) * turn
            ix = t * (1 - turn) + i * turn
            return mod4(pos["y"] + offset(iy)), mod4(pos["x"] + offset(ix))

        mm(c, 2 * i + 1, coords)

    def squares(i):
        rr = pl.ds(pl.multiple_of(core * TOK + i * 128, 128), 128)

        def step(t, s):
            for k in range(4):
                v = tok[rr, pl.ds(pl.multiple_of(t * 512 + k * 128, 128), 128)].astype(F32)
                s = s + v * v
            return s

        s = lax.fori_loop(0, D // 512, step, jnp.zeros((128, 128), F32))
        mean = jnp.sum(s, axis=1, keepdims=True) * (1.0 / D)
        ss[rr, :] = jnp.broadcast_to(lax.rsqrt(mean + 1e-05) * (D ** -0.5), (128, 128))

    def finish(c):
        lo, width = CLS[c]

        def scale(m, carry):
            mr = pl.ds(pl.multiple_of(m * 64, 64), 64)
            for k in range(width // 128):
                at = pl.ds(lo + 128 * k, 128)
                kv[mr, at] = (acc[mr, at] * ss[mr, :]).astype(BF16)
            return carry

        lax.fori_loop(0, 2 * TOK // 64, scale, 0)

    s_cp = remote(ss.at[mine, :], ss.at[mine, :], t_snd.at[8], t_rcv.at[8], other)
    left = []
    def own_tokens():
        if once("own tokens"):
            for t in l_tk:
                t.wait()

    finished = set()
    for at, (kind, *key) in enumerate(SCHEDULE):
        key = tuple(key)
        if kind == "S":
            for m in M[key]:
                m.start()
            left.append(key)
        elif kind == "W":
            if once("wait"):
                early()
            if key[0] == "d":
                if once("prepare"):
                    prepare()
                c = PARTS[key[1]][0]
                if once(("factors", c)):
                    expand(*CLS[c])
            for m in M[key]:
                m.wait_recv()
        elif kind == "D":
            for m in M[key]:
                m.wait_send()
            left.remove(key)
        elif kind == "E":
            encode(*key)
        elif key[0] == "tk":
            l_tk[key[1]].start()
            go(t_cp[key[1]])
            if once("total"):
                acc[...] = jnp.zeros_like(acc)
        elif key[0] == "sq":
            own_tokens()
            squares(key[1])
            if key[1] == 2:
                go(s_cp)
        elif key[0] == "fin":
            if key[1] not in finished:
                if once("factors"):
                    s_cp.wait_recv()
                finish(key[1])
        else:
            own_tokens()
            if once("all tokens"):
                for t in t_cp:
                    t.wait_recv()
            c, i, how = key[1:]
            if how == "far":
                last = at == max(n for n, row in enumerate(SCHEDULE) if row[:3] == ("C", "mm", c))
                if last:
                    finished.add(c)
                    if once("factors"):
                        s_cp.wait_recv()
                mm_far(c, i, last)
            else:
                {"near": mm_near, "all": mm_row if same else mm_level}[how](c, i)
    for key in left:
        for m in M[key]:
            m.wait_send()

    for p in pending:
        p.wait_send()


def body(tokens, norm_gain, fragment, exponents, base_weight, momentum):
    any_ = pl.BlockSpec(memory_space=pl.ANY)
    dma = pltpu.SemaphoreType.DMA
    vm = pltpu.VMEM
    return pl.pallas_call(
        kernel,
        out_shape=(vm((ROWS, KVW), F32), vm((ROWS, KVW), F32), vm((2 * TOK, KVW), BF16)),
        in_specs=[any_] * 6,
        out_specs=[pl.BlockSpec(memory_space=vm)] * 3,
        scratch_shapes=[
            *[vm((4, 4, FROWS, width), BF16) for _, width in CLS],
            vm((2 * TOK, D), BF16),
            vm((2 * TOK, KVW), F32),
            vm((4, ROWS, KVW), BF16),
            vm((4, ROWS, KVW), BF16),
            vm((2, ROWS // 2, KVW), BF16),
            vm((ROWS, KVW), F32),
            vm((ROWS, KVW), F32),
            vm((D // 128, 128), BF16),
            vm((D // 128, 128), F32),
            vm((256, 128), F32),
            vm((BLOCK, 4 * ROWS), jnp.int32),
            vm((BLOCK, 4 * ROWS), BF16),
            vm((4, BLOCK, 256), BF16),
            vm((4, 256, KVW), BF16),
            vm((4, 256, KVW), BF16),
            vm((2 * TOK, 128), F32),
            dma((13,)),
            dma((6 * len(PARTS),)),
            dma((6 * len(PARTS),)),
            dma((3,)),
            dma((3,)),
            dma((9,)),
            dma((9,)),
            dma((42 * len(PARTS),)),
            dma((42 * len(PARTS),)),
        ],
        compiler_params=pltpu.CompilerParams(
            collective_id=0, has_side_effects=True, vmem_limit_bytes=59 * 1024 * 1024
        ),
        cost_estimate=pl.CostEstimate(flops=2 * 768 * 12288 * 1024, bytes_accessed=30_000_000, transcendentals=0),
    )(
        tokens,
        norm_gain.reshape(D // 128, 128),
        fragment.reshape(4, ROWS, KVW),
        exponents[0].T,
        base_weight,
        momentum,
    )


def solution(mesh):
    in_specs = (
        P(("replica", "fsdp", "tensor"), None),
        P(),
        P("replica", "fsdp", "tensor"),
        P("replica", "fsdp", "tensor"),
        P(("fsdp", "replica"), "tensor"),
        P(("fsdp", "replica"), "tensor"),
    )
    out_specs = (
        P(("fsdp", "replica"), "tensor"),
        P(("fsdp", "replica"), "tensor"),
        P(("replica", "fsdp"), "tensor"),
    )
    return jax.shard_map(body, mesh=mesh, in_specs=in_specs, out_specs=out_specs, check_vma=False)
```

```python
import jax
import jax.numpy as jnp
from jax import lax
from jax.experimental import pallas as pl
from jax.experimental.pallas import tpu as pltpu
from jax.sharding import PartitionSpec as P

MESH = pl.DeviceIdType.MESH
F32, BF16 = jnp.float32, jnp.bfloat16
D, KVW, BLOCK, TOK = 12288, 1024, 32, 384
ROWS = 192
FROWS = 768
SLAB = 48
OUTER_RATE = 0.7
MOMENTUM_COEF = 0.9
CLS = ((0, 256), (256, 384), (640, 384))
PARTS = (
    (0, 0, 128, ("x", "y", "z")),
    (0, 128, 128, ("y", "x", "z")),
    (2, 0, 128, ("z", "x", "y")),
    (1, 0, 128, ("z", "y", "x")),
    (2, 128, 256, ("x", "z", "y")),
    (1, 128, 256, ("y", "z", "x")),
)

DIRECT = 2
SCHEDULE = (
    ("S", "r", 0), ("S", "d", 0), ("S", "r", 1), ("D", "r", 0), ("S", "d", 1), ("D", "d", 0), ("S", "r", 2),
    ("W", "d", 0), ("W", "r", 0), ("E", 0), ("S", "1", 0), ("S", "2", 0, 0), ("D", "r", 1), ("D", "d", 1),
    ("D", "r", 2), ("S", "d", 2), ("S", "r", 3), ("W", "d", 1), ("W", "r", 1), ("E", 1), ("D", "1", 0),
    ("S", "2", 1, 0), ("D", "2", 0, 0), ("S", "1", 1), ("W", "r", 2), ("S", "f", 2), ("D", "r", 3), ("D", "d", 2),
    ("S", "d", 3), ("W", "1", 0), ("S", "1h", 0), ("W", "2", 0, 0), ("S", "2h", 0, 0), ("S", "2", 0, 1),
    ("S", "2", 0, 2), ("D", "f", 2), ("W", "r", 3), ("S", "f", 3), ("S", "r", 4), ("W", "d", 2), ("W", "f", 2),
    ("E", 2), ("D", "2", 1, 0), ("D", "1h", 0), ("W", "2", 1, 0), ("S", "2h", 1, 0), ("D", "d", 3), ("D", "f", 3),
    ("S", "d", 4), ("W", "1", 1), ("S", "2", 1, 1), ("D", "1", 1), ("D", "2h", 0, 0), ("S", "1h", 1), ("W", "1h", 0),
    ("S", "2", 0, 3), ("D", "2h", 1, 0), ("S", "2", 1, 2), ("S", "2", 2, 0), ("D", "2", 0, 1), ("D", "2", 0, 2),
    ("S", "3", 2, 0), ("W", "d", 3), ("W", "f", 3), ("E", 3), ("D", "r", 4), ("W", "r", 4), ("S", "f", 4),
    ("D", "1h", 1), ("W", "2", 0, 1), ("S", "2h", 0, 1), ("W", "2", 0, 2), ("S", "2h", 0, 2), ("S", "2", 3, 0),
    ("D", "d", 4), ("S", "r", 5), ("D", "2", 1, 1), ("W", "1h", 1), ("S", "2", 1, 3), ("S", "3", 3, 0),
    ("W", "2", 1, 1), ("S", "2h", 1, 1), ("S", "d", 5), ("D", "f", 4), ("S", "1", 2), ("S", "1", 3), ("D", "2", 1, 2),
    ("D", "2", 2, 0), ("W", "2", 1, 2), ("S", "2h", 1, 2), ("D", "2", 0, 3), ("D", "2h", 0, 1), ("D", "3", 2, 0),
    ("D", "2h", 0, 2), ("W", "2", 0, 3), ("S", "2h", 0, 3), ("W", "2", 2, 0), ("S", "2h", 2, 0), ("W", "d", 4),
    ("W", "f", 4), ("E", 4), ("D", "2h", 1, 1), ("S", "1", 4), ("D", "2", 3, 0), ("D", "2h", 0, 3), ("W", "2", 3, 0),
    ("S", "2h", 3, 0), ("S", "3", 4, 0), ("D", "r", 5), ("D", "1", 2), ("D", "1", 3), ("W", "r", 5), ("S", "f", 5),
    ("D", "2", 1, 3), ("D", "2h", 1, 2), ("D", "3", 3, 0), ("D", "2h", 2, 0), ("W", "2", 1, 3), ("S", "2h", 1, 3),
    ("S", "2", 4, 0), ("W", "1", 2), ("S", "2", 2, 1), ("D", "2h", 3, 0), ("W", "1", 3), ("S", "2", 3, 1),
    ("S", "2", 3, 2), ("S", "2", 2, 2), ("D", "d", 5), ("S", "1h", 2), ("S", "1h", 3), ("S", "3", 2, 1),
    ("D", "2h", 1, 3), ("S", "3", 3, 1), ("C", "tk", 0), ("D", "3", 4, 0), ("S", "3", 2, 2), ("S", "3", 0, 0),
    ("D", "1", 4), ("S", "3", 3, 2), ("C", "tk", 1), ("D", "f", 5), ("D", "1h", 2), ("D", "1h", 3), ("W", "1", 4),
    ("S", "2", 4, 1), ("S", "1h", 4), ("S", "2", 4, 2), ("W", "d", 5), ("W", "f", 5), ("E", 5), ("D", "2", 3, 1),
    ("D", "2", 3, 2), ("D", "3", 2, 1), ("S", "1", 5), ("D", "2", 2, 1), ("D", "2", 2, 2), ("W", "2", 2, 1),
    ("S", "2h", 2, 1), ("W", "1h", 2), ("S", "2", 2, 3), ("D", "3", 2, 2), ("W", "2", 3, 1), ("S", "2h", 3, 1),
    ("W", "2", 3, 2), ("S", "2h", 3, 2), ("D", "3", 3, 1), ("W", "2", 2, 2), ("S", "2h", 2, 2), ("W", "1h", 3),
    ("S", "2", 3, 3), ("D", "3", 0, 0), ("S", "2", 5, 0), ("S", "3", 5, 0), ("C", "tk", 2), ("C", "tk", 3),
    ("S", "3", 2, 3), ("D", "2", 4, 0), ("W", "2", 4, 0), ("S", "2h", 4, 0), ("D", "2h", 3, 1), ("D", "2h", 3, 2),
    ("S", "3", 4, 1), ("D", "3", 3, 2), ("D", "2h", 2, 1), ("D", "1h", 4), ("D", "2h", 2, 2), ("S", "3", 3, 3),
    ("W", "1h", 4), ("S", "2", 4, 3), ("C", "tk", 4), ("D", "2", 2, 3), ("W", "2", 2, 3), ("S", "2h", 2, 3),
    ("S", "3", 4, 2), ("C", "tk", 5), ("D", "2", 3, 3), ("D", "1", 5), ("D", "3", 2, 3), ("W", "1", 5),
    ("S", "1h", 5), ("D", "2", 4, 1), ("S", "2", 5, 1), ("W", "2", 3, 3), ("S", "2h", 3, 3), ("D", "2", 4, 2),
    ("S", "2", 5, 2), ("D", "3", 3, 3), ("D", "2h", 2, 3), ("D", "3", 5, 0), ("S", "3", 3, 4), ("W", "2", 4, 1),
    ("S", "2h", 4, 1), ("W", "2", 4, 2), ("S", "2h", 4, 2), ("C", "tk", 6), ("W", "2h", 4, 0), ("S", "3", 4, 3),
    ("S", "3", 3, 5), ("C", "tk", 7), ("D", "2h", 4, 0), ("D", "2h", 3, 3), ("D", "3", 4, 1), ("D", "1h", 5),
    ("S", "3", 2, 4), ("D", "2", 5, 0), ("W", "1h", 5), ("S", "2", 5, 3), ("W", "2", 5, 0), ("S", "2h", 5, 0),
    ("D", "3", 3, 4), ("S", "3", 5, 1), ("D", "3", 4, 2), ("D", "3", 4, 3), ("W", "2h", 4, 1), ("S", "3", 4, 4),
    ("S", "3", 5, 2), ("W", "3", 2, 0), ("W", "3", 2, 1), ("W", "3", 2, 2), ("W", "3", 2, 3), ("W", "3", 4, 0),
    ("W", "3", 4, 1), ("W", "3", 4, 2), ("W", "3", 4, 3), ("C", "mm", 2, 0, "near"), ("D", "2h", 4, 1),
    ("D", "2h", 4, 2), ("D", "2", 4, 3), ("D", "2h", 5, 0), ("D", "2", 5, 1), ("D", "2", 5, 2), ("W", "2", 4, 3),
    ("S", "2h", 4, 3), ("W", "2", 5, 1), ("S", "2h", 5, 1), ("D", "2", 5, 3), ("W", "2", 5, 2), ("S", "2h", 5, 2),
    ("D", "3", 3, 5), ("W", "2h", 5, 0), ("S", "3", 5, 3), ("W", "2", 5, 3), ("S", "2h", 5, 3), ("D", "3", 5, 1),
    ("W", "2h", 3, 0), ("W", "2h", 3, 1), ("W", "2h", 3, 2), ("W", "2h", 3, 3), ("S", "3", 3, 6), ("C", "sq", 0),
    ("S", "3", 1, 0), ("C", "sq", 1), ("D", "2h", 4, 3), ("S", "3", 0, 1), ("C", "sq", 2), ("D", "2h", 5, 1),
    ("D", "2h", 5, 2), ("S", "3", 1, 1), ("D", "3", 2, 4), ("S", "3", 2, 5), ("D", "3", 5, 2), ("D", "2h", 5, 3),
    ("S", "3", 0, 2), ("D", "3", 5, 3), ("W", "2h", 5, 1), ("S", "3", 5, 4), ("S", "3", 1, 2), ("W", "3", 3, 0),
    ("W", "3", 3, 1), ("W", "3", 3, 2), ("W", "3", 3, 3), ("W", "3", 5, 0), ("W", "3", 5, 1), ("W", "3", 5, 2),
    ("W", "3", 5, 3), ("C", "mm", 1, 0, "near"), ("D", "3", 1, 0), ("D", "3", 0, 1), ("D", "3", 1, 1),
    ("S", "3", 0, 3), ("S", "3", 1, 3), ("D", "3", 4, 4), ("W", "2h", 4, 2), ("S", "3", 4, 5), ("D", "3", 0, 2),
    ("S", "3", 0, 4), ("W", "3", 2, 4), ("W", "3", 4, 4), ("C", "mm", 2, 1, "near"), ("D", "3", 3, 6),
    ("D", "3", 1, 2), ("D", "3", 0, 3), ("D", "3", 1, 3), ("W", "3", 0, 0), ("W", "3", 0, 1), ("W", "3", 0, 2),
    ("W", "3", 0, 3), ("S", "3h", 0, 0), ("W", "2h", 5, 2), ("S", "3", 5, 5), ("D", "3", 2, 5), ("W", "3", 1, 0),
    ("W", "3", 1, 1), ("W", "3", 1, 2), ("W", "3", 1, 3), ("S", "3h", 1, 0), ("W", "2h", 2, 0), ("W", "2h", 2, 1),
    ("W", "2h", 2, 2), ("W", "2h", 2, 3), ("S", "3", 2, 6), ("S", "3", 1, 4), ("W", "3", 3, 4), ("W", "3", 5, 4),
    ("C", "mm", 1, 1, "near"), ("D", "3", 5, 4), ("D", "3", 0, 4), ("D", "3", 4, 5), ("W", "2h", 4, 3),
    ("S", "3", 4, 6), ("D", "3h", 0, 0), ("D", "3h", 1, 0), ("W", "3", 0, 4), ("S", "3h", 0, 1), ("W", "2h", 5, 3),
    ("S", "3", 5, 6), ("W", "3", 2, 5), ("W", "3", 4, 5), ("C", "mm", 2, 2, "near"), ("S", "3", 0, 5),
    ("W", "3h", 0, 0), ("W", "3h", 1, 0), ("C", "mm", 0, 0, "all"), ("W", "3", 3, 5), ("W", "3", 5, 5),
    ("C", "mm", 1, 2, "near"), ("D", "3", 1, 4), ("D", "3h", 0, 1), ("W", "3", 1, 4), ("S", "3h", 1, 1),
    ("D", "3", 2, 6), ("D", "3", 5, 5), ("S", "3h", 2, 0), ("S", "3", 1, 5), ("S", "3h", 3, 0), ("S", "3h", 4, 0),
    ("S", "3h", 5, 0), ("D", "3", 0, 5), ("D", "3h", 1, 1), ("W", "3", 0, 5), ("S", "3h", 0, 2), ("W", "3h", 0, 1),
    ("W", "3h", 1, 1), ("C", "mm", 0, 1, "all"), ("D", "3", 4, 6), ("D", "3h", 2, 0), ("S", "3h", 2, 1),
    ("W", "2h", 0, 0), ("W", "2h", 0, 1), ("W", "2h", 0, 2), ("W", "2h", 0, 3), ("S", "3", 0, 6), ("D", "3", 5, 6),
    ("D", "3h", 3, 0), ("S", "3h", 3, 1), ("S", "3h", 4, 1), ("W", "3", 2, 6), ("W", "3", 4, 6),
    ("C", "mm", 2, 3, "near"), ("S", "3h", 5, 1), ("D", "3", 1, 5), ("D", "3h", 0, 2), ("W", "3", 1, 5),
    ("S", "3h", 1, 2), ("W", "3", 3, 6), ("W", "3", 5, 6), ("C", "mm", 1, 3, "near"), ("D", "3h", 4, 0),
    ("D", "3h", 2, 1), ("S", "3h", 2, 2), ("W", "2h", 1, 0), ("W", "2h", 1, 1), ("W", "2h", 1, 2), ("W", "2h", 1, 3),
    ("S", "3", 1, 6), ("D", "3h", 5, 0), ("D", "3h", 3, 1), ("S", "3h", 3, 2), ("W", "3h", 2, 0), ("W", "3h", 4, 0),
    ("C", "mm", 2, 0, "far"), ("S", "3h", 4, 2), ("W", "3h", 3, 0), ("W", "3h", 5, 0), ("C", "mm", 1, 0, "far"),
    ("S", "3h", 5, 2), ("W", "3h", 0, 2), ("W", "3h", 1, 2), ("C", "mm", 0, 2, "all"), ("D", "3h", 1, 2),
    ("D", "3", 0, 6), ("W", "3", 0, 6), ("S", "3h", 0, 3), ("D", "3h", 4, 1), ("D", "3h", 2, 2), ("S", "3h", 2, 3),
    ("W", "3h", 2, 1), ("W", "3h", 4, 1), ("C", "mm", 2, 1, "far"), ("D", "3", 1, 6), ("W", "3", 1, 6),
    ("S", "3h", 1, 3), ("D", "3h", 5, 1), ("D", "3h", 3, 2), ("S", "3h", 3, 3), ("W", "3h", 3, 1), ("W", "3h", 5, 1),
    ("C", "mm", 1, 1, "far"), ("S", "3h", 4, 3), ("S", "3h", 5, 3), ("W", "3h", 2, 2), ("W", "3h", 4, 2),
    ("C", "mm", 2, 2, "far"), ("W", "3h", 3, 2), ("W", "3h", 5, 2), ("C", "mm", 1, 2, "far"), ("W", "3h", 0, 3),
    ("W", "3h", 1, 3), ("C", "mm", 0, 3, "all"), ("W", "3h", 2, 3), ("W", "3h", 4, 3), ("C", "mm", 2, 3, "far"),
    ("W", "3h", 3, 3), ("W", "3h", 5, 3), ("C", "mm", 1, 3, "far"), ("C", "fin", 1), ("C", "fin", 2), ("C", "fin", 0),
    ("D", "3h", 4, 2), ("D", "3h", 0, 3), ("D", "3h", 5, 2), ("D", "3h", 1, 3), ("D", "3h", 2, 3), ("D", "3h", 3, 3),
    ("D", "3h", 4, 3), ("D", "3h", 5, 3),
)

THRESH = ((0.25, 0.5), (0.75, 1.0), (1.25, 1.5), (1.75, 2.0), (2.5, 3.0), (3.5, 4.0), (5.0, 6.0))


def mod4(v):
    return lax.rem(v + 8, 4)


def kernel(
    tokens, gain, frag, exps, base, mom,
    nb, nm, kv,
    w0, w1, w2, tok, acc, fv, fb, rl, bs, ms, gb, gf, gn, ex, eb, er, sc, iv, ss,
    loc, a_snd, a_rcv, e_snd, e_rcv, t_snd, t_rcv, g_snd, g_rcv,
):
    W = (w0, w1, w2)
    rep = lax.axis_index("replica")
    fs = lax.axis_index("fsdp")
    core = lax.axis_index("tensor")
    pos = {"x": lax.rem(fs, 4), "y": lax.div(fs, 4), "z": rep}

    def nbr(axis, step):
        c = dict(pos)
        c[axis] = mod4(pos[axis] + step)
        return (c["z"], c["y"] * 4 + c["x"], core)

    other = (rep, fs, 1 - core)

    def remote(src, dst, ss_, rs_, dev):
        return pltpu.make_async_remote_copy(
            src_ref=src, dst_ref=dst, send_sem=ss_, recv_sem=rs_, device_id=dev, device_id_type=MESH
        )

    seen = set()

    def once(name):
        new = name not in seen
        seen.add(name)
        return new

    pending = []

    def go(copy):
        copy.start()
        pending.append(copy)

    barrier = pltpu.get_barrier_semaphore()
    peers = [nbr(a, s) for a in "xyz" for s in (1, -1)] + [nbr("z", 2), other]
    for p in peers:
        pl.semaphore_signal(barrier, inc=1, device_id=p, device_id_type=MESH)

    l_ex = pltpu.make_async_copy(exps, ex, loc.at[0])
    l_ex.start()
    l_fr = pltpu.make_async_copy(frag, fv, loc.at[1])
    l_fr.start()
    l_bs = pltpu.make_async_copy(base, bs, loc.at[2])
    l_bs.start()
    l_ms = pltpu.make_async_copy(mom, ms, loc.at[3])
    l_ms.start()
    l_gn = pltpu.make_async_copy(gain, gb, loc.at[4])
    l_gn.start()

    pl.semaphore_wait(barrier, len(peers))
    l_fr.wait()

    up, down = nbr("z", 1), nbr("z", -1)
    zu, zd, zo = mod4(rep + 1), mod4(rep - 1), mod4(rep + 2)

    def window(d):
        return eb.at[:, pl.ds(pl.multiple_of(128 * lax.div(3 * d, 2), 128), 256)]

    off = 64 * lax.rem(rep, 2)

    def expand(lo, width):
        j = lax.broadcasted_iota(jnp.int32, (BLOCK, width), 0)
        n = lax.broadcasted_iota(jnp.int32, (BLOCK, width), 1)
        pick = jnp.where(j == lax.div(n + lo, BLOCK), 1.0, 0.0).astype(BF16)
        for slot in range(4):
            if slot == 3 and once("far exponents"):
                e_cp[0].wait_recv()
            e = (window(rep)[...] if slot == 0 else er[slot]).astype(F32)
            for ref, sign in ((sc, 1.0), (iv, -1.0)):
                small = jnp.exp2(sign * e).astype(BF16)
                full = lax.dot_general(small, pick, (((0,), (0,)), ((), ())), preferred_element_type=F32)
                ref[slot, :, pl.ds(lo, width)] = full.astype(BF16)

    e_cp = [
        remote(window(zo), er.at[3], e_snd.at[0], e_rcv.at[0], nbr("z", 2)),
        remote(window(zu), er.at[1], e_snd.at[1], e_rcv.at[1], up),
        remote(window(zd), er.at[2], e_snd.at[2], e_rcv.at[2], down),
    ]

    def cols(p):
        c, lo, width, _ = PARTS[p]
        return pl.ds(CLS[c][0] + lo, width)

    H = ROWS // 2

    def a2a(p):
        k = 6 * p
        cc = cols(p)
        return [
            remote(fv.at[zo, pl.ds(0, H), cc], rl.at[0, :, cc], a_snd.at[k], a_rcv.at[k], up),
            remote(fv.at[zo, pl.ds(H, H), cc], rl.at[1, :, cc], a_snd.at[k + 1], a_rcv.at[k + 1], down),
            remote(fv.at[zu, :, cc], fb.at[1, :, cc], a_snd.at[k + 2], a_rcv.at[k + 2], up),
            remote(fv.at[zd, :, cc], fb.at[2, :, cc], a_snd.at[k + 3], a_rcv.at[k + 3], down),
            remote(rl.at[0, :, cc], fb.at[3, pl.ds(0, H), cc], a_snd.at[k + 4], a_rcv.at[k + 4], up),
            remote(rl.at[1, :, cc], fb.at[3, pl.ds(H, H), cc], a_snd.at[k + 5], a_rcv.at[k + 5], down),
        ]

    mine = pl.ds(pl.multiple_of(core * TOK, TOK), TOK)
    t_cp, l_tk = [], []
    for i in range(8):
        src = tokens.at[pl.ds(i * SLAB, SLAB), :]
        dst = tok.at[pl.ds(pl.multiple_of(core * TOK + i * SLAB, SLAB), SLAB), :]
        t_cp.append(remote(src, dst, t_snd.at[i], t_rcv.at[i], other))
        l_tk.append(pltpu.make_async_copy(src, dst, loc.at[5 + i]))

    def early():
        l_ex.wait()
        eb[...] = ex[...].astype(F32).astype(BF16)
        for m in e_cp:
            go(m)
        l_gn.wait()
        gf[...] = gb[...].astype(F32)
        first = 6 * fs + lax.div(3 * rep, 2)
        i = lax.broadcasted_iota(jnp.int32, (128, 128), 0)
        l = lax.broadcasted_iota(jnp.int32, (128, 128), 1)
        for h in range(2):
            row = jnp.broadcast_to(gf[pl.ds(first + h, 1), :], (128, 128))
            column = jnp.sum(jnp.where(i == l, row, 0.0), axis=1, keepdims=True)
            gn[pl.ds(128 * h, 128), :] = jnp.broadcast_to(column, (128, 128))

    def prepare():
        for s in (1, 2):
            e_cp[s].wait_recv()
        l_bs.wait()
        l_ms.wait()

    def encode(p):
        c, sub, width, _ = PARTS[p]
        lo = CLS[c][0] + sub
        row0 = pl.multiple_of(rep * ROWS, ROWS)

        def step(t, carry):
            rr = pl.ds(pl.multiple_of(t * SLAB, SLAB), SLAB)
            wr = pl.ds(pl.multiple_of(row0 + t * SLAB, SLAB), SLAB)
            fr = pl.ds(pl.multiple_of(off + t * SLAB, 16), SLAB)
            g = gn[fr, :]
            for k in range(width // 128):
                cc = pl.ds(lo + 128 * k, 128)
                b = bs[rr, cc]
                total = jnp.zeros((SLAB, 128), F32)
                for s in range(4):
                    v = (b - (fv[rep, rr, cc] if s == 0 else fb[s, rr, cc]).astype(F32)) * iv[s, fr, cc].astype(F32)
                    m = jnp.abs(v)
                    level = jnp.zeros_like(m)
                    for mid, val in THRESH:
                        level = jnp.where(m >= mid, val, level)
                    total = total + jnp.where(v < 0.0, -level, level) * sc[s, fr, cc].astype(F32)
                grad = total * 0.25
                moment = MOMENTUM_COEF * ms[rr, cc] + grad
                new = b - OUTER_RATE * (grad + MOMENTUM_COEF * moment)
                nm[rr, cc] = moment
                nb[rr, cc] = new
                W[c][pos["y"], pos["x"], wr, pl.ds(sub + 128 * k, 128)] = (new * g).astype(BF16)
            return carry

        lax.fori_loop(0, ROWS // SLAB, step, 0)

    def place(p, **at):
        half = at.pop("half", None)
        xs, ys = at.get("x", slice(None)), at.get("y", slice(None))
        if "z" in at:
            r0, n = at["z"] * ROWS, ROWS
        else:
            r0, n = 0, FROWS
        if half is not None:
            n = n // 2
            r0 = r0 + half * n
        if not isinstance(r0, int):
            r0 = pl.multiple_of(r0, 96)
        c, lo, width, _ = PARTS[p]
        return W[c].at[ys, xs, pl.ds(r0, n), pl.ds(lo, width)]

    M = {}
    OFF = (0, 1, -1, 2)
    used = [0]

    def both(*pair):
        out = []
        for j, s in enumerate((1, -1)):
            axis, ref = pair[j]
            out.append(remote(ref, ref, g_snd.at[used[0]], g_rcv.at[used[0]], nbr(axis, s)))
            used[0] += 1
        return out

    def full(p, axis, **fixed):
        here = place(p, **fixed, **{axis: pos[axis]})
        return both((axis, here), (axis, here))

    def half(p, axis, **fixed):
        return both(
            *[(axis, place(p, **fixed, **{axis: mod4(pos[axis] - s), "half": j})) for j, s in enumerate((1, -1))]
        )

    for p in range(len(PARTS)):
        m = a2a(p)
        M["r", p], M["d", p], M["f", p] = m[:2], m[2:4], m[4:]
        if p < DIRECT:
            far = remote(fv.at[zo, :, cols(p)], fb.at[3, :, cols(p)], a_snd.at[6 * p], a_rcv.at[6 * p], nbr("z", 2))
            M["r", p] = [far]
        a, b, l = PARTS[p][3]
        R, S = (a, b) if b == "z" else (b, a)
        at = {b: pos[b], l: pos[l]}
        M["1", p], M["1h", p] = full(p, a, **at), half(p, a, **at)
        for i in range(4):
            at = {a: mod4(pos[a] + OFF[i]), l: pos[l]}
            M["2", p, i], M["2h", p, i] = full(p, b, **at), half(p, b, **at)
            M["3", p, i] = full(p, l, **{R: pos[R], S: mod4(pos[S] + OFF[i])})
            M["3h", p, i] = half(p, l, **{R: mod4(pos[R] + OFF[i])})
            if i:
                M["3", p, 3 + i] = full(p, l, **{R: mod4(pos[R] + OFF[i])})

    def mm(c, count, coords, last=False):
        lo, width = CLS[c]
        cc = pl.ds(lo, width)
        rows = 2 * TOK if c == 0 else TOK

        def chunk(t, carry):
            yy, xx = coords(t)
            kk = pl.ds(pl.multiple_of((yy * 4 + xx) * FROWS, FROWS), FROWS)

            def block(m, carry):
                mr = pl.ds(pl.multiple_of(m * rows, rows), rows)
                total = acc[mr, cc] + jnp.dot(tok[mr, kk], W[c][yy, xx], preferred_element_type=F32)
                if last:
                    for k in range(width // 128):
                        part = total[:, 128 * k : 128 * (k + 1)] * ss[mr, :]
                        kv[mr, pl.ds(lo + 128 * k, 128)] = part.astype(BF16)
                else:
                    acc[mr, cc] = total
                return carry

            return lax.fori_loop(0, 2 * TOK // rows, block, carry)

        lax.fori_loop(0, count, chunk, 0)

    def offset(i):
        return i + lax.div(i, 2) - 2 * lax.div(i, 3)

    def mm_near(c, i):
        if c == 1:
            yy = mod4(pos["y"] + OFF[i])
            mm(c, 3, lambda t: (yy, mod4(pos["x"] + offset(t))))
        else:
            xx = mod4(pos["x"] + OFF[i])
            mm(c, 3, lambda t: (mod4(pos["y"] + offset(t)), xx))

    def mm_far(c, i, last):
        if c == 1:
            mm(c, 1, lambda t: (mod4(pos["y"] + OFF[i]), mod4(pos["x"] + 2)), last)
        else:
            mm(c, 1, lambda t: (mod4(pos["y"] + 2), mod4(pos["x"] + OFF[i])), last)

    same = len({p[3] for p in PARTS if p[0] == 0}) == 1

    def mm_row(c, i):
        by_y = PARTS[[p[0] for p in PARTS].index(0)][3][1] == "y"
        at = mod4(pos["y" if by_y else "x"] + OFF[i])
        mm(c, 4, (lambda t: (at, t)) if by_y else (lambda t: (t, at)))

    def mm_level(c, i):
        def coords(t):
            turn = lax.div(t, i + 1)
            iy = i * (1 - turn) + (t - i - 1) * turn
            ix = t * (1 - turn) + i * turn
            return mod4(pos["y"] + offset(iy)), mod4(pos["x"] + offset(ix))

        mm(c, 2 * i + 1, coords)

    def squares(i):
        rr = pl.ds(pl.multiple_of(core * TOK + i * 128, 128), 128)

        def step(t, s):
            for k in range(4):
                v = tok[rr, pl.ds(pl.multiple_of(t * 512 + k * 128, 128), 128)].astype(F32)
                s = s + v * v
            return s

        s = lax.fori_loop(0, D // 512, step, jnp.zeros((128, 128), F32))
        mean = jnp.sum(s, axis=1, keepdims=True) * (1.0 / D)
        ss[rr, :] = jnp.broadcast_to(lax.rsqrt(mean + 1e-05) * (D ** -0.5), (128, 128))

    def finish(c):
        lo, width = CLS[c]

        def scale(m, carry):
            mr = pl.ds(pl.multiple_of(m * 64, 64), 64)
            for k in range(width // 128):
                at = pl.ds(lo + 128 * k, 128)
                kv[mr, at] = (acc[mr, at] * ss[mr, :]).astype(BF16)
            return carry

        lax.fori_loop(0, 2 * TOK // 64, scale, 0)

    s_cp = remote(ss.at[mine, :], ss.at[mine, :], t_snd.at[8], t_rcv.at[8], other)
    left = []
    def own_tokens():
        if once("own tokens"):
            for t in l_tk:
                t.wait()

    finished = set()
    for at, (kind, *key) in enumerate(SCHEDULE):
        key = tuple(key)
        if kind == "S":
            for m in M[key]:
                m.start()
            left.append(key)
        elif kind == "W":
            if once("wait"):
                early()
            if key[0] == "d":
                if once("prepare"):
                    prepare()
                c = PARTS[key[1]][0]
                if once(("factors", c)):
                    expand(*CLS[c])
            for m in M[key]:
                m.wait_recv()
        elif kind == "D":
            for m in M[key]:
                m.wait_send()
            left.remove(key)
        elif kind == "E":
            encode(*key)
        elif key[0] == "tk":
            l_tk[key[1]].start()
            go(t_cp[key[1]])
            if once("total"):
                acc[...] = jnp.zeros_like(acc)
        elif key[0] == "sq":
            own_tokens()
            squares(key[1])
            if key[1] == 2:
                go(s_cp)
        elif key[0] == "fin":
            if key[1] not in finished:
                if once("factors"):
                    s_cp.wait_recv()
                finish(key[1])
        else:
            own_tokens()
            if once("all tokens"):
                for t in t_cp:
                    t.wait_recv()
            c, i, how = key[1:]
            if how == "far":
                last = at == max(n for n, row in enumerate(SCHEDULE) if row[:3] == ("C", "mm", c))
                if last:
                    finished.add(c)
                    if once("factors"):
                        s_cp.wait_recv()
                mm_far(c, i, last)
            else:
                {"near": mm_near, "all": mm_row if same else mm_level}[how](c, i)
    for key in left:
        for m in M[key]:
            m.wait_send()

    for p in pending:
        p.wait_send()


def body(tokens, norm_gain, fragment, exponents, base_weight, momentum):
    any_ = pl.BlockSpec(memory_space=pl.ANY)
    dma = pltpu.SemaphoreType.DMA
    vm = pltpu.VMEM
    return pl.pallas_call(
        kernel,
        out_shape=(vm((ROWS, KVW), F32), vm((ROWS, KVW), F32), vm((2 * TOK, KVW), BF16)),
        in_specs=[any_] * 6,
        out_specs=[pl.BlockSpec(memory_space=vm)] * 3,
        scratch_shapes=[
            *[vm((4, 4, FROWS, width), BF16) for _, width in CLS],
            vm((2 * TOK, D), BF16),
            vm((2 * TOK, KVW), F32),
            vm((4, ROWS, KVW), BF16),
            vm((4, ROWS, KVW), BF16),
            vm((2, ROWS // 2, KVW), BF16),
            vm((ROWS, KVW), F32),
            vm((ROWS, KVW), F32),
            vm((D // 128, 128), BF16),
            vm((D // 128, 128), F32),
            vm((256, 128), F32),
            vm((BLOCK, 4 * ROWS), jnp.int32),
            vm((BLOCK, 4 * ROWS), BF16),
            vm((4, BLOCK, 256), BF16),
            vm((4, 256, KVW), BF16),
            vm((4, 256, KVW), BF16),
            vm((2 * TOK, 128), F32),
            dma((13,)),
            dma((6 * len(PARTS),)),
            dma((6 * len(PARTS),)),
            dma((3,)),
            dma((3,)),
            dma((9,)),
            dma((9,)),
            dma((42 * len(PARTS),)),
            dma((42 * len(PARTS),)),
        ],
        compiler_params=pltpu.CompilerParams(
            collective_id=0, has_side_effects=True, vmem_limit_bytes=59 * 1024 * 1024
        ),
        cost_estimate=pl.CostEstimate(flops=2 * 768 * 12288 * 1024, bytes_accessed=30_000_000, transcendentals=0),
    )(
        tokens,
        norm_gain.reshape(D // 128, 128),
        fragment.reshape(4, ROWS, KVW),
        exponents[0].T,
        base_weight,
        momentum,
    )


def solution(mesh):
    in_specs = (
        P(("replica", "fsdp", "tensor"), None),
        P(),
        P("replica", "fsdp", "tensor"),
        P("replica", "fsdp", "tensor"),
        P(("fsdp", "replica"), "tensor"),
        P(("fsdp", "replica"), "tensor"),
    )
    out_specs = (
        P(("fsdp", "replica"), "tensor"),
        P(("fsdp", "replica"), "tensor"),
        P(("replica", "fsdp"), "tensor"),
    )
    return jax.shard_map(body, mesh=mesh, in_specs=in_specs, out_specs=out_specs, check_vma=False)
```
